32 devices in a mesh: grp: 4 (over y, core), wide: 8 (over z, x).
Axes of the slice: x: 2, y: 2, z: 4, core: 2. Of those that a mesh axis runs over, the one named last changes fastest.
Arguments:
- stem_maps: bfloat16 [256, 13, 13, 256], P(('grp', 'wide')), may hold values from -6 to 6
- validity: int32 [256], P(('grp', 'wide')), may hold values from 0 to 1, as said below
- labels: int32 [256], P(('grp', 'wide')), may hold values from 0 to 9999
- conv_weight: float32 [2304, 384], replicated, may hold values from -0.125 to 0.125
- fc6_weight: float32 [13824, 4096], P('wide'), may hold values from -0.125 to 0.125
- head_weight: float32 [4096, 10000], P('wide'), may hold values from -0.375 to 0.375
- vectors: float32 [14864], replicated, may hold values from -1.5 to 1.6, as said below
- pca_matrix: float32 [4096, 256], P('wide'), may hold values from -0.09375 to 0.09375
- conv_row_state: float32 [2304], replicated, may hold values from 0.128 to 0.512
- conv_col_state: float32 [384], replicated, may hold values from 0.128 to 0.512
- fc6_row_state: float32 [13824], P('wide'), may hold values from 0.00768 to 0.03072
- fc6_col_state: float32 [4096], replicated, may hold values from 0.00768 to 0.03072
- head_row_state: float32 [4096], P('wide'), may hold values from 0.0011946667 to 0.004778667
- head_col_state: float32 [10000], replicated, may hold values from 0.07 to 0.28
- vector_state: float32 [14864], replicated
Outputs:
- loss_sum: float32 [], replicated
- loss_weight: float32 [], replicated
- embedded: float32 [256, 256], P(('grp', 'wide'))
- conv_grad: float32 [2304, 384], replicated
- conv_row_new: float32 [2304], replicated
- conv_col_new: float32 [384], replicated
- conv_new: float32 [2304, 384], replicated
- fc6_grad: float32 [13824, 4096], P('wide')
- fc6_row_new: float32 [13824], P('wide')
- fc6_col_new: float32 [4096], replicated
- fc6_new: float32 [13824, 4096], P('wide')
- head_grad: float32 [4096, 10000], P('wide')
- head_row_new: float32 [4096], P('wide')
- head_col_new: float32 [10000], replicated
- head_new: float32 [4096, 10000], P('wide')
- vector_grad: float32 [14864], replicated
- vector_state_new: float32 [14864], replicated
- vector_new: float32 [14864], replicated
The draws below stay inside these ranges and needn't reach their ends.
Inputs may be any that keep to these rules, and one draw needn't show every extreme that they name: `validity`: the last sample of the whole batch is real. `vectors`: batch norm gains lie in 0.5 to 1.6.
All inputs are finite; a program needn't handle non-finite values.
Results may differ from the reference program's by a relative error of at most 0.013.
Values may be sent and summed in bfloat16 or wider, within the bound.
No kernel may reach another device: no remote copies, remote signals or barrier semaphores. Data moves between devices by JAX's collectives and lax.ppermute only.
A program may use at most 512 MiB of HBM per device.

```python
import math
import jax
import jax.numpy as jnp
from jax import lax

C_IN = 256
C3 = 384
F6 = 4096
CLASSES = 10000
PCA_DIM = 256
GRID = 13
STEP = 10
FC_IN = 13824
SAMPLES = 256


def draw_validity(key, part):
    key = jax.random.fold_in(key, 11)
    draws = jax.random.randint(key, (SAMPLES,), 0, 900)
    position = jnp.arange(SAMPLES)
    limit = 300 + 600 * (position + 1) // SAMPLES
    return (draws < limit).astype(jnp.int32)


def draw_vectors(key, part):
    key = jax.random.fold_in(key, 12)
    first_key, second_key = jax.random.split(key)
    gains = jax.random.uniform(first_key, (C3,), jnp.float32, 0.5, 1.5)
    others = 0.3 * jax.random.truncated_normal(second_key, -5.0, 5.0, (C3 + F6 + CLASSES,), jnp.float32)
    return jnp.concatenate([gains, others]).astype(jnp.float32)


def draw_vector_state(key, part):
    key = jax.random.fold_in(key, 13)
    level = jnp.concatenate([jnp.full((2 * C3,), 0.00085 * SAMPLES, jnp.float32), jnp.full((F6,), 0.0002 * SAMPLES, jnp.float32), jnp.full((CLASSES,), 0.1, jnp.float32)])
    factor = jnp.exp(jax.random.uniform(key, (2 * C3 + F6 + CLASSES,), jnp.float32, 0.0, 1.3862944))
    return (level * factor).astype(jnp.float32)


def set_ends(drawn, own_key, low, high):
    index_at = [jax.random.randint(jax.random.fold_in(own_key, axis), (), 0, length) for axis, length in enumerate(drawn.shape)]
    widest = drawn.shape.index(max(drawn.shape))
    next_to = index_at[:widest] + [(index_at[widest] + 1) % drawn.shape[widest]] + index_at[widest + 1:]
    return drawn.at[tuple(index_at)].set(low).at[tuple(next_to)].set(high)


def shard_levels(own_key, dims, cuts, low, high):
    def one(dim, shards_of):
        steps = jax.random.uniform(jax.random.fold_in(jax.random.fold_in(own_key, 6), dim), (shards_of,), jnp.float32, low / len(cuts), high / len(cuts))
        return jnp.repeat(jnp.exp(steps), dims[dim] // shards_of).reshape((-1,) + (1,) * (len(dims) - dim - 1))

    gain = one(*cuts[0])
    for cut in cuts[1:]:
        gain = gain * one(*cut)
    return gain


def normal_values(key, dims, scale, most, pieces=(), held_as=jnp.bfloat16):
    gain = shard_levels(key, dims, pieces, -0.22, 0.18) if pieces else 1.0
    result = jax.random.normal(key, dims, jnp.float32) * scale * gain
    return jnp.minimum(jnp.maximum(result, -most), most).astype(held_as)


def setup_inputs(seed: int = 0) -> dict:
    splits = jax.random.split(jax.random.key(seed), 16)
    return {
        "stem_maps": normal_values(splits[0], (SAMPLES, GRID, GRID, C_IN), 1.0, 6.0, ((0, 32),)),
        "validity": draw_validity(jax.random.fold_in(splits[15], 71), 0),
        "labels": set_ends(jax.random.randint(splits[2], (SAMPLES,), 0, CLASSES), jax.random.fold_in(splits[2], 1), 0, CLASSES - 1).astype(jnp.int32),
        "conv_weight": normal_values(splits[3], (9 * C_IN, C3), (9 * C_IN) ** -0.5, 0.125, (), jnp.float32),
        "fc6_weight": normal_values(splits[4], (FC_IN, F6), (FC_IN // 6) ** -0.5, 0.125, ((0, 8),), jnp.float32),
        "head_weight": normal_values(splits[5], (F6, CLASSES), (F6 // 16) ** -0.5, 0.375, ((0, 8),), jnp.float32),
        "vectors": draw_vectors(jax.random.fold_in(splits[15], 71), 0),
        "pca_matrix": normal_values(splits[7], (F6, PCA_DIM), F6 ** -0.5, 0.09375, ((0, 8),), jnp.float32),
        "conv_row_state": jnp.clip(jnp.exp(jax.random.uniform(splits[8], (9 * C_IN,), jnp.float32, math.log(0.128), math.log(0.512))), 0.128, 0.512),
        "conv_col_state": jnp.clip(jnp.exp(jax.random.uniform(splits[9], (C3,), jnp.float32, math.log(0.128), math.log(0.512))), 0.128, 0.512),
        "fc6_row_state": jnp.clip(jnp.exp(math.log(0.03072) - 1.3862944 * jax.random.uniform(splits[10], (FC_IN,), jnp.float32) ** shard_levels(splits[10], (FC_IN,), ((0, 8),), -0.2, 0.2)), 0.00768, 0.03072),
        "fc6_col_state": jnp.clip(jnp.exp(jax.random.uniform(splits[11], (F6,), jnp.float32, math.log(0.00768), math.log(0.03072))), 0.00768, 0.03072),
        "head_row_state": jnp.clip(jnp.exp(math.log(0.004778667) - 1.3862944 * jax.random.uniform(splits[12], (F6,), jnp.float32) ** shard_levels(splits[12], (F6,), ((0, 8),), -0.2, 0.2)), 0.0011946667, 0.004778667),
        "head_col_state": jnp.clip(jnp.exp(jax.random.uniform(splits[13], (CLASSES,), jnp.float32, math.log(0.07), math.log(0.28))), 0.07, 0.28),
        "vector_state": draw_vector_state(jax.random.fold_in(splits[15], 71), 0),
    }


EPSILON = 1e-05
TINY = 1e-30
RATE = 0.5
FLOOR = 0.001
NORM_EPS = 1e-06
HIGHEST = lax.Precision.HIGHEST

@jax.custom_vjp
def low(v):
    return lax.optimization_barrier(v.astype(jnp.bfloat16)).astype(jnp.float32)

@jax.custom_vjp
def low_back(v):
    return v

def low_keep(v):
    return (low(v), None)

def low_pass(kept, grad):
    return (grad,)

def back_keep(v):
    return (v, None)

def back_low(kept, grad):
    return (low(grad),)
low.defvjp(low_keep, low_pass)
low_back.defvjp(back_keep, back_low)

def pool_table(grid):
    pooled_grid = (grid - 1) // 2
    pixel_index = jnp.arange(grid * grid)
    pooled_cell = jnp.arange(pooled_grid * pooled_grid)
    pixel_row = (pixel_index // grid)[:, None]
    pixel_col = (pixel_index % grid)[:, None]
    cell_row = (pooled_cell // pooled_grid)[None, :]
    cell_col = (pooled_cell % pooled_grid)[None, :]
    inside_rows = (pixel_row >= 2 * cell_row) & (pixel_row <= 2 * cell_row + 2)
    inside_cols = (pixel_col >= 2 * cell_col) & (pixel_col <= 2 * cell_col + 2)
    return (inside_rows & inside_cols).astype(jnp.float32) / 9.0

def forward(conv_w, fc6_w, head_w, vectors, stem_f, mask_values, label_hits, sample_weight):
    samples, grid = (stem_f.shape[0], stem_f.shape[1])
    pixels = grid * grid
    channels = conv_w.shape[1]
    hidden_width = fc6_w.shape[1]
    kernel = low(conv_w).reshape(3, 3, stem_f.shape[3], channels)
    conv_out = lax.conv_general_dilated(stem_f, kernel, (1, 1), 'SAME', dimension_numbers=('NHWC', 'HWIO', 'NHWC'), precision=HIGHEST)
    conv_out = low_back(conv_out).reshape(samples, pixels, channels)
    pixel_mask = mask_values[:, None, None]
    pixel_total = pixels * jnp.sum(mask_values)
    center = lax.optimization_barrier(jnp.sum(conv_out * pixel_mask, axis=(0, 1))) / pixel_total
    variance = lax.optimization_barrier(jnp.sum(conv_out * conv_out * pixel_mask, axis=(0, 1))) / pixel_total - center * center
    bn_gain = vectors[:channels]
    bn_shift = vectors[channels:2 * channels]
    bias_hidden = vectors[2 * channels:2 * channels + hidden_width]
    bias_head = vectors[2 * channels + hidden_width:]
    normed = (conv_out - center) * lax.rsqrt(variance + EPSILON)
    activated = jax.nn.silu(normed * bn_gain + bn_shift)
    pooled = jnp.einsum('spc,pq->sqc', activated, pool_table(grid), precision=HIGHEST).reshape(samples, -1)
    pre_hidden = low_back(jnp.dot(low(pooled), low(fc6_w), precision=HIGHEST) + bias_hidden)
    feats = low(jax.nn.silu(pre_hidden))
    logits = low_back(jnp.dot(feats, low(head_w), precision=HIGHEST) + bias_head)
    log_total = jax.nn.logsumexp(logits, axis=1)
    target = lax.optimization_barrier(jnp.sum(logits * label_hits, axis=1))
    return (jnp.sum(sample_weight * (log_total - target)), feats)

def factor_update(gradient, weight, row_state, col_state, decay):
    squared = gradient * gradient + TINY
    row_new = decay * row_state + (1.0 - decay) * lax.optimization_barrier(jnp.mean(squared, axis=1))
    col_new = decay * col_state + (1.0 - decay) * lax.optimization_barrier(jnp.mean(squared, axis=0))
    second = row_new[:, None] * col_new[None, :] / jnp.mean(row_new)
    scale = RATE * jnp.maximum(FLOOR, jnp.sqrt(jnp.mean(weight * weight)))
    return (row_new, col_new, weight - scale * gradient * lax.rsqrt(second))

def vector_update(gradient, values, state, decay, seg_widths):
    state_new = decay * state + (1.0 - decay) * (gradient * gradient + TINY)
    scales = []
    offset = 0
    for seg_width in seg_widths:
        segment = values[offset:offset + seg_width]
        scales.append(jnp.full((seg_width,), 1.0, jnp.float32) * (RATE * jnp.maximum(FLOOR, jnp.sqrt(jnp.mean(segment * segment)))))
        offset += seg_width
    return (state_new, values - jnp.concatenate(scales) * gradient * lax.rsqrt(state_new))

def reference(stem_maps, validity, labels, conv_weight, fc6_weight, head_weight, vectors, pca_matrix, conv_row_state, conv_col_state, fc6_row_state, fc6_col_state, head_row_state, head_col_state, vector_state):
    decay = 1.0 - STEP ** (-0.8)
    mask_values = validity.astype(jnp.float32)
    label_hits = (labels[:, None] == jnp.arange(CLASSES)[None, :]).astype(jnp.float32)
    label_counts = lax.optimization_barrier(jnp.sum(label_hits * mask_values[:, None], axis=0))
    sample_weight = mask_values / jnp.maximum(lax.optimization_barrier(jnp.sum(label_hits * label_counts[None, :], axis=1)), 1.0)
    stem_f = stem_maps.astype(jnp.float32)

    def loss_of(conv_w, fc6_w, head_w, vec):
        return forward(conv_w, fc6_w, head_w, vec, stem_f, mask_values, label_hits, sample_weight)
    loss_sum, pullback, feats = jax.vjp(loss_of, conv_weight, fc6_weight, head_weight, vectors, has_aux=True)
    conv_grad, fc6_grad, head_grad, vector_grad = pullback(jnp.ones((), jnp.float32))
    loss_weight = jnp.sum(sample_weight)
    conv_row_new, conv_col_new, conv_new = factor_update(conv_grad, conv_weight, conv_row_state, conv_col_state, decay)
    fc6_row_new, fc6_col_new, fc6_new = factor_update(fc6_grad, fc6_weight, fc6_row_state, fc6_col_state, decay)
    head_row_new, head_col_new, head_new = factor_update(head_grad, head_weight, head_row_state, head_col_state, decay)
    vector_state_new, vector_new = vector_update(vector_grad, vectors, vector_state, decay, (C3, C3, F6, CLASSES))
    kept = feats * mask_values[:, None]
    valid_count = jnp.sum(mask_values)
    feat_center = lax.optimization_barrier(jnp.sum(kept, axis=0)) / valid_count
    feat_var = lax.optimization_barrier(jnp.sum(kept * kept, axis=0)) / valid_count - feat_center * feat_center
    standard = low((kept - feat_center) * lax.rsqrt(feat_var + EPSILON))
    projected = jnp.dot(standard, low(pca_matrix), precision=HIGHEST)
    embedded = projected * lax.rsqrt(lax.optimization_barrier(jnp.sum(projected * projected, axis=1, keepdims=True)) + NORM_EPS)
    return (loss_sum, loss_weight, embedded, conv_grad, conv_row_new, conv_col_new, conv_new, fc6_grad, fc6_row_new, fc6_col_new, fc6_new, head_grad, head_row_new, head_col_new, head_new, vector_grad, vector_state_new, vector_new)
```

```python
import jax
import jax.numpy as jnp
from jax import lax
from jax.sharding import PartitionSpec as P

STEP = 10


EPSILON = 1e-05
TINY = 1e-30
RATE = 0.5
FLOOR = 0.001
NORM_EPS = 1e-06
HIGHEST = lax.Precision.HIGHEST
ALL = ("grp", "wide")


def pool_table(grid):
    pooled_grid = (grid - 1) // 2
    pixel_index = jnp.arange(grid * grid)
    pooled_cell = jnp.arange(pooled_grid * pooled_grid)
    pixel_row = (pixel_index // grid)[:, None]
    pixel_col = (pixel_index % grid)[:, None]
    cell_row = (pooled_cell // pooled_grid)[None, :]
    cell_col = (pooled_cell % pooled_grid)[None, :]
    inside_rows = (pixel_row >= 2 * cell_row) & (pixel_row <= 2 * cell_row + 2)
    inside_cols = (pixel_col >= 2 * cell_col) & (pixel_col <= 2 * cell_col + 2)
    return (inside_rows & inside_cols).astype(jnp.float32) / 9.0


def silu_slope(values):
    sigma = jax.nn.sigmoid(values)
    return sigma * (1.0 + values * (1.0 - sigma))


def patches_of(stem_maps):
    grid = stem_maps.shape[1]
    padded = jnp.pad(stem_maps, ((0, 0), (1, 1), (1, 1), (0, 0)))
    shifted = [
        padded[:, row_shift : row_shift + grid, col_shift : col_shift + grid, :]
        for row_shift in range(3)
        for col_shift in range(3)
    ]
    return jnp.concatenate(shifted, axis=3).reshape(-1, 9 * stem_maps.shape[3])


def contract_rows(left, right):
    return lax.dot_general(
        left, right, (((0,), (0,)), ((), ())), preferred_element_type=jnp.float32
    )


def exchange(blocks, axis):
    return lax.all_to_all(blocks, axis, 0, 0, tiled=True)


def gather(values, axis):
    return exchange(
        jnp.broadcast_to(values[None], (lax.axis_size(axis),) + values.shape), axis
    )


def total(values, axis):
    return jnp.sum(gather(values, axis).astype(jnp.float32), axis=0)


def vector_step(gradient, values, state, decay, seg_widths):
    state_new = decay * state + (1.0 - decay) * (gradient * gradient + TINY)
    scales = []
    offset = 0
    for seg_width in seg_widths:
        segment = values[offset : offset + seg_width]
        scales.append(
            jnp.full((seg_width,), 1.0, jnp.float32)
            * (RATE * jnp.maximum(FLOOR, jnp.sqrt(jnp.mean(segment * segment))))
        )
        offset += seg_width
    return (state_new, values - jnp.concatenate(scales) * gradient * lax.rsqrt(state_new))


def row_stats(gradient, row_state, decay):
    squared = gradient * gradient + TINY
    row_new = decay * row_state + (1.0 - decay) * jnp.mean(squared, axis=1)
    return row_new, jnp.sum(squared, axis=0)


def factor_step(gradient, weight, row_new, col_new, row_mean, weight_rms):
    scale = RATE * jnp.maximum(FLOOR, weight_rms)
    by_row = scale * lax.rsqrt(row_new / row_mean)
    return weight - (by_row[:, None] * gradient) * lax.rsqrt(col_new)[None, :]


def per_device(
    stem_maps,
    validity,
    labels,
    conv_weight,
    fc6_weight,
    head_weight,
    vectors,
    pca_matrix,
    conv_row_state,
    conv_col_state,
    fc6_row_state,
    fc6_col_state,
    head_row_state,
    head_col_state,
    vector_state,
):
    bf16, f32 = jnp.bfloat16, jnp.float32
    samples, grid = stem_maps.shape[0], stem_maps.shape[1]
    pixels = grid * grid
    channels = conv_weight.shape[1]
    fc_rows, hidden = fc6_weight.shape
    head_rows, classes = head_weight.shape
    wide_count = lax.axis_size("wide")
    grp_count = lax.axis_size("grp")
    count = wide_count * grp_count
    group = samples * wide_count
    my_wide = lax.axis_index("wide")
    my_grp = lax.axis_index("grp")
    decay = 1.0 - STEP ** (-0.8)
    mask = validity.astype(f32)

    bn_gain = vectors[:channels]
    bn_shift = vectors[channels : 2 * channels]
    bias_hidden = vectors[2 * channels : 2 * channels + hidden]
    bias_head = vectors[2 * channels + hidden :]

    patches = patches_of(stem_maps)
    conv_out = jnp.dot(
        patches, conv_weight.astype(bf16), preferred_element_type=f32
    ).reshape(samples, pixels, channels)
    pixel_mask = mask[:, None, None]
    packed = jnp.concatenate(
        [
            jnp.sum(conv_out * pixel_mask, axis=(0, 1)),
            jnp.sum(conv_out * conv_out * pixel_mask, axis=(0, 1)),
            mask,
            labels.astype(f32),
        ]
    )
    everyone = gather(packed, ALL)
    col_sums = jnp.sum(everyone[:, :channels], axis=0)
    col_squares = jnp.sum(everyone[:, channels : 2 * channels], axis=0)
    mask_all = everyone[:, 2 * channels : 2 * channels + samples].reshape(-1)
    labels_all = everyone[:, 2 * channels + samples :].reshape(-1)
    valid_count = jnp.sum(mask_all)
    same = labels.astype(f32)[:, None] == labels_all[None, :]
    label_count = jnp.sum(jnp.where(same, mask_all[None, :], 0.0), axis=1)
    sample_weight = mask / jnp.maximum(label_count, 1.0)

    pixel_total = valid_count * pixels
    center = col_sums / pixel_total
    inv_std = lax.rsqrt(col_squares / pixel_total - center * center + EPSILON)
    normed = (conv_out - center) * inv_std
    bn_out = normed * bn_gain + bn_shift
    pool_map = pool_table(grid)
    pooled = jnp.einsum(
        "spc,pq->sqc", jax.nn.silu(bn_out), pool_map, precision=HIGHEST
    ).reshape(samples, -1)
    pooled_low = pooled.astype(bf16)

    pooled_rows = exchange(
        pooled_low.reshape(samples, wide_count, fc_rows).transpose(1, 0, 2), "wide"
    ).reshape(group, fc_rows)
    fc6_low = fc6_weight.astype(bf16)
    pre_part = jnp.dot(pooled_rows, fc6_low, preferred_element_type=f32).astype(bf16)
    pre_hidden = jnp.sum(
        exchange(
            pre_part.reshape(group, wide_count, head_rows).transpose(1, 0, 2), "wide"
        ).astype(f32),
        axis=0,
    ) + lax.dynamic_slice_in_dim(bias_hidden, my_wide * head_rows, head_rows)
    feats = jax.nn.silu(pre_hidden).astype(bf16)

    head_low = head_weight.astype(bf16)
    logit_part = jnp.dot(feats, head_low, preferred_element_type=f32).astype(bf16)
    logits = (
        jnp.sum(
            exchange(logit_part.reshape(wide_count, samples, classes), "wide").astype(f32),
            axis=0,
        )
        + bias_head
    )
    label_hits = (labels[:, None] == jnp.arange(classes)[None, :]).astype(f32)
    top_logit = jnp.max(logits, axis=1, keepdims=True)
    expo = jnp.exp(logits - top_logit)
    totals = jnp.sum(expo, axis=1, keepdims=True)
    log_total = top_logit[:, 0] + jnp.log(totals[:, 0])
    loss_part = jnp.sum(sample_weight * (log_total - jnp.sum(logits * label_hits, axis=1)))
    weight_part = jnp.sum(sample_weight)
    grad_logits = (sample_weight[:, None] * (expo / totals - label_hits)).astype(bf16)

    logits_group = gather(grad_logits, "wide").reshape(group, classes)
    grad_feats = lax.dot_general(
        logits_group, head_low, (((1,), (1,)), ((), ())), preferred_element_type=f32
    )
    grad_pre = (grad_feats * silu_slope(pre_hidden)).astype(bf16)
    pre_group = gather(grad_pre, "wide").transpose(1, 0, 2).reshape(group, hidden)
    grad_pooled_rows = lax.dot_general(
        pre_group, fc6_low, (((1,), (1,)), ((), ())), preferred_element_type=f32
    ).astype(bf16)
    grad_pooled = (
        exchange(grad_pooled_rows.reshape(wide_count, samples, fc_rows), "wide")
        .transpose(1, 0, 2)
        .reshape(samples, -1, channels)
        .astype(f32)
    )
    grad_act = jnp.einsum("sqc,pq->spc", grad_pooled, pool_map, precision=HIGHEST)
    grad_bn = grad_act * silu_slope(bn_out)
    sums = total(
        jnp.concatenate(
            [
                jnp.sum(grad_bn * normed, axis=(0, 1)),
                jnp.sum(grad_bn, axis=(0, 1)),
                jnp.stack([loss_part, weight_part]),
            ]
        ),
        ALL,
    )
    grad_gain, grad_shift = sums[:channels], sums[channels : 2 * channels]
    grad_conv_out = (
        (
            inv_std
            * bn_gain
            * (grad_bn - pixel_mask * (grad_shift + normed * grad_gain) / pixel_total)
        )
        .astype(bf16)
        .reshape(-1, channels)
    )
    conv_part = contract_rows(patches, grad_conv_out).astype(bf16)
    conv_rows = conv_weight.shape[0]
    conv_share = jnp.sum(
        exchange(conv_part.reshape(count, conv_rows // count, channels), ALL).astype(f32),
        axis=0,
    ).astype(bf16)
    conv_grad = gather(conv_share, ALL).reshape(conv_rows, channels).astype(f32)

    pooled_all = gather(pooled_rows, "grp").reshape(-1, fc_rows)
    feats_all = gather(feats, "grp").reshape(-1, head_rows)
    logits_all = gather(logits_group, "grp").reshape(-1, classes)
    pre_all = gather(pre_group, "grp").reshape(-1, hidden)
    fc6_grad = contract_rows(pooled_all, pre_all)
    head_grad = contract_rows(feats_all, logits_all)
    grad_bias_hidden = jnp.sum(pre_all.astype(f32), axis=0)
    grad_bias_head = jnp.sum(logits_all.astype(f32), axis=0)
    vector_grad = jnp.concatenate([grad_gain, grad_shift, grad_bias_hidden, grad_bias_head])

    conv_row_new, conv_col_part = row_stats(conv_grad, conv_row_state, decay)
    conv_col_new = decay * conv_col_state + (1.0 - decay) * conv_col_part / conv_rows
    conv_new = factor_step(
        conv_grad,
        conv_weight,
        conv_row_new,
        conv_col_new,
        jnp.mean(conv_row_new),
        jnp.sqrt(jnp.mean(conv_weight * conv_weight)),
    )
    fc6_row_new, fc6_col_part = row_stats(fc6_grad, fc6_row_state, decay)
    head_row_new, head_col_part = row_stats(head_grad, head_row_state, decay)
    stats = total(
        jnp.concatenate(
            [
                fc6_col_part,
                head_col_part,
                jnp.stack(
                    [
                        jnp.sum(fc6_row_new),
                        jnp.sum(fc6_weight * fc6_weight),
                        jnp.sum(head_row_new),
                        jnp.sum(head_weight * head_weight),
                    ]
                ),
            ]
        ),
        "wide",
    )
    fc6_rows_total = fc_rows * wide_count
    fc6_col_new = decay * fc6_col_state + (1.0 - decay) * stats[:hidden] / fc6_rows_total
    head_col_new = (
        decay * head_col_state + (1.0 - decay) * stats[hidden : hidden + classes] / hidden
    )
    factors = stats[hidden + classes :]
    fc6_new = factor_step(
        fc6_grad,
        fc6_weight,
        fc6_row_new,
        fc6_col_new,
        factors[0] / fc6_rows_total,
        jnp.sqrt(factors[1] / (fc6_rows_total * hidden)),
    )
    head_new = factor_step(
        head_grad,
        head_weight,
        head_row_new,
        head_col_new,
        factors[2] / hidden,
        jnp.sqrt(factors[3] / (hidden * classes)),
    )
    vector_state_new, vector_new = vector_step(
        vector_grad, vectors, vector_state, decay, (channels, channels, hidden, classes)
    )

    kept_all = feats_all.astype(f32) * mask_all[:, None]
    feat_center = jnp.sum(kept_all, axis=0) / valid_count
    feat_square = jnp.sum(kept_all * kept_all, axis=0) / valid_count
    feat_scale = lax.rsqrt(feat_square - feat_center * feat_center + EPSILON)
    group_mask = lax.dynamic_slice_in_dim(mask_all, my_grp * group, group)
    kept = feats.astype(f32) * group_mask[:, None]
    standard = ((kept - feat_center) * feat_scale).astype(bf16)
    projected = jnp.dot(standard, pca_matrix.astype(bf16), preferred_element_type=f32)
    projected = jnp.sum(
        exchange(
            projected.astype(bf16).reshape(wide_count, samples, -1), "wide"
        ).astype(f32),
        axis=0,
    )
    embedded = projected * lax.rsqrt(
        jnp.sum(projected * projected, axis=1, keepdims=True) + NORM_EPS
    )
    return (
        sums[2 * channels],
        sums[2 * channels + 1],
        embedded,
        conv_grad,
        conv_row_new,
        conv_col_new,
        conv_new,
        fc6_grad,
        fc6_row_new,
        fc6_col_new,
        fc6_new,
        head_grad,
        head_row_new,
        head_col_new,
        head_new,
        vector_grad,
        vector_state_new,
        vector_new,
    )


def solution(mesh):
    in_specs = (
        P(("grp", "wide"), None, None, None),
        P(("grp", "wide")),
        P(("grp", "wide")),
        P(),
        P("wide", None),
        P("wide", None),
        P(),
        P("wide", None),
        P(),
        P(),
        P("wide"),
        P(),
        P("wide"),
        P(),
        P(),
    )
    out_specs = (
        P(),
        P(),
        P(("grp", "wide"), None),
        P(),
        P(),
        P(),
        P(),
        P("wide", None),
        P("wide"),
        P(),
        P("wide", None),
        P("wide", None),
        P("wide"),
        P(),
        P("wide", None),
        P(),
        P(),
        P(),
    )
    return jax.shard_map(
        per_device, mesh=mesh, in_specs=in_specs, out_specs=out_specs, check_vma=False
    )
```

```python
import functools

import jax
import jax.numpy as jnp
from jax import lax
from jax.experimental import pallas as pl
from jax.experimental.pallas import tpu as pltpu
from jax.sharding import PartitionSpec as P

STEP = 10


EPSILON = 1e-05
TINY = 1e-30
RATE = 0.5
FLOOR = 0.001
NORM_EPS = 1e-06
HIGHEST = lax.Precision.HIGHEST
ALL = ("grp", "wide")


def block_of(rows, row_bytes, limit):
    sizes = [n for n in range(16, rows + 1, 16) if rows % n == 0 and n * row_bytes <= limit]
    return max(sizes) if sizes else rows


def vmem(megabytes):
    return pltpu.CompilerParams(vmem_limit_bytes=megabytes << 20)


def follow_kernel(*refs):
    refs[-1][...] = refs[0][...]


def follow(values, *others):
    return pl.pallas_call(
        follow_kernel,
        in_specs=[pl.BlockSpec(memory_space=pltpu.VMEM)]
        + [pl.BlockSpec(memory_space=pl.ANY)] * len(others),
        out_specs=pl.BlockSpec(memory_space=pltpu.VMEM),
        out_shape=jax.ShapeDtypeStruct(values.shape, values.dtype),
        name="follow",
    )(values, *others)


def low_kernel(weight_ref, _, low_ref, square_ref):
    @pl.when(pl.program_id(0) == 0)
    def _():
        square_ref[...] = jnp.zeros_like(square_ref)

    weight = weight_ref[...]
    low_ref[...] = weight.astype(jnp.bfloat16)
    square_ref[...] += jnp.sum((weight * weight).reshape(-1, 8, weight.shape[1]), axis=0)


def in_hbm(array):
    return pltpu.with_memory_space_constraint(array, pltpu.HBM)


HBM = pl.BlockSpec(memory_space=pltpu.HBM)
VMEM = pl.BlockSpec(memory_space=pltpu.VMEM)


def spans(length, step):
    return [(first, min(first + step, length)) for first in range(0, length, step)]


def fetch_all(pairs, arrived):
    copies = [
        pltpu.make_async_copy(source, target, arrived.at[number])
        for number, (source, target) in enumerate(pairs)
    ]
    for copy in copies:
        copy.start()
    return copies


def low_and_squares(weight, first, cols, start):
    rows = weight.shape[0]
    block = block_of(rows, 4 * cols, 4 << 20)
    low, squares = pl.pallas_call(
        low_kernel,
        grid=(rows // block,),
        in_specs=[
            pl.BlockSpec((block, cols), lambda i: (i, first // cols)),
            pl.BlockSpec(memory_space=pl.ANY),
        ],
        out_specs=[
            pl.BlockSpec((block, cols), lambda i: (i, 0)),
            pl.BlockSpec((8, cols), lambda i: (0, 0)),
        ],
        out_shape=[
            pltpu.HBM((rows, cols), jnp.bfloat16),
            jax.ShapeDtypeStruct((8, cols), jnp.float32),
        ],
        compiler_params=vmem(24),
        name="low_and_squares",
    )(in_hbm(weight), start)
    return low, squares


def fc6_kernel(rows_ref, left_ref, right_ref, out_ref, buffer, arrived):
    half = left_ref.shape[1]
    blocks = [
        (ref, first, last, side * half)
        for side, ref in enumerate((left_ref, right_ref))
        for first, last in spans(half, 512)
    ]
    copies = fetch_all(
        [
            (ref.at[:, first:last], buffer.at[:, base + first : base + last])
            for ref, first, last, base in blocks
        ],
        arrived,
    )
    for copy, (_, first, last, base) in zip(copies, blocks):
        copy.wait()
        out_ref[:, base + first : base + last] = jnp.dot(
            rows_ref[...],
            buffer[:, base + first : base + last],
            preferred_element_type=jnp.float32,
        ).astype(out_ref.dtype)


def fc6_forward(values, left, right):
    depth, half = left.shape
    blocks = 2 * len(spans(half, 512))
    return pl.pallas_call(
        fc6_kernel,
        in_specs=[VMEM, HBM, HBM],
        out_specs=VMEM,
        out_shape=jax.ShapeDtypeStruct((values.shape[0], 2 * half), jnp.bfloat16),
        scratch_shapes=[
            pltpu.VMEM((depth, 2 * half), left.dtype),
            pltpu.SemaphoreType.DMA((blocks,)),
        ],
        compiler_params=vmem(32),
        name="fc6_forward",
    )(values, in_hbm(left), in_hbm(right))


def fc6_back_kernel(grad_ref, left_ref, right_ref, *refs):
    out_ref, buffer, arrived = refs[-3:]
    rows, half = left_ref.shape
    blocks = spans(rows, 256)
    copies = fetch_all(
        [
            (ref.at[first:last], buffer.at[side, first:last])
            for first, last in blocks
            for side, ref in enumerate((left_ref, right_ref))
        ],
        arrived,
    )
    for number, (first, last) in enumerate(blocks):
        part = 0.0
        for side in range(2):
            copies[2 * number + side].wait()
            part += lax.dot_general(
                grad_ref[:, side * half : (side + 1) * half],
                buffer[side, first:last],
                (((1,), (1,)), ((), ())),
                preferred_element_type=jnp.float32,
            )
        out_ref[:, first:last] = part.astype(out_ref.dtype)


def fc6_backward(grad, left, right, *others):
    rows, half = left.shape
    return pl.pallas_call(
        fc6_back_kernel,
        in_specs=[VMEM, HBM, HBM] + [pl.BlockSpec(memory_space=pl.ANY)] * len(others),
        out_specs=VMEM,
        out_shape=jax.ShapeDtypeStruct((grad.shape[0], rows), jnp.bfloat16),
        scratch_shapes=[
            pltpu.VMEM((2, rows, half), left.dtype),
            pltpu.SemaphoreType.DMA((2 * len(spans(rows, 256)),)),
        ],
        compiler_params=vmem(32),
        name="fc6_backward",
    )(grad, in_hbm(left), in_hbm(right), *others)


def head_kernel(feats_ref, weight_ref, out_ref, buffer, arrived):
    blocks = spans(weight_ref.shape[0], 2048)
    copies = fetch_all(
        [(weight_ref.at[first:last], buffer.at[first:last]) for first, last in blocks], arrived
    )
    for copy, (first, last) in zip(copies, blocks):
        copy.wait()
        out_ref[:, first:last] = lax.dot_general(
            feats_ref[...],
            buffer[first:last],
            (((1,), (1,)), ((), ())),
            preferred_element_type=jnp.float32,
        ).astype(out_ref.dtype)


def head_forward(feats, weight):
    classes = weight.shape[0]
    return pl.pallas_call(
        head_kernel,
        in_specs=[VMEM, HBM],
        out_specs=VMEM,
        out_shape=jax.ShapeDtypeStruct((feats.shape[0], classes), jnp.bfloat16),
        scratch_shapes=[
            pltpu.VMEM(weight.shape, weight.dtype),
            pltpu.SemaphoreType.DMA((len(spans(classes, 2048)),)),
        ],
        compiler_params=vmem(32),
        name="head_forward",
    )(feats, in_hbm(weight))


def head_back_kernel(grad_ref, weight_ref, pre_ref, *refs):
    out_ref, buffer, arrived = refs[-3:]
    blocks = spans(weight_ref.shape[0], 2048)
    copies = fetch_all(
        [(weight_ref.at[first:last], buffer.at[first:last]) for first, last in blocks], arrived
    )
    total = 0.0
    for copy, (first, last) in zip(copies, blocks):
        copy.wait()
        total += jnp.dot(
            grad_ref[:, first:last], buffer[first:last], preferred_element_type=jnp.float32
        )
    out_ref[...] = (total * silu_slope(pre_ref[...])).astype(out_ref.dtype)


def head_backward(grad, weight, pre_hidden):
    return pl.pallas_call(
        head_back_kernel,
        in_specs=[VMEM, HBM, VMEM],
        out_specs=VMEM,
        out_shape=jax.ShapeDtypeStruct(pre_hidden.shape, jnp.bfloat16),
        scratch_shapes=[
            pltpu.VMEM(weight.shape, weight.dtype),
            pltpu.SemaphoreType.DMA((len(spans(weight.shape[0], 2048)),)),
        ],
        compiler_params=vmem(32),
        name="head_backward",
    )(grad, in_hbm(weight), pre_hidden)


def pieces(matrix):
    first = matrix.astype(jnp.bfloat16)
    rest = matrix - first.astype(jnp.float32)
    second = rest.astype(jnp.bfloat16)
    third = (rest - second.astype(jnp.float32)).astype(jnp.bfloat16)
    return first, second, third


def quadratic(matrix, values):
    product = sum(
        jnp.dot(piece, values, preferred_element_type=jnp.float32) for piece in pieces(matrix)
    )
    return jnp.sum(product * values.astype(jnp.float32), axis=0, keepdims=True)


def row_stats_kernel(decay, rows, sum_ref, left_ref, right_ref, gram_ref, state_ref, new_ref, scale_ref):
    right = right_ref[...]
    cols = right.shape[1]
    right_gram = lax.dot_general(
        right, right, (((1,), (1,)), ((), ())), preferred_element_type=jnp.float32
    )
    mean_square = jnp.sum(gram_ref[...] * right_gram) / (rows * cols)
    row_new = decay * state_ref[...] + (1.0 - decay) * (
        quadratic(right_gram, left_ref[...]) / cols + TINY
    )
    row_mean = decay * sum_ref[0] / rows + (1.0 - decay) * (mean_square + TINY)
    new_ref[...] = row_new
    scale_ref[...] = sum_ref[1] * lax.rsqrt(row_new / row_mean)


def row_stats(left, right, left_gram, row_state, sums, rows, decay):
    row = jax.ShapeDtypeStruct((1, left.shape[1]), jnp.float32)
    whole = pl.BlockSpec(memory_space=pltpu.VMEM)
    new, scale = pl.pallas_call(
        functools.partial(row_stats_kernel, decay, rows),
        in_specs=[pl.BlockSpec(memory_space=pltpu.SMEM)] + [whole] * 4,
        out_specs=[whole] * 2,
        out_shape=[row, row],
        compiler_params=vmem(40),
        name="row_stats",
    )(sums, left, right, left_gram, row_state[None, :])
    return new[0], scale


def row_update_kernel(left_ref, right_ref, weight_ref, row_ref, col_ref, _, grad_ref, new_ref, mark_ref):
    mark_ref[...] = jnp.zeros_like(mark_ref)
    cols = weight_ref.shape[1]
    step = 512 if cols % 512 == 0 else cols
    left = left_ref[...]
    row = row_ref[...]
    for at in range(0, cols, step):
        grad = jnp.dot(left, right_ref[:, at : at + step], preferred_element_type=jnp.float32)
        grad_ref[:, at : at + step] = grad
        new_ref[:, at : at + step] = (
            weight_ref[:, at : at + step] - (row * grad) * col_ref[:, at : at + step]
        )


def row_update(left, right, weight, row_scale, col_scale, start):
    rows, cols = weight.shape
    depth = left.shape[1]
    block = block_of(rows, 4 * cols, 8 << 20)
    out = jax.ShapeDtypeStruct((rows, cols), jnp.float32)
    return pl.pallas_call(
        row_update_kernel,
        grid=(rows // block,),
        in_specs=[
            pl.BlockSpec((block, depth), lambda i: (i, 0)),
            pl.BlockSpec((depth, cols), lambda i: (0, 0)),
            pl.BlockSpec((block, cols), lambda i: (i, 0)),
            pl.BlockSpec((block, 1), lambda i: (i, 0)),
            pl.BlockSpec((1, cols), lambda i: (0, 0)),
            pl.BlockSpec(memory_space=pl.ANY),
        ],
        out_specs=[pl.BlockSpec((block, cols), lambda i: (i, 0))] * 2
        + [pl.BlockSpec((8, 128), lambda i: (0, 0))],
        out_shape=[out, out, jax.ShapeDtypeStruct((8, 128), jnp.float32)],
        compiler_params=vmem(60),
        name="row_update",
    )(left, right, in_hbm(weight), row_scale[:, None], col_scale[None, :], start)


def col_update_kernel(
    decay, rows, left_ref, right_ref, weight_ref, gram_ref, state_ref, scale_ref, _, grad_ref, new_ref, col_ref, sum_ref
):
    left = left_ref[...]
    grad = lax.dot_general(
        left, right_ref[...], (((0,), (0,)), ((), ())), preferred_element_type=jnp.float32
    )
    grad_ref[...] = grad
    col_new = decay * state_ref[...] + (1.0 - decay) * (
        quadratic(gram_ref[...], left) / rows + TINY
    )
    col_ref[...] = col_new
    sum_ref[...] = jnp.sum(left.astype(jnp.float32), axis=0, keepdims=True)
    block, width = grad.shape
    by_class = jnp.broadcast_to(lax.rsqrt(col_new), (128, block)).T
    for at in range(0, width, 128):
        new_ref[:, at : at + 128] = weight_ref[:, at : at + 128] - (
            by_class * grad[:, at : at + 128]
        ) * scale_ref[:, at : at + 128]


def col_update(left, right, weight, right_gram, col_state, row_scale, rows, decay, start):
    classes, width = weight.shape
    depth = left.shape[0]
    block = 2048
    out = jax.ShapeDtypeStruct((classes, width), jnp.float32)
    line = jax.ShapeDtypeStruct((1, classes), jnp.float32)
    grad, new, col_new, sums = pl.pallas_call(
        functools.partial(col_update_kernel, decay, rows),
        grid=(pl.cdiv(classes, block),),
        in_specs=[
            pl.BlockSpec((depth, block), lambda i: (0, i)),
            pl.BlockSpec((depth, width), lambda i: (0, 0)),
            pl.BlockSpec((block, width), lambda i: (i, 0)),
            pl.BlockSpec((depth, depth), lambda i: (0, 0)),
            pl.BlockSpec((1, block), lambda i: (0, i)),
            pl.BlockSpec((1, width), lambda i: (0, 0)),
            pl.BlockSpec(memory_space=pl.ANY),
        ],
        out_specs=[pl.BlockSpec((block, width), lambda i: (i, 0))] * 2
        + [pl.BlockSpec((1, block), lambda i: (0, i))] * 2,
        out_shape=[out, out, line, line],
        compiler_params=vmem(60),
        name="col_update",
    )(left, right, in_hbm(weight), right_gram, col_state[None, :], row_scale, start)
    return grad, new, col_new[0], sums[0]


def pad_into(maps_ref, padded_ref):
    rows, cols = maps_ref.shape[0], maps_ref.shape[1]
    padded_ref[...] = jnp.zeros_like(padded_ref)
    padded_ref[1 : rows + 1, 1 : cols + 1] = maps_ref[...].astype(jnp.float32)


def conv_grad_kernel(maps_ref, grad_ref, normed_ref, mask_ref, factor_ref, *refs):
    out_ref, padded_ref = refs[-2:]
    rows, cols, samples, depth = maps_ref.shape
    pad_into(maps_ref, padded_ref)
    gain, shift_mean, gain_mean = factor_ref[0:1, :], factor_ref[1:2, :], factor_ref[2:3, :]
    by_sample = (rows * cols, samples, grad_ref.shape[1])
    mean = (shift_mean + normed_ref[...] * gain_mean).reshape(by_sample) * mask_ref[...]
    grad = (gain * (grad_ref[...] - mean.reshape(grad_ref.shape))).astype(jnp.bfloat16)
    for shift in range(9):
        down, right = shift // 3, shift % 3
        shifted = padded_ref[down : down + rows, right : right + cols]
        out_ref[shift * depth : (shift + 1) * depth] = lax.dot_general(
            shifted.reshape(-1, depth).astype(jnp.bfloat16),
            grad,
            (((0,), (0,)), ((), ())),
            preferred_element_type=jnp.float32,
        ).astype(out_ref.dtype)


def conv_grad_of(maps, grad_bn, normed, mask, factors, *others):
    rows, cols, samples, depth = maps.shape
    return pl.pallas_call(
        conv_grad_kernel,
        in_specs=[pl.BlockSpec(memory_space=pltpu.VMEM)] * 5
        + [pl.BlockSpec(memory_space=pl.ANY)] * len(others),
        out_shape=jax.ShapeDtypeStruct((9 * depth, grad_bn.shape[1]), jnp.bfloat16),
        scratch_shapes=[pltpu.VMEM((rows + 2, cols + 2, samples, depth), jnp.float32)],
        compiler_params=vmem(56),
        name="conv_grad",
    )(maps, grad_bn, normed, mask[:, None], factors, *others)


def silu_slope(values):
    sigma = jax.nn.sigmoid(values)
    return sigma * (1.0 + values * (1.0 - sigma))


def norm_kernel(conv_ref, factor_ref, *refs):
    normed_ref, pooled_ref = refs[-2:]
    cells = (normed_ref.shape[0] - 1) // 2
    center, inv_std = factor_ref[0:1, :], factor_ref[1:2, :]
    gain, shift = factor_ref[2:3, :], factor_ref[3:4, :]
    normed = (conv_ref[...] - center) * inv_std
    normed_ref[...] = normed.reshape(normed_ref.shape)
    act = jax.nn.silu(normed * gain + shift).reshape(normed_ref.shape)
    for row in range(cells):
        line = act[2 * row] + act[2 * row + 1] + act[2 * row + 2]
        for col in range(cells):
            window = line[2 * col] + line[2 * col + 1] + line[2 * col + 2]
            pooled_ref[row * cells + col] = (window / 9.0).astype(jnp.bfloat16)


def norm_and_pool(conv_out, factors, grid, samples, *others):
    channels = conv_out.shape[1]
    cells = ((grid - 1) // 2) ** 2
    whole = pl.BlockSpec(memory_space=pltpu.VMEM)
    return pl.pallas_call(
        norm_kernel,
        in_specs=[whole] * 2 + [pl.BlockSpec(memory_space=pl.ANY)] * len(others),
        out_specs=[whole] * 2,
        out_shape=[
            jax.ShapeDtypeStruct((grid, grid, samples, channels), jnp.float32),
            jax.ShapeDtypeStruct((cells, samples, channels), jnp.bfloat16),
        ],
        compiler_params=vmem(24),
        name="norm_and_pool",
    )(conv_out, factors, *others)


def norm_back_kernel(pooled_ref, normed_ref, factor_ref, grad_ref, sum_ref):
    grid, _, samples, channels = normed_ref.shape
    cells = (grid - 1) // 2
    gain, shift = factor_ref[2:3, :], factor_ref[3:4, :]

    def windows(pixel):
        return [cell for cell in range(cells) if 2 * cell <= pixel <= 2 * cell + 2]

    with_normed = jnp.zeros((samples, channels), jnp.float32)
    alone = jnp.zeros((samples, channels), jnp.float32)
    for row in range(grid):
        line = [
            sum(pooled_ref[cell * cells + col].astype(jnp.float32) for cell in windows(row)) / 9.0
            for col in range(cells)
        ]
        for col in range(grid):
            act = sum(line[cell] for cell in windows(col))
            normed = normed_ref[row, col]
            grad = act * silu_slope(normed * gain + shift)
            grad_ref[row, col] = grad
            with_normed += grad * normed
            alone += grad
    sum_ref[0:1, :] = jnp.sum(with_normed, axis=0, keepdims=True)
    sum_ref[1:2, :] = jnp.sum(alone, axis=0, keepdims=True)


def norm_backward(grad_pooled, normed, factors):
    return pl.pallas_call(
        norm_back_kernel,
        out_shape=[
            jax.ShapeDtypeStruct(normed.shape, jnp.float32),
            jax.ShapeDtypeStruct((2, normed.shape[3]), jnp.float32),
        ],
        compiler_params=vmem(24),
        name="norm_backward",
    )(grad_pooled, normed, factors)


def conv_kernel(maps_ref, weight_ref, mask_ref, out_ref, sum_ref, padded_ref, patch_ref):
    rows, cols, samples, depth = maps_ref.shape
    pad_into(maps_ref, padded_ref)
    for shift in range(9):
        down, right = shift // 3, shift % 3
        shifted = padded_ref[down : down + rows, right : right + cols]
        patch_ref[:, shift * depth : (shift + 1) * depth] = shifted.reshape(-1, depth).astype(
            jnp.bfloat16
        )
    out = jnp.dot(
        patch_ref[...],
        weight_ref[...].astype(jnp.bfloat16),
        preferred_element_type=jnp.float32,
    )
    out_ref[...] = out
    mask = mask_ref[...]
    by_sample = out.reshape(rows * cols, samples, out.shape[1])
    sum_ref[0:1, :] = jnp.sum(jnp.sum(by_sample, axis=0) * mask, axis=0, keepdims=True)
    sum_ref[1:2, :] = jnp.sum(
        jnp.sum(by_sample * by_sample, axis=0) * mask, axis=0, keepdims=True
    )


def conv_of(maps, weight, mask):
    rows, cols, samples, depth = maps.shape
    channels = weight.shape[1]
    pixels = rows * cols * samples
    return pl.pallas_call(
        conv_kernel,
        out_shape=[
            jax.ShapeDtypeStruct((pixels, channels), jnp.float32),
            jax.ShapeDtypeStruct((2, channels), jnp.float32),
        ],
        scratch_shapes=[
            pltpu.VMEM((rows + 2, cols + 2, samples, depth), jnp.float32),
            pltpu.VMEM((pixels, 9 * depth), jnp.bfloat16),
        ],
        compiler_params=vmem(32),
        name="conv",
    )(maps, weight, mask[:, None])


def sum_kernel(blocks_ref, *refs):
    refs[-1][...] = jnp.sum(blocks_ref[...].astype(jnp.float32), axis=0).astype(jnp.bfloat16)


def sum_blocks(blocks, *others):
    return pl.pallas_call(
        sum_kernel,
        in_specs=[pl.BlockSpec(memory_space=pltpu.VMEM)]
        + [pl.BlockSpec(memory_space=pl.ANY)] * len(others),
        out_shape=jax.ShapeDtypeStruct(blocks.shape[1:], jnp.bfloat16),
        compiler_params=vmem(24),
        name="sum_blocks",
    )(blocks, *others)


def conv_update_kernel(
    decay, core_ref, own_ref, other_ref, weight_ref, row_ref, col_ref, *refs
):
    grad_ref, new_ref, row_new_ref, col_new_ref = refs[-4:]
    rows, channels = weight_ref.shape
    half = rows // 2
    first = core_ref[0] == 0
    own = own_ref[...].astype(jnp.float32)
    other = other_ref[...].astype(jnp.float32)
    grad_ref[:half] = jnp.where(first, own, other)
    grad_ref[half:] = jnp.where(first, other, own)
    grad = grad_ref[...]
    weight = weight_ref[...]
    squared = grad * grad
    row_new = decay * row_ref[...] + (1.0 - decay) * (
        jnp.sum(squared, axis=1, keepdims=True) / channels + TINY
    )
    col_new = decay * col_ref[...] + (1.0 - decay) * (
        jnp.sum(squared, axis=0, keepdims=True) / rows + TINY
    )
    row_new_ref[...] = row_new
    col_new_ref[...] = col_new
    mean_square = jnp.sum(jnp.sum(weight * weight, axis=0, keepdims=True)) / (rows * channels)
    row_mean = jnp.sum(row_new) / rows
    scale = RATE * jnp.maximum(FLOOR, jnp.sqrt(mean_square))
    by_row = scale * lax.rsqrt(row_new / row_mean)
    new_ref[...] = weight - (by_row * grad) * lax.rsqrt(col_new)


def conv_update(core, own, other, weight, row_state, col_state, decay, *others):
    rows, channels = weight.shape
    whole = pl.BlockSpec(memory_space=pltpu.VMEM)
    out = jax.ShapeDtypeStruct(weight.shape, jnp.float32)
    grad, new, row_new, col_new = pl.pallas_call(
        functools.partial(conv_update_kernel, decay),
        in_specs=[pl.BlockSpec(memory_space=pltpu.SMEM)]
        + [whole] * 5
        + [pl.BlockSpec(memory_space=pl.ANY)] * len(others),
        out_specs=[whole] * 4,
        out_shape=[
            out,
            out,
            jax.ShapeDtypeStruct((rows, 1), jnp.float32),
            jax.ShapeDtypeStruct((1, channels), jnp.float32),
        ],
        compiler_params=vmem(40),
        name="conv_update",
    )(core[None], own, other, weight, row_state[:, None], col_state[None, :], *others)
    return grad, new, row_new[:, 0], col_new[0]


def contract_rows(left, right):
    return lax.dot_general(
        left, right, (((0,), (0,)), ((), ())), preferred_element_type=jnp.float32
    )


def exchange(blocks, axis, groups=None):
    return lax.all_to_all(blocks, axis, 0, 0, tiled=True, axis_index_groups=groups)


def gather(values, axis, size, groups=None):
    return exchange(jnp.broadcast_to(values[None], (size,) + values.shape), axis, groups)


class Ring:
    def __init__(self, axis, size, inner):
        self.axis, self.size, self.inner = axis, size, inner
        self.length = lax.axis_size(axis)
        self.own = lax.axis_index(axis) // inner % size

    def other(self, index, shift):
        own = index // self.inner % self.size
        return index + ((own + shift) % self.size - own) * self.inner

    def fetch(self, values, shift):
        pairs = [(self.other(index, shift), index) for index in range(self.length)]
        return lax.ppermute(values, self.axis, pairs)

    def stack(self, parts):
        if self.size == 2:
            first = self.own == 0
            parts = [jnp.where(first, parts[0], parts[1]), jnp.where(first, parts[1], parts[0])]
            return jnp.stack(parts)
        return jnp.roll(jnp.stack(parts), self.own, axis=0)

    def gather(self, values):
        return self.stack([values] + [self.fetch(values, k) for k in range(1, self.size)])

    def scatter_sum(self, blocks, dim):
        def block(shift):
            return lax.dynamic_index_in_dim(
                blocks, (self.own + shift) % self.size, dim, keepdims=False
            )

        result = block(0).astype(jnp.float32)
        for shift in range(1, self.size):
            result += self.fetch(block(-shift), shift).astype(jnp.float32)
        return result


def double_sum(values, axis):
    size, inner = lax.axis_size(axis), 1
    while inner < size:
        pairs = [(index, index ^ inner) for index in range(size)]
        values = values + lax.ppermute(values, axis, pairs)
        inner *= 2
    return values


def vector_step(gradient, values, state, decay, seg_widths):
    state_new = decay * state + (1.0 - decay) * (gradient * gradient + TINY)
    scales = []
    offset = 0
    for seg_width in seg_widths:
        segment = values[offset : offset + seg_width]
        scales.append(
            jnp.full((seg_width,), 1.0, jnp.float32)
            * (RATE * jnp.maximum(FLOOR, jnp.sqrt(jnp.mean(segment * segment))))
        )
        offset += seg_width
    return (state_new, values - jnp.concatenate(scales) * gradient * lax.rsqrt(state_new))


def gram(values):
    return lax.dot_general(
        values, values, (((1,), (1,)), ((), ())), preferred_element_type=jnp.float32
    )


def square_sums(gram_matrix, values):
    values = values.astype(jnp.float32)
    return jnp.sum(values * jnp.dot(gram_matrix, values, precision=HIGHEST), axis=0)


def factor_scales(
    left, right, left_gram, right_gram, row_state, col_state, sums, rows, decay
):
    cols = right.shape[1]
    row_new = decay * row_state + (1.0 - decay) * (square_sums(right_gram, left) / cols + TINY)
    col_new = decay * col_state + (1.0 - decay) * (square_sums(left_gram, right) / rows + TINY)
    mean_square = jnp.sum(left_gram * right_gram) / (rows * cols)
    row_mean = decay * sums[0] / rows + (1.0 - decay) * (mean_square + TINY)
    scale = RATE * jnp.maximum(FLOOR, jnp.sqrt(sums[1] / (rows * cols)))
    return row_new, col_new, scale * lax.rsqrt(row_new / row_mean), lax.rsqrt(col_new)


def plain_update(left, right, weight, row_scale, col_scale):
    grad = contract_rows(left, right)
    return grad, weight - (row_scale[:, None] * grad) * col_scale[None, :]


def per_device(
    stem_maps,
    validity,
    labels,
    conv_weight,
    fc6_weight,
    head_weight,
    vectors,
    pca_matrix,
    conv_row_state,
    conv_col_state,
    fc6_row_state,
    fc6_col_state,
    head_row_state,
    head_col_state,
    vector_state,
):
    bf16, f32 = jnp.bfloat16, jnp.float32
    samples, grid = stem_maps.shape[0], stem_maps.shape[1]
    pixels = grid * grid
    channels = conv_weight.shape[1]
    fc_rows, hidden = fc6_weight.shape
    head_rows, classes = head_weight.shape
    wide_count = lax.axis_size("wide")
    grp_count = lax.axis_size("grp")
    count = wide_count * grp_count
    group = samples * wide_count
    my_wide = lax.axis_index("wide")
    decay = 1.0 - STEP ** (-0.8)
    mask = validity.astype(f32)

    core = Ring("grp", 2, 1)
    planes = Ring("grp", grp_count // 2, 2)
    near = Ring("wide", wide_count // 4, 1)
    far = Ring("wide", 4, wide_count // 4)

    bn_gain = vectors[:channels]
    bn_shift = vectors[channels : 2 * channels]
    bias_hidden = vectors[2 * channels : 2 * channels + hidden]
    bias_head = vectors[2 * channels + hidden :]

    maps = stem_maps.transpose(1, 2, 0, 3)
    conv_out, conv_sums = conv_of(maps, conv_weight, mask)
    packed = jnp.concatenate([conv_sums.reshape(-1), mask, labels.astype(f32)])
    everyone = gather(packed, ALL, count)
    fc6_left, left_squares = low_and_squares(fc6_weight, 0, hidden // 2, packed)
    stat_sums = jnp.sum(everyone[:, : 2 * channels], axis=0)
    mask_all = everyone[:, 2 * channels : 2 * channels + samples].reshape(-1)
    labels_all = everyone[:, 2 * channels + samples :].reshape(-1)
    valid_count = jnp.sum(mask_all)

    pixel_total = valid_count * pixels
    center = stat_sums[:channels] / pixel_total
    inv_std = lax.rsqrt(stat_sums[channels:] / pixel_total - center * center + EPSILON)
    factors = jnp.stack([center, inv_std, bn_gain, bn_shift])
    normed, pooled = norm_and_pool(conv_out, factors, grid, samples, left_squares)
    pooled_low = pooled.transpose(1, 0, 2).reshape(samples, -1)

    pooled_blocks = pooled_low.reshape(samples, wide_count, fc_rows).transpose(1, 0, 2)
    pooled_rows = exchange(pooled_blocks, "wide").reshape(group, fc_rows)
    fc6_right, right_squares = low_and_squares(
        fc6_weight, hidden // 2, hidden // 2, pooled_blocks
    )
    pre_part = fc6_forward(pooled_rows, fc6_left, fc6_right)
    pre_blocks = exchange(
        pre_part.reshape(group, wide_count, head_rows).transpose(1, 0, 2), "wide"
    )
    head_low, head_squares = low_and_squares(head_weight.T, 0, head_rows, pre_part)
    pre_hidden = jnp.sum(pre_blocks.astype(f32), axis=0)
    pre_hidden += lax.dynamic_slice_in_dim(bias_hidden, my_wide * head_rows, head_rows)
    feats = jax.nn.silu(pre_hidden).astype(bf16)

    logit_part = head_forward(feats, head_low)
    logit_blocks = exchange(logit_part.reshape(wide_count, samples, classes), "wide")

    pooled_all = lax.all_gather(pooled_rows, "grp", axis=0, tiled=True)
    feats_all = lax.all_gather(feats, "grp", axis=0, tiled=True)
    pooled_gram, feats_gram = gram(pooled_all), gram(feats_all)
    numbers = jnp.stack(
        [
            jnp.sum(fc6_row_state),
            jnp.sum(left_squares + right_squares),
            jnp.sum(head_row_state),
            jnp.sum(head_squares),
        ]
    )
    all_samples = pooled_all.shape[0]
    per_share = 2 * all_samples // grp_count
    numbers = jnp.pad(numbers, (0, all_samples - numbers.size))
    both_part = jnp.concatenate([pooled_gram, feats_gram])
    both_part = lax.dynamic_slice_in_dim(
        both_part, lax.axis_index("grp") * per_share, per_share
    )
    both_part = jnp.concatenate([both_part, numbers[None]])
    both = lax.all_gather(double_sum(both_part, "wide"), "grp")
    sums = both[0, per_share]
    both = both[:, :per_share].reshape(-1, all_samples)
    kept_all = feats_all.astype(f32) * mask_all[:, None]
    feat_center = jnp.sum(kept_all, axis=0) / valid_count
    feat_square = jnp.sum(kept_all * kept_all, axis=0) / valid_count
    feat_scale = lax.rsqrt(feat_square - feat_center * feat_center + EPSILON)
    group_mask = lax.dynamic_slice_in_dim(mask_all, lax.axis_index("grp") * group, group)
    kept = feats.astype(f32) * group_mask[:, None]
    standard = ((kept - feat_center) * feat_scale).astype(bf16)
    projected = jnp.dot(standard, pca_matrix.astype(bf16), preferred_element_type=f32)
    projected = projected.astype(bf16)
    logits = jnp.sum(logit_blocks.astype(f32), axis=0) + bias_head

    same = labels.astype(f32)[:, None] == labels_all[None, :]
    label_count = jnp.sum(jnp.where(same, mask_all[None, :], 0.0), axis=1)
    sample_weight = mask / jnp.maximum(label_count, 1.0)
    sample_weight = follow(sample_weight, both_part)
    label_hits = labels[:, None] == jnp.arange(classes)[None, :]
    top_logit = jnp.max(logits, axis=1, keepdims=True)
    expo = jnp.exp(logits - top_logit)
    totals = jnp.sum(expo, axis=1, keepdims=True)
    log_total = top_logit[:, 0] + jnp.log(totals[:, 0])
    label_logit = jnp.sum(jnp.where(label_hits, logits, 0.0), axis=1)
    loss_part = jnp.sum(sample_weight * (log_total - label_logit))
    weight_part = jnp.sum(sample_weight)
    grad_logits = (
        sample_weight[:, None] * (expo / totals - label_hits.astype(f32))
    ).astype(bf16)

    logits_group = gather(grad_logits, "wide", wide_count).reshape(group, classes)
    grad_pre = head_backward(logits_group, head_low, pre_hidden)
    rows = samples * projected.shape[1] // head_rows
    pre_blocks = exchange(
        jnp.concatenate(
            [
                jnp.broadcast_to(grad_pre, (wide_count,) + grad_pre.shape),
                projected.reshape(wide_count, rows, head_rows),
            ],
            axis=1,
        ),
        "wide",
    )
    projected = pre_blocks[:, group:].reshape(wide_count, samples, -1)
    pre_blocks = pre_blocks[:, :group]
    pre_group = pre_blocks.transpose(1, 0, 2).reshape(group, hidden)
    logits_all = lax.all_gather(logits_group, "grp", axis=0, tiled=True)
    pre_all = core.gather(planes.gather(pre_group))
    pre_all = jnp.swapaxes(pre_all, 0, 1).reshape(-1, hidden)

    fc6_row_new, fc6_col_new, fc6_by_row, fc6_by_col = factor_scales(
        pooled_all,
        pre_all,
        both[:all_samples],
        gram(pre_all),
        fc6_row_state,
        fc6_col_state,
        sums[:2],
        fc_rows * wide_count,
        decay,
    )
    grad_pooled_rows = fc6_backward(pre_group, fc6_left, fc6_right, both)
    grad_pooled = exchange(grad_pooled_rows.reshape(wide_count, samples, fc_rows), "wide")
    grad_pooled = grad_pooled.transpose(1, 0, 2).reshape(samples, -1, channels)
    grad_bn, bn_sums = norm_backward(grad_pooled.transpose(1, 0, 2), normed, factors)
    bn_sums = jnp.concatenate([bn_sums.reshape(-1), jnp.stack([loss_part, weight_part])])
    bn_sums = jnp.sum(gather(bn_sums, ALL, count), axis=0)
    grad_gain, grad_shift = bn_sums[:channels], bn_sums[channels : 2 * channels]
    conv_factors = jnp.stack(
        [inv_std * bn_gain, grad_shift / pixel_total, grad_gain / pixel_total]
    )
    conv_part = conv_grad_of(
        maps,
        grad_bn.reshape(-1, channels),
        normed.reshape(-1, channels),
        mask,
        conv_factors,
        fc6_by_col,
        fc6_by_row,
    )
    conv_rows = conv_weight.shape[0]
    chips = count // 2
    same_core = [
        [grp * wide_count + wide for grp in range(first, grp_count, 2) for wide in range(wide_count)]
        for first in range(2)
    ]
    conv_half = core.scatter_sum(conv_part.reshape(2, conv_rows // 2, channels), 0)
    conv_half = conv_half.astype(bf16)
    conv_blocks = exchange(conv_half.reshape(chips, -1, channels), ALL, same_core)

    grad_bias_hidden = jnp.sum(pre_all.astype(f32), axis=0)
    feats_gram = both[all_samples:]
    if pre_all.shape[0] <= 512:
        fc6_grad, fc6_new, mark = row_update(
            pooled_all.T, pre_all, fc6_weight, fc6_by_row, fc6_by_col, conv_half
        )
        conv_share = sum_blocks(conv_blocks, mark)
        head_step = RATE * jnp.maximum(FLOOR, jnp.sqrt(sums[3] / (hidden * classes)))
        head_row_new, head_by_row = row_stats(
            feats_all,
            logits_all,
            feats_gram,
            head_row_state,
            jnp.stack([sums[2], head_step]),
            hidden,
            decay,
        )
        head_grad, head_new, head_col_new, grad_bias_head = col_update(
            logits_all,
            feats_all,
            head_weight.T,
            feats_gram,
            head_col_state,
            head_by_row,
            hidden,
            decay,
            conv_share,
        )
        mark = head_col_new
        head_grad, head_new = head_grad.T, head_new.T
    else:
        conv_share = sum_blocks(conv_blocks)
        mark = conv_share
        fc6_grad, fc6_new = plain_update(pooled_all, pre_all, fc6_weight, fc6_by_row, fc6_by_col)
        head_row_new, head_col_new, head_by_row, head_by_col = factor_scales(
            feats_all,
            logits_all,
            feats_gram,
            gram(logits_all),
            head_row_state,
            head_col_state,
            sums[2:],
            hidden,
            decay,
        )
        head_grad, head_new = plain_update(
            feats_all, logits_all, head_weight, head_by_row, head_by_col
        )
        grad_bias_head = jnp.sum(logits_all.astype(f32), axis=0)
    conv_own = gather(conv_share, ALL, chips, same_core).reshape(-1, channels)
    conv_own = follow(conv_own, mark)
    conv_grad, conv_new, conv_row_new, conv_col_new = conv_update(
        core.own,
        conv_own,
        core.fetch(conv_own, 1),
        conv_weight,
        conv_row_state,
        conv_col_state,
        decay,
    )
    vector_grad = jnp.concatenate([grad_gain, grad_shift, grad_bias_hidden, grad_bias_head])
    vector_state_new, vector_new = vector_step(
        vector_grad, vectors, vector_state, decay, (channels, channels, hidden, classes)
    )

    projected = jnp.sum(projected.astype(f32), axis=0)
    embedded = projected * lax.rsqrt(
        jnp.sum(projected * projected, axis=1, keepdims=True) + NORM_EPS
    )
    return (
        bn_sums[2 * channels],
        bn_sums[2 * channels + 1],
        embedded,
        conv_grad,
        conv_row_new,
        conv_col_new,
        conv_new,
        fc6_grad,
        fc6_row_new,
        fc6_col_new,
        fc6_new,
        head_grad,
        head_row_new,
        head_col_new,
        head_new,
        vector_grad,
        vector_state_new,
        vector_new,
    )


def solution(mesh):
    in_specs = (
        P(("grp", "wide"), None, None, None),
        P(("grp", "wide")),
        P(("grp", "wide")),
        P(),
        P("wide", None),
        P("wide", None),
        P(),
        P("wide", None),
        P(),
        P(),
        P("wide"),
        P(),
        P("wide"),
        P(),
        P(),
    )
    out_specs = (
        P(),
        P(),
        P(("grp", "wide"), None),
        P(),
        P(),
        P(),
        P(),
        P("wide", None),
        P("wide"),
        P(),
        P("wide", None),
        P("wide", None),
        P("wide"),
        P(),
        P("wide", None),
        P(),
        P(),
        P(),
    )
    return jax.shard_map(
        per_device, mesh=mesh, in_specs=in_specs, out_specs=out_specs, check_vma=False
    )
```

```python
import functools

import jax
import jax.numpy as jnp
from jax import lax
from jax.experimental import pallas as pl
from jax.experimental.pallas import tpu as pltpu
from jax.sharding import PartitionSpec as P

STEP = 10


EPSILON = 1e-05
TINY = 1e-30
RATE = 0.5
FLOOR = 0.001
NORM_EPS = 1e-06
HIGHEST = lax.Precision.HIGHEST
ALL = ("grp", "wide")


def block_of(rows, row_bytes, limit):
    sizes = [n for n in range(16, rows + 1, 16) if rows % n == 0 and n * row_bytes <= limit]
    return max(sizes) if sizes else rows


def vmem(megabytes):
    return pltpu.CompilerParams(vmem_limit_bytes=megabytes << 20)


def follow_kernel(*refs):
    refs[-1][...] = refs[0][...]


def follow(values, *others):
    return pl.pallas_call(
        follow_kernel,
        in_specs=[pl.BlockSpec(memory_space=pltpu.VMEM)]
        + [pl.BlockSpec(memory_space=pl.ANY)] * len(others),
        out_specs=pl.BlockSpec(memory_space=pltpu.VMEM),
        out_shape=jax.ShapeDtypeStruct(values.shape, values.dtype),
        name="follow",
    )(values, *others)


def low_kernel(weight_ref, _, low_ref, square_ref):
    @pl.when(pl.program_id(0) == 0)
    def _():
        square_ref[...] = jnp.zeros_like(square_ref)

    weight = weight_ref[...]
    low_ref[...] = weight.astype(jnp.bfloat16)
    square_ref[...] += jnp.sum((weight * weight).reshape(-1, 8, weight.shape[1]), axis=0)


def in_hbm(array):
    return pltpu.with_memory_space_constraint(array, pltpu.HBM)


HBM = pl.BlockSpec(memory_space=pltpu.HBM)
VMEM = pl.BlockSpec(memory_space=pltpu.VMEM)


def spans(length, step):
    return [(first, min(first + step, length)) for first in range(0, length, step)]


class Fetch:
    def __init__(self, pairs, arrived, depth):
        self.copies = [
            pltpu.make_async_copy(source, target, arrived.at[number])
            for number, (source, target) in enumerate(pairs)
        ]
        self.depth, self.done = depth, 0
        for copy in self.copies[:depth]:
            copy.start()

    def wait(self):
        self.copies[self.done].wait()
        for copy in self.copies[self.done + self.depth : self.done + self.depth + 1]:
            copy.start()
        self.done += 1


def low_and_squares(weight, first, cols, start):
    rows = weight.shape[0]
    block = block_of(rows, 4 * cols, 4 << 20)
    low, squares = pl.pallas_call(
        low_kernel,
        grid=(rows // block,),
        in_specs=[
            pl.BlockSpec((block, cols), lambda i: (i, first // cols)),
            pl.BlockSpec(memory_space=pl.ANY),
        ],
        out_specs=[
            pl.BlockSpec((block, cols), lambda i: (i, 0)),
            pl.BlockSpec((8, cols), lambda i: (0, 0)),
        ],
        out_shape=[
            pltpu.HBM((rows, cols), jnp.bfloat16),
            jax.ShapeDtypeStruct((8, cols), jnp.float32),
        ],
        compiler_params=vmem(24),
        name="low_and_squares",
    )(in_hbm(weight), start)
    return low, squares


def fc6_kernel(rows_ref, left_ref, right_ref, out_ref, buffer, arrived):
    half = left_ref.shape[1]
    blocks = [
        (ref, first, last, side * half)
        for side, ref in enumerate((left_ref, right_ref))
        for first, last in spans(half, 512)
    ]
    fetch = Fetch(
        [
            (ref.at[:, first:last], buffer.at[:, base + first : base + last])
            for ref, first, last, base in blocks
        ],
        arrived,
        4,
    )
    for _, first, last, base in blocks:
        fetch.wait()
        out_ref[:, base + first : base + last] = jnp.dot(
            rows_ref[...],
            buffer[:, base + first : base + last],
            preferred_element_type=jnp.float32,
        ).astype(out_ref.dtype)


def fc6_forward(values, left, right):
    depth, half = left.shape
    blocks = 2 * len(spans(half, 512))
    return pl.pallas_call(
        fc6_kernel,
        in_specs=[VMEM, HBM, HBM],
        out_specs=VMEM,
        out_shape=jax.ShapeDtypeStruct((values.shape[0], 2 * half), jnp.bfloat16),
        scratch_shapes=[
            pltpu.VMEM((depth, 2 * half), left.dtype),
            pltpu.SemaphoreType.DMA((blocks,)),
        ],
        compiler_params=vmem(32),
        name="fc6_forward",
    )(values, in_hbm(left), in_hbm(right))


def fc6_back_kernel(grad_ref, left_ref, right_ref, *refs):
    out_ref, buffer, arrived = refs[-3:]
    rows, half = left_ref.shape
    blocks = spans(rows, 512)
    fetch = Fetch(
        [
            (ref.at[first:last], buffer.at[side, first:last])
            for first, last in blocks
            for side, ref in enumerate((left_ref, right_ref))
        ],
        arrived,
        4,
    )
    for first, last in blocks:
        part = 0.0
        for side in range(2):
            fetch.wait()
            part += lax.dot_general(
                grad_ref[:, side * half : (side + 1) * half],
                buffer[side, first:last],
                (((1,), (1,)), ((), ())),
                preferred_element_type=jnp.float32,
            )
        out_ref[:, first:last] = part.astype(out_ref.dtype)


def fc6_backward(grad, left, right, *others):
    rows, half = left.shape
    return pl.pallas_call(
        fc6_back_kernel,
        in_specs=[VMEM, HBM, HBM] + [pl.BlockSpec(memory_space=pl.ANY)] * len(others),
        out_specs=VMEM,
        out_shape=jax.ShapeDtypeStruct((grad.shape[0], rows), jnp.bfloat16),
        scratch_shapes=[
            pltpu.VMEM((2, rows, half), left.dtype),
            pltpu.SemaphoreType.DMA((2 * len(spans(rows, 512)),)),
        ],
        compiler_params=vmem(32),
        name="fc6_backward",
    )(grad, in_hbm(left), in_hbm(right), *others)


def head_kernel(feats_ref, weight_ref, out_ref, buffer, arrived):
    blocks = spans(weight_ref.shape[0], 1024)
    fetch = Fetch(
        [(weight_ref.at[first:last], buffer.at[first:last]) for first, last in blocks], arrived, 4
    )
    for first, last in blocks:
        fetch.wait()
        out_ref[:, first:last] = lax.dot_general(
            feats_ref[...],
            buffer[first:last],
            (((1,), (1,)), ((), ())),
            preferred_element_type=jnp.float32,
        ).astype(out_ref.dtype)


def head_forward(feats, weight):
    classes = weight.shape[0]
    return pl.pallas_call(
        head_kernel,
        in_specs=[VMEM, HBM],
        out_specs=VMEM,
        out_shape=jax.ShapeDtypeStruct((feats.shape[0], classes), jnp.bfloat16),
        scratch_shapes=[
            pltpu.VMEM(weight.shape, weight.dtype),
            pltpu.SemaphoreType.DMA((len(spans(classes, 1024)),)),
        ],
        compiler_params=vmem(32),
        name="head_forward",
    )(feats, in_hbm(weight))


def head_back_kernel(grad_ref, weight_ref, pre_ref, *refs):
    out_ref, grad_buffer, buffer, arrived = refs[-4:]
    blocks = spans(weight_ref.shape[0], 1024)
    fetch = Fetch(
        [(grad_ref, grad_buffer)]
        + [(weight_ref.at[first:last], buffer.at[first:last]) for first, last in blocks],
        arrived,
        5,
    )
    fetch.wait()
    total = 0.0
    for first, last in blocks:
        fetch.wait()
        total += jnp.dot(
            grad_buffer[:, first:last], buffer[first:last], preferred_element_type=jnp.float32
        )
    out_ref[...] = (total * silu_slope(pre_ref[...])).astype(out_ref.dtype)


def head_backward(grad, weight, pre_hidden, *others):
    return pl.pallas_call(
        head_back_kernel,
        in_specs=[HBM, HBM, VMEM] + [pl.BlockSpec(memory_space=pl.ANY)] * len(others),
        out_specs=VMEM,
        out_shape=jax.ShapeDtypeStruct(pre_hidden.shape, jnp.bfloat16),
        scratch_shapes=[
            pltpu.VMEM(grad.shape, grad.dtype),
            pltpu.VMEM(weight.shape, weight.dtype),
            pltpu.SemaphoreType.DMA((1 + len(spans(weight.shape[0], 1024)),)),
        ],
        compiler_params=vmem(32),
        name="head_backward",
    )(in_hbm(grad), in_hbm(weight), pre_hidden, *others)


def pieces(matrix):
    first = matrix.astype(jnp.bfloat16)
    rest = matrix - first.astype(jnp.float32)
    second = rest.astype(jnp.bfloat16)
    third = (rest - second.astype(jnp.float32)).astype(jnp.bfloat16)
    return first, second, third


def quadratic(matrix, values):
    product = sum(
        jnp.dot(piece, values, preferred_element_type=jnp.float32) for piece in pieces(matrix)
    )
    return jnp.sum(product * values.astype(jnp.float32), axis=0, keepdims=True)


def step_size(squares, count):
    return RATE * jnp.maximum(FLOOR, jnp.sqrt(squares / count))


def head_stats_kernel(
    decay,
    rows,
    sum_ref,
    left_ref,
    right_ref,
    gram_ref,
    state_ref,
    new_ref,
    scale_ref,
    total_ref,
    buffer,
    arrived,
):
    cols = right_ref.shape[1]
    blocks = spans(cols, 2048)
    fetch = Fetch(
        [(right_ref.at[:, first:last], buffer.at[:, first:last]) for first, last in blocks],
        arrived,
        len(blocks),
    )
    right_gram, totals = 0.0, []
    for first, last in blocks:
        fetch.wait()
        right = buffer[:, first:last]
        right_gram += lax.dot_general(
            right, right, (((1,), (1,)), ((), ())), preferred_element_type=jnp.float32
        )
        totals.append(jnp.sum(right.astype(jnp.float32), axis=0, keepdims=True))
    total_ref[...] = jnp.concatenate(totals, axis=1).reshape(cols)
    mean_square = jnp.sum(gram_ref[...] * right_gram) / (rows * cols)
    width = left_ref.shape[1]
    row_new = decay * state_ref[...].reshape(1, width) + (1.0 - decay) * (
        quadratic(right_gram, left_ref[...]) / cols + TINY
    )
    row_mean = decay * sum_ref[2] / rows + (1.0 - decay) * (mean_square + TINY)
    new_ref[...] = row_new.reshape(width)
    step = step_size(jnp.full(row_new.shape, sum_ref[3]), rows * cols)
    scale_ref[...] = step * lax.rsqrt(row_new / row_mean)


def head_stats(left, right, left_gram, row_state, sums, rows, decay):
    width, cols = left.shape[1], right.shape[1]
    smem = pl.BlockSpec(memory_space=pltpu.SMEM)
    return pl.pallas_call(
        functools.partial(head_stats_kernel, decay, rows),
        in_specs=[smem, VMEM, HBM, VMEM, VMEM],
        out_specs=[VMEM] * 3,
        out_shape=[
            jax.ShapeDtypeStruct((width,), jnp.float32),
            jax.ShapeDtypeStruct((1, width), jnp.float32),
            jax.ShapeDtypeStruct((cols,), jnp.float32),
        ],
        scratch_shapes=[
            pltpu.VMEM(right.shape, right.dtype),
            pltpu.SemaphoreType.DMA((len(spans(cols, 2048)),)),
        ],
        compiler_params=vmem(40),
        name="head_stats",
    )(sums, left, in_hbm(right), left_gram, row_state)


def fc6_stats_kernel(
    decay,
    rows,
    sum_ref,
    place_ref,
    left_ref,
    gram_ref,
    row_state_ref,
    col_state_ref,
    *refs,
):
    parts, refs = refs[:-6], refs[-6:]
    right_ref, row_new_ref, col_new_ref, row_scale_ref, col_scale_ref, total_ref = refs
    height, cols = parts[0].shape
    for number, part in enumerate(parts):
        at = pl.multiple_of(place_ref[number] * height, height)
        right_ref[pl.ds(at, height), :] = part[...]
    left_gram = gram_ref[...]
    width = left_ref.shape[1]
    col_state = col_state_ref[...].reshape(1, cols)
    right_gram, news, totals = 0.0, [], []
    for first, last in spans(cols, 512):
        right = right_ref[:, first:last]
        right_gram += lax.dot_general(
            right, right, (((1,), (1,)), ((), ())), preferred_element_type=jnp.float32
        )
        col_new = decay * col_state[:, first:last] + (1.0 - decay) * (
            quadratic(left_gram, right) / rows + TINY
        )
        col_scale_ref[:, first:last] = lax.rsqrt(col_new)
        news.append(col_new)
        totals.append(jnp.sum(right.astype(jnp.float32), axis=0, keepdims=True))
    col_new_ref[...] = jnp.concatenate(news, axis=1).reshape(cols)
    total_ref[...] = jnp.concatenate(totals, axis=1).reshape(cols)
    mean_square = jnp.sum(left_gram * right_gram) / (rows * cols)
    row_new = decay * row_state_ref[...].reshape(1, width) + (1.0 - decay) * (
        quadratic(right_gram, left_ref[...]) / cols + TINY
    )
    row_mean = decay * sum_ref[0] / rows + (1.0 - decay) * (mean_square + TINY)
    row_new_ref[...] = row_new.reshape(row_new_ref.shape)
    step = step_size(jnp.full(row_new.shape, sum_ref[1]), rows * cols)
    row_scale = step * lax.rsqrt(row_new / row_mean)
    row_scale_ref[...] = jnp.broadcast_to(row_scale, (128, row_scale.shape[1])).T


def fc6_stats(left, parts, places, left_gram, row_state, col_state, sums, rows, decay):
    height, cols = parts[0].shape
    width = left.shape[1]
    smem = pl.BlockSpec(memory_space=pltpu.SMEM)
    return pl.pallas_call(
        functools.partial(fc6_stats_kernel, decay, rows),
        in_specs=[smem] * 2 + [VMEM] * (4 + len(parts)),
        out_specs=[VMEM] * 6,
        out_shape=[
            jax.ShapeDtypeStruct((height * len(parts), cols), jnp.bfloat16),
            jax.ShapeDtypeStruct((width,), jnp.float32),
            jax.ShapeDtypeStruct((cols,), jnp.float32),
            jax.ShapeDtypeStruct((width, 128), jnp.float32),
            jax.ShapeDtypeStruct((1, cols), jnp.float32),
            jax.ShapeDtypeStruct((cols,), jnp.float32),
        ],
        compiler_params=vmem(40),
        name="fc6_stats",
    )(sums, places, left, left_gram, row_state, col_state, *parts)


def transpose_kernel(values_ref, out_ref):
    out_ref[...] = values_ref[...].T


def transposed(values):
    return pl.pallas_call(
        transpose_kernel,
        out_shape=jax.ShapeDtypeStruct(values.shape[::-1], values.dtype),
        compiler_params=vmem(24),
        name="transposed",
    )(values)


def row_update_kernel(left_ref, right_ref, weight_ref, row_ref, col_ref, _, grad_ref, new_ref, mark_ref):
    mark_ref[...] = jnp.zeros_like(mark_ref)
    left = left_ref[...]
    row = row_ref[...]
    for first, last in spans(weight_ref.shape[1], 512):
        grad = jnp.dot(left, right_ref[:, first:last], preferred_element_type=jnp.float32)
        grad_ref[:, first:last] = grad
        for at in range(first, last, 128):
            new_ref[:, at : at + 128] = weight_ref[:, at : at + 128] - (
                row * grad[:, at - first : at - first + 128]
            ) * col_ref[:, at : at + 128]


def row_update(left, right, weight, row_scale, col_scale, start):
    rows, cols = weight.shape
    depth = left.shape[1]
    block = block_of(rows, 4 * cols, 8 << 20)
    out = jax.ShapeDtypeStruct((rows, cols), jnp.float32)
    return pl.pallas_call(
        row_update_kernel,
        grid=(rows // block,),
        in_specs=[
            pl.BlockSpec((block, depth), lambda i: (i, 0)),
            pl.BlockSpec((depth, cols), lambda i: (0, 0)),
            pl.BlockSpec((block, cols), lambda i: (i, 0)),
            pl.BlockSpec((block, 128), lambda i: (i, 0)),
            pl.BlockSpec((1, cols), lambda i: (0, 0)),
            pl.BlockSpec(memory_space=pl.ANY),
        ],
        out_specs=[pl.BlockSpec((block, cols), lambda i: (i, 0))] * 2
        + [pl.BlockSpec((8, 128), lambda i: (0, 0))],
        out_shape=[out, out, jax.ShapeDtypeStruct((8, 128), jnp.float32)],
        compiler_params=vmem(60),
        name="row_update",
    )(left, right, in_hbm(weight), row_scale, col_scale, start)


def col_update_kernel(
    decay, rows, left_ref, right_ref, weight_ref, gram_ref, state_ref, scale_ref, *refs
):
    grad_ref, new_ref, col_ref = refs[-3:]
    left = left_ref[...]
    grad = lax.dot_general(
        left, right_ref[...], (((0,), (0,)), ((), ())), preferred_element_type=jnp.float32
    )
    grad_ref[...] = grad
    col_new = decay * state_ref[...].reshape(1, left.shape[1]) + (1.0 - decay) * (
        quadratic(gram_ref[...], left) / rows + TINY
    )
    col_ref[...] = col_new.reshape(col_ref.shape)
    block, width = grad.shape
    by_class = jnp.broadcast_to(lax.rsqrt(col_new), (128, block)).T
    for at in range(0, width, 128):
        new_ref[:, at : at + 128] = weight_ref[:, at : at + 128] - (
            by_class * grad[:, at : at + 128]
        ) * scale_ref[:, at : at + 128]


def col_update(steps, begun, left, right, weight, right_gram, col_state, row_scale, rows, decay, start):
    classes, width = weight.shape
    depth = left.shape[0]
    block = 2048
    first, last = steps
    out = jax.ShapeDtypeStruct((classes, width), jnp.float32)
    any_space = pl.BlockSpec(memory_space=pl.ANY)
    return pl.pallas_call(
        functools.partial(col_update_kernel, decay, rows),
        grid=(last - first,),
        in_specs=[
            pl.BlockSpec((depth, block), lambda i: (0, i + first)),
            pl.BlockSpec((depth, width), lambda i: (0, 0)),
            pl.BlockSpec((block, width), lambda i: (i + first, 0)),
            pl.BlockSpec((depth, depth), lambda i: (0, 0)),
            pl.BlockSpec((block,), lambda i: (i + first,)),
            pl.BlockSpec((1, width), lambda i: (0, 0)),
            any_space,
        ]
        + [any_space] * len(begun),
        out_specs=[pl.BlockSpec((block, width), lambda i: (i + first, 0))] * 2
        + [pl.BlockSpec((block,), lambda i: (i + first,))],
        out_shape=[out, out, jax.ShapeDtypeStruct((classes,), jnp.float32)],
        input_output_aliases={7 + number: number for number in range(len(begun))},
        compiler_params=vmem(60),
        name="col_update",
    )(left, right, in_hbm(weight), right_gram, col_state, row_scale, start, *begun)


def pad_into(maps_ref, padded_ref):
    rows, cols = maps_ref.shape[0], maps_ref.shape[1]
    padded_ref[...] = jnp.zeros_like(padded_ref)
    padded_ref[1 : rows + 1, 1 : cols + 1] = maps_ref[...].astype(jnp.float32)


def norm_sums_kernel(parts_ref, factor_ref, total_ref, *refs):
    sum_ref, conv_ref = refs[-2:]
    channels = factor_ref.shape[1]
    sums = jnp.sum(parts_ref[...], axis=0)
    sum_ref[...] = sums
    conv_ref[0:1, :] = factor_ref[0:1, :] * factor_ref[1:2, :]
    conv_ref[1:2, :] = sums[:, channels : 2 * channels] / total_ref[:, 0:1]
    conv_ref[2:3, :] = sums[:, :channels] / total_ref[:, 0:1]


def norm_sums(parts, factors, pixel_total, *others):
    width, channels = parts.shape[2], factors.shape[1]
    return pl.pallas_call(
        norm_sums_kernel,
        in_specs=[VMEM] * 3
        + [pl.BlockSpec(memory_space=pl.ANY)] * len(others),
        out_specs=[VMEM] * 2,
        out_shape=[
            jax.ShapeDtypeStruct((1, width), jnp.float32),
            jax.ShapeDtypeStruct((3, channels), jnp.float32),
        ],
        compiler_params=vmem(24),
        name="norm_sums",
    )(parts, factors, pixel_total, *others)


def conv_grad_kernel(core_ref, maps_ref, grad_ref, normed_ref, mask_ref, factor_ref, *refs):
    send_ref, keep_ref, padded_ref, grad_buffer, normed_buffer, out, arrived, left = refs[-8:]
    rows, cols, samples, depth = maps_ref.shape
    channels = grad_buffer.shape[3]
    fetch = Fetch([(grad_ref, grad_buffer), (normed_ref, normed_buffer)], arrived, 2)
    pad_into(maps_ref, padded_ref)
    gain, shift_mean, gain_mean = factor_ref[0:1, :], factor_ref[1:2, :], factor_ref[2:3, :]
    fetch.wait()
    fetch.wait()
    mean = (shift_mean + normed_buffer[...] * gain_mean) * mask_ref[...]
    grad = gain * (grad_buffer[...] - mean)
    grad = grad.reshape(-1, channels).T.astype(jnp.bfloat16)
    for shift in range(9):
        down, right = shift // 3, shift % 3
        shifted = padded_ref[down : down + rows, right : right + cols]
        out[shift * depth : (shift + 1) * depth] = jnp.dot(
            grad,
            shifted.reshape(-1, depth).astype(jnp.bfloat16),
            preferred_element_type=jnp.float32,
        ).T.astype(out.dtype)
    half = keep_ref.shape[0]
    own = pl.multiple_of(core_ref[0] * half, half)
    other = pl.multiple_of((1 - core_ref[0]) * half, half)
    copies = [
        pltpu.make_async_copy(out.at[pl.ds(other, half)], send_ref, left.at[0]),
        pltpu.make_async_copy(out.at[pl.ds(own, half)], keep_ref, left.at[1]),
    ]
    for copy in copies:
        copy.start()
    for copy in copies:
        copy.wait()


def conv_grad_of(core, maps, grad_bn, normed, mask, factors):
    rows, cols, samples, depth = maps.shape
    channels = normed.shape[3]
    buffer = pltpu.VMEM(normed.shape, jnp.float32)
    half = pltpu.HBM((9 * depth // 2, channels), jnp.bfloat16)
    return pl.pallas_call(
        conv_grad_kernel,
        in_specs=[pl.BlockSpec(memory_space=pltpu.SMEM), VMEM, HBM, HBM, VMEM, VMEM],
        out_specs=[HBM] * 2,
        out_shape=[half, half],
        scratch_shapes=[
            pltpu.VMEM((rows + 2, cols + 2, samples, depth), jnp.float32),
            buffer,
            buffer,
            pltpu.VMEM((9 * depth, channels), jnp.bfloat16),
            pltpu.SemaphoreType.DMA((2,)),
            pltpu.SemaphoreType.DMA((2,)),
        ],
        compiler_params=vmem(32),
        name="conv_grad",
    )(core[None], maps, in_hbm(grad_bn), in_hbm(normed), mask[:, None], factors)


def silu_slope(values):
    sigma = jax.nn.sigmoid(values)
    return sigma * (1.0 + values * (1.0 - sigma))


def norm_kernel(parts_ref, conv_ref, affine_ref, *refs):
    normed_ref, pooled_ref, factor_ref, count_ref, normed, arrived = refs[-6:]
    grid, _, samples, channels = normed_ref.shape
    cells = (grid - 1) // 2
    sums = jnp.sum(parts_ref[...], axis=0)
    pixels = jnp.sum(sums[:, 2 * channels : 2 * channels + samples]) * (grid * grid)
    center = sums[:, :channels] / pixels
    inv_std = lax.rsqrt(sums[:, channels : 2 * channels] / pixels - center * center + EPSILON)
    gain, shift = affine_ref[0:1, :], affine_ref[1:2, :]
    factor_ref[0:1, :] = inv_std
    factor_ref[1:2, :] = gain
    factor_ref[2:3, :] = shift
    count_ref[...] = jnp.full(count_ref.shape, pixels)
    normed[...] = ((conv_ref[...] - center) * inv_std).reshape(normed.shape)
    copy = pltpu.make_async_copy(normed, normed_ref, arrived.at[0])
    copy.start()
    act = jax.nn.silu(normed[...] * gain + shift)
    for row in range(cells):
        line = act[2 * row] + act[2 * row + 1] + act[2 * row + 2]
        for col in range(cells):
            window = line[2 * col] + line[2 * col + 1] + line[2 * col + 2]
            pooled_ref[row * cells + col] = (window / 9.0).astype(jnp.bfloat16)
    copy.wait()


def norm_and_pool(parts, conv_out, affine, grid, samples, *others):
    channels = conv_out.shape[1]
    cells = ((grid - 1) // 2) ** 2
    shape = (grid, grid, samples, channels)
    return pl.pallas_call(
        norm_kernel,
        in_specs=[VMEM] * 3 + [pl.BlockSpec(memory_space=pl.ANY)] * len(others),
        out_specs=[HBM] + [VMEM] * 3,
        out_shape=[
            pltpu.HBM(shape, jnp.float32),
            jax.ShapeDtypeStruct((cells, samples, channels), jnp.bfloat16),
            jax.ShapeDtypeStruct((3, channels), jnp.float32),
            jax.ShapeDtypeStruct((1, 128), jnp.float32),
        ],
        scratch_shapes=[pltpu.VMEM(shape, jnp.float32), pltpu.SemaphoreType.DMA((1,))],
        compiler_params=vmem(24),
        name="norm_and_pool",
    )(parts, conv_out, affine, *others)


def norm_back_kernel(pooled_ref, normed_ref, factor_ref, *refs):
    grad_ref, sum_ref, normed_buffer, grad_buffer, arrived, left = refs[-6:]
    grid, _, samples, channels = normed_ref.shape
    cells = (grid - 1) // 2
    gain, shift = factor_ref[1:2, :], factor_ref[2:3, :]
    fetch = Fetch([(normed_ref.at[row], normed_buffer.at[row]) for row in range(grid)], arrived, grid)

    def windows(pixel):
        return [cell for cell in range(cells) if 2 * cell <= pixel <= 2 * cell + 2]

    with_normed = jnp.zeros((samples, channels), jnp.float32)
    alone = jnp.zeros((samples, channels), jnp.float32)
    copies = []
    for row in range(grid):
        line = [
            sum(pooled_ref[cell * cells + col].astype(jnp.float32) for cell in windows(row)) / 9.0
            for col in range(cells)
        ]
        fetch.wait()
        for col in range(grid):
            act = sum(line[cell] for cell in windows(col))
            normed = normed_buffer[row, col]
            grad = act * silu_slope(normed * gain + shift)
            grad_buffer[row, col] = grad
            with_normed += grad * normed
            alone += grad
        copy = pltpu.make_async_copy(grad_buffer.at[row], grad_ref.at[row], left.at[row])
        copy.start()
        copies.append(copy)
    sum_ref[0:1, :] = jnp.sum(with_normed, axis=0, keepdims=True)
    sum_ref[1:2, :] = jnp.sum(alone, axis=0, keepdims=True)
    for copy in copies:
        copy.wait()


def norm_backward(grad_pooled, normed, factors, *others):
    buffer = pltpu.VMEM(normed.shape, jnp.float32)
    arrivals = pltpu.SemaphoreType.DMA((normed.shape[0],))
    return pl.pallas_call(
        norm_back_kernel,
        in_specs=[VMEM, HBM, VMEM] + [pl.BlockSpec(memory_space=pl.ANY)] * len(others),
        out_specs=[HBM, VMEM],
        out_shape=[
            pltpu.HBM(normed.shape, jnp.float32),
            jax.ShapeDtypeStruct((2, normed.shape[3]), jnp.float32),
        ],
        scratch_shapes=[buffer, buffer, arrivals, arrivals],
        compiler_params=vmem(24),
        name="norm_backward",
    )(grad_pooled, in_hbm(normed), factors, *others)


def conv_kernel(maps_ref, weight_ref, mask_ref, out_ref, sum_ref, padded_ref, patch_ref):
    rows, cols, samples, depth = maps_ref.shape
    pad_into(maps_ref, padded_ref)
    for shift in range(9):
        down, right = shift // 3, shift % 3
        shifted = padded_ref[down : down + rows, right : right + cols]
        patch_ref[:, shift * depth : (shift + 1) * depth] = shifted.reshape(-1, depth).astype(
            jnp.bfloat16
        )
    out = jnp.dot(
        patch_ref[...],
        weight_ref[...].astype(jnp.bfloat16),
        preferred_element_type=jnp.float32,
    )
    out_ref[...] = out
    mask = mask_ref[...]
    by_sample = out.reshape(rows * cols, samples, out.shape[1])
    sum_ref[0:1, :] = jnp.sum(jnp.sum(by_sample, axis=0) * mask, axis=0, keepdims=True)
    sum_ref[1:2, :] = jnp.sum(
        jnp.sum(by_sample * by_sample, axis=0) * mask, axis=0, keepdims=True
    )


def conv_of(maps, weight, mask):
    rows, cols, samples, depth = maps.shape
    channels = weight.shape[1]
    pixels = rows * cols * samples
    return pl.pallas_call(
        conv_kernel,
        out_shape=[
            jax.ShapeDtypeStruct((pixels, channels), jnp.float32),
            jax.ShapeDtypeStruct((2, channels), jnp.float32),
        ],
        scratch_shapes=[
            pltpu.VMEM((rows + 2, cols + 2, samples, depth), jnp.float32),
            pltpu.VMEM((pixels, 9 * depth), jnp.bfloat16),
        ],
        compiler_params=vmem(32),
        name="conv",
    )(maps, weight, mask[:, None])


def sum_kernel(blocks_ref, *refs):
    refs[-1][...] = jnp.sum(blocks_ref[...].astype(jnp.float32), axis=0).astype(jnp.bfloat16)


def sum_blocks(blocks, *others):
    return pl.pallas_call(
        sum_kernel,
        in_specs=[pl.BlockSpec(memory_space=pltpu.VMEM)]
        + [pl.BlockSpec(memory_space=pl.ANY)] * len(others),
        out_shape=jax.ShapeDtypeStruct(blocks.shape[1:], jnp.bfloat16),
        compiler_params=vmem(24),
        name="sum_blocks",
    )(blocks, *others)


def conv_update_kernel(
    decay, core_ref, own_ref, other_ref, weight_ref, row_ref, col_ref, *refs
):
    grad_ref, new_ref, row_new_ref, col_new_ref = refs[-4:]
    rows, channels = weight_ref.shape
    half = rows // 2
    first = core_ref[0] == 0
    own = own_ref[...].astype(jnp.float32)
    other = other_ref[...].astype(jnp.float32)
    grad_ref[:half] = jnp.where(first, own, other)
    grad_ref[half:] = jnp.where(first, other, own)
    grad = grad_ref[...]
    weight = weight_ref[...]
    squared = grad * grad
    row_square = jnp.broadcast_to(jnp.sum(squared, axis=1, keepdims=True), (rows, 128)).T[:1]
    row_new = decay * row_ref[...].reshape(1, rows) + (1.0 - decay) * (
        row_square / channels + TINY
    )
    col_new = decay * col_ref[...].reshape(1, channels) + (1.0 - decay) * (
        jnp.sum(squared, axis=0, keepdims=True) / rows + TINY
    )
    row_new_ref[...] = row_new.reshape(row_new_ref.shape)
    col_new_ref[...] = col_new.reshape(col_new_ref.shape)
    mean_square = jnp.sum(jnp.sum(weight * weight, axis=0, keepdims=True)) / (rows * channels)
    row_mean = jnp.sum(row_new) / rows
    scale = RATE * jnp.maximum(FLOOR, jnp.sqrt(mean_square))
    by_row = jnp.broadcast_to(scale * lax.rsqrt(row_new / row_mean), (128, rows)).T
    by_col = lax.rsqrt(col_new)
    for first, last in spans(channels, 128):
        new_ref[:, first:last] = weight[:, first:last] - (
            by_row * grad[:, first:last]
        ) * by_col[:, first:last]


def conv_update(core, own, other, weight, row_state, col_state, decay, *others):
    rows, channels = weight.shape
    whole = pl.BlockSpec(memory_space=pltpu.VMEM)
    out = jax.ShapeDtypeStruct(weight.shape, jnp.float32)
    grad, new, row_new, col_new = pl.pallas_call(
        functools.partial(conv_update_kernel, decay),
        in_specs=[pl.BlockSpec(memory_space=pltpu.SMEM)]
        + [whole] * 5
        + [pl.BlockSpec(memory_space=pl.ANY)] * len(others),
        out_specs=[whole] * 4,
        out_shape=[
            out,
            out,
            jax.ShapeDtypeStruct((rows,), jnp.float32),
            jax.ShapeDtypeStruct((channels,), jnp.float32),
        ],
        compiler_params=vmem(40),
        name="conv_update",
    )(core[None], own, other, weight, row_state, col_state, *others)
    return grad, new, row_new, col_new


def contract_rows(left, right):
    return lax.dot_general(
        left, right, (((0,), (0,)), ((), ())), preferred_element_type=jnp.float32
    )


def exchange(blocks, axis, groups=None):
    return lax.all_to_all(blocks, axis, 0, 0, tiled=True, axis_index_groups=groups)


def gather(values, axis, size, groups=None):
    return exchange(jnp.broadcast_to(values[None], (size,) + values.shape), axis, groups)


class Ring:
    def __init__(self, axis, size, inner):
        self.axis, self.size, self.inner = axis, size, inner
        self.length = lax.axis_size(axis)
        self.own = lax.axis_index(axis) // inner % size

    def other(self, index, shift):
        own = index // self.inner % self.size
        return index + ((own + shift) % self.size - own) * self.inner

    def fetch(self, values, shift):
        pairs = [(self.other(index, shift), index) for index in range(self.length)]
        return lax.ppermute(values, self.axis, pairs)

    def stack(self, parts):
        if self.size == 2:
            first = self.own == 0
            parts = [jnp.where(first, parts[0], parts[1]), jnp.where(first, parts[1], parts[0])]
            return jnp.stack(parts)
        return jnp.roll(jnp.stack(parts), self.own, axis=0)

    def gather(self, values):
        return self.stack([values] + [self.fetch(values, k) for k in range(1, self.size)])

    def scatter_sum(self, blocks, dim):
        def block(shift):
            return lax.dynamic_index_in_dim(
                blocks, (self.own + shift) % self.size, dim, keepdims=False
            )

        result = block(0).astype(jnp.float32)
        for shift in range(1, self.size):
            result += self.fetch(block(-shift), shift).astype(jnp.float32)
        return result


def double_sums(values, axis):
    size = lax.axis_size(axis)
    inner, steps = 1, []
    while inner < size:
        pairs = [(index, index ^ inner) for index in range(size)]
        values = values + lax.ppermute(values, axis, pairs)
        steps.append(values)
        inner *= 2
    return steps


def vector_step(gradient, values, state, decay, seg_widths):
    state_new = decay * state + (1.0 - decay) * (gradient * gradient + TINY)
    scales = []
    offset = 0
    for seg_width in seg_widths:
        segment = values[offset : offset + seg_width]
        scales.append(
            jnp.full((seg_width,), 1.0, jnp.float32)
            * (RATE * jnp.maximum(FLOOR, jnp.sqrt(jnp.mean(segment * segment))))
        )
        offset += seg_width
    return (state_new, values - jnp.concatenate(scales) * gradient * lax.rsqrt(state_new))


def gram(values):
    return lax.dot_general(
        values, values, (((1,), (1,)), ((), ())), preferred_element_type=jnp.float32
    )


def square_sums(gram_matrix, values):
    values = values.astype(jnp.float32)
    return jnp.sum(values * jnp.dot(gram_matrix, values, precision=HIGHEST), axis=0)


def factor_scales(
    left, right, left_gram, right_gram, row_state, col_state, sums, rows, decay
):
    cols = right.shape[1]
    row_new = decay * row_state + (1.0 - decay) * (square_sums(right_gram, left) / cols + TINY)
    col_new = decay * col_state + (1.0 - decay) * (square_sums(left_gram, right) / rows + TINY)
    mean_square = jnp.sum(left_gram * right_gram) / (rows * cols)
    row_mean = decay * sums[0] / rows + (1.0 - decay) * (mean_square + TINY)
    scale = RATE * jnp.maximum(FLOOR, jnp.sqrt(sums[1] / (rows * cols)))
    return row_new, col_new, scale * lax.rsqrt(row_new / row_mean), lax.rsqrt(col_new)


def plain_update(left, right, weight, row_scale, col_scale):
    grad = contract_rows(left, right)
    return grad, weight - (row_scale[:, None] * grad) * col_scale[None, :]


def per_device(
    stem_maps,
    validity,
    labels,
    conv_weight,
    fc6_weight,
    head_weight,
    vectors,
    pca_matrix,
    conv_row_state,
    conv_col_state,
    fc6_row_state,
    fc6_col_state,
    head_row_state,
    head_col_state,
    vector_state,
):
    bf16, f32 = jnp.bfloat16, jnp.float32
    samples, grid = stem_maps.shape[0], stem_maps.shape[1]
    pixels = grid * grid
    channels = conv_weight.shape[1]
    fc_rows, hidden = fc6_weight.shape
    head_rows, classes = head_weight.shape
    wide_count = lax.axis_size("wide")
    grp_count = lax.axis_size("grp")
    count = wide_count * grp_count
    group = samples * wide_count
    my_wide = lax.axis_index("wide")
    decay = 1.0 - STEP ** (-0.8)
    mask = validity.astype(f32)

    core = Ring("grp", 2, 1)
    planes = Ring("grp", grp_count // 2, 2)
    near = Ring("wide", wide_count // 4, 1)
    far = Ring("wide", 4, wide_count // 4)

    bn_gain = vectors[:channels]
    bn_shift = vectors[channels : 2 * channels]
    bias_hidden = vectors[2 * channels : 2 * channels + hidden]
    bias_head = vectors[2 * channels + hidden :]

    maps = stem_maps.transpose(1, 2, 0, 3)
    conv_out, conv_sums = conv_of(maps, conv_weight, mask)
    packed = jnp.concatenate([conv_sums.reshape(-1), mask, labels.astype(f32)])
    everyone = gather(packed[None], ALL, count)
    fc6_left, left_squares = low_and_squares(fc6_weight, 0, hidden // 2, packed)
    normed, pooled, factors, pixel_total = norm_and_pool(
        everyone, conv_out, jnp.stack([bn_gain, bn_shift]), grid, samples, left_squares
    )
    everyone = everyone[:, 0]
    mask_all = everyone[:, 2 * channels : 2 * channels + samples].reshape(-1)
    labels_all = everyone[:, 2 * channels + samples :].reshape(-1)
    valid_count = jnp.sum(mask_all)
    pooled_low = pooled.transpose(1, 0, 2).reshape(samples, -1)

    pooled_blocks = pooled_low.reshape(samples, wide_count, fc_rows).transpose(1, 0, 2)
    pooled_rows = exchange(pooled_blocks, "wide").reshape(group, fc_rows)
    fc6_right, right_squares = low_and_squares(
        fc6_weight, hidden // 2, hidden // 2, pooled_blocks
    )
    pre_part = fc6_forward(pooled_rows, fc6_left, fc6_right)
    pre_blocks = exchange(
        pre_part.reshape(group, wide_count, head_rows).transpose(1, 0, 2), "wide"
    )
    head_low, head_squares = low_and_squares(head_weight.T, 0, head_rows, pre_part)
    pre_hidden = jnp.sum(pre_blocks.astype(f32), axis=0)
    pre_hidden += lax.dynamic_slice_in_dim(bias_hidden, my_wide * head_rows, head_rows)
    feats = jax.nn.silu(pre_hidden).astype(bf16)

    logit_part = head_forward(feats, head_low)
    logit_blocks = exchange(logit_part.reshape(wide_count, samples, classes), "wide")

    pooled_all = lax.all_gather(pooled_rows, "grp", axis=0, tiled=True)
    feats_all = lax.all_gather(feats, "grp", axis=0, tiled=True)
    pooled_columns = transposed(pooled_all)
    pooled_gram, feats_gram = gram(pooled_all), gram(feats_all)
    numbers = jnp.stack(
        [
            jnp.sum(fc6_row_state),
            jnp.sum(left_squares + right_squares),
            jnp.sum(head_row_state),
            jnp.sum(head_squares),
        ]
    )
    all_samples = pooled_all.shape[0]
    per_share = 2 * all_samples // grp_count
    numbers = jnp.pad(numbers, (0, all_samples - numbers.size))
    both_part = jnp.concatenate([pooled_gram, feats_gram])
    both_part = lax.dynamic_slice_in_dim(
        both_part, lax.axis_index("grp") * per_share, per_share
    )
    both_part = jnp.concatenate([both_part, numbers[None]])
    both_steps = double_sums(both_part, "wide")
    both = lax.all_gather(both_steps[-1], "grp")
    sums = both[0, per_share, :8]
    both = both[:, :per_share].reshape(-1, all_samples)
    kept_all = feats_all.astype(f32) * mask_all[:, None]
    feat_center = jnp.sum(kept_all, axis=0) / valid_count
    feat_square = jnp.sum(kept_all * kept_all, axis=0) / valid_count
    feat_scale = lax.rsqrt(feat_square - feat_center * feat_center + EPSILON)
    group_mask = lax.dynamic_slice_in_dim(mask_all, lax.axis_index("grp") * group, group)
    kept = feats.astype(f32) * group_mask[:, None]
    standard = ((kept - feat_center) * feat_scale).astype(bf16)
    projected = jnp.dot(standard, pca_matrix.astype(bf16), preferred_element_type=f32)
    projected = projected.astype(bf16)
    logits = jnp.sum(logit_blocks.astype(f32), axis=0) + bias_head

    same = labels.astype(f32)[:, None] == labels_all[None, :]
    label_count = jnp.sum(jnp.where(same, mask_all[None, :], 0.0), axis=1)
    sample_weight = mask / jnp.maximum(label_count, 1.0)
    sample_weight = follow(sample_weight, both_steps[0], projected, pooled_columns)
    label_hits = labels[:, None] == jnp.arange(classes)[None, :]
    top_logit = jnp.max(logits, axis=1, keepdims=True)
    expo = jnp.exp(logits - top_logit)
    totals = jnp.sum(expo, axis=1, keepdims=True)
    log_total = top_logit[:, 0] + jnp.log(totals[:, 0])
    label_logit = jnp.sum(jnp.where(label_hits, logits, 0.0), axis=1)
    loss_part = jnp.sum(sample_weight * (log_total - label_logit))
    weight_part = jnp.sum(sample_weight)
    grad_logits = (
        sample_weight[:, None] * (expo / totals - label_hits.astype(f32))
    ).astype(bf16)

    logits_group = gather(grad_logits, "wide", wide_count).reshape(group, classes)
    grad_pre = head_backward(logits_group, head_low, pre_hidden)
    rows = samples * projected.shape[1] // head_rows
    pre_blocks = exchange(
        jnp.concatenate(
            [
                jnp.broadcast_to(grad_pre, (wide_count,) + grad_pre.shape),
                projected.reshape(wide_count, rows, head_rows),
            ],
            axis=1,
        ),
        "wide",
    )
    projected = pre_blocks[:, group:].reshape(wide_count, samples, -1)
    pre_blocks = pre_blocks[:, :group]
    pre_group = pre_blocks.transpose(1, 0, 2).reshape(group, hidden)
    grad_pooled_rows = fc6_backward(pre_group, fc6_left, fc6_right)
    feats_gram, pooled_gram = both[all_samples:], both[:all_samples]
    by_kernels = grp_count == 4 and all_samples <= 512
    fc6_rows_total = fc_rows * wide_count
    if by_kernels:
        parts = [pre_group, planes.fetch(pre_group, 1)]
        parts += [core.fetch(part, 1) for part in parts]
        my_grp = lax.axis_index("grp")
        places = jnp.stack([my_grp, my_grp ^ 2, my_grp ^ 1, my_grp ^ 3])
        pre_all, fc6_row_new, fc6_col_new, fc6_by_row, fc6_by_col, grad_bias_hidden = fc6_stats(
            pooled_all,
            parts,
            places,
            pooled_gram,
            fc6_row_state,
            fc6_col_state,
            sums,
            fc6_rows_total,
            decay,
        )
    else:
        pre_all = lax.all_gather(pre_group, "grp", axis=0, tiled=True)
        fc6_row_new, fc6_col_new, fc6_by_row, fc6_by_col = factor_scales(
            pooled_all,
            pre_all,
            pooled_gram,
            gram(pre_all),
            fc6_row_state,
            fc6_col_state,
            sums[:2],
            fc6_rows_total,
            decay,
        )
        grad_bias_hidden = jnp.sum(pre_all.astype(f32), axis=0)
    logits_all = lax.all_gather(logits_group, "grp", axis=0, tiled=True)
    grad_pooled = exchange(grad_pooled_rows.reshape(wide_count, samples, fc_rows), "wide")
    grad_pooled = grad_pooled.transpose(1, 0, 2).reshape(samples, -1, channels)
    grad_bn, bn_sums = norm_backward(
        grad_pooled.transpose(1, 0, 2), normed, factors, both
    )
    bn_sums = jnp.concatenate([bn_sums.reshape(-1), jnp.stack([loss_part, weight_part])])
    bn_sums, conv_factors = norm_sums(
        gather(bn_sums[None], ALL, count), factors, pixel_total, fc6_by_col
    )
    bn_sums = bn_sums[0]
    grad_gain, grad_shift = bn_sums[:channels], bn_sums[channels : 2 * channels]
    conv_send, conv_keep = conv_grad_of(core.own, maps, grad_bn, normed, mask, conv_factors)
    chips = count // 2
    same_core = [
        [grp * wide_count + wide for grp in range(first, grp_count, 2) for wide in range(wide_count)]
        for first in range(2)
    ]
    conv_half = (conv_keep.astype(f32) + core.fetch(conv_send, 1).astype(f32)).astype(bf16)
    conv_blocks = exchange(conv_half.reshape(chips, -1, channels), ALL, same_core)

    if by_kernels:
        fc6_grad, fc6_new, mark = row_update(
            pooled_columns, pre_all, fc6_weight, fc6_by_row, fc6_by_col, conv_half
        )
        conv_share = sum_blocks(conv_blocks, mark)
        head_row_new, head_by_row, grad_bias_head = head_stats(
            feats_all,
            logits_all,
            feats_gram,
            head_row_state,
            sums,
            hidden,
            decay,
        )
        update_head = functools.partial(
            col_update,
            left=logits_all,
            right=feats_all,
            weight=head_weight.T,
            right_gram=feats_gram,
            col_state=head_col_state,
            row_scale=head_by_row,
            rows=hidden,
            decay=decay,
        )
        blocks = pl.cdiv(classes, 2048)
        begun = update_head((0, blocks // 2 + 1), (), start=conv_share)
        conv_own = gather(conv_share, ALL, chips, same_core).reshape(-1, channels)
        conv_own = follow(conv_own, begun[2])
        head_grad, head_new, head_col_new = update_head(
            (blocks // 2 + 1, blocks), begun, start=conv_own
        )
        head_grad, head_new = head_grad.T, head_new.T
    else:
        fc6_grad, fc6_new = plain_update(pooled_all, pre_all, fc6_weight, fc6_by_row, fc6_by_col)
        head_row_new, head_col_new, head_by_row, head_by_col = factor_scales(
            feats_all,
            logits_all,
            feats_gram,
            gram(logits_all),
            head_row_state,
            head_col_state,
            sums[2:],
            hidden,
            decay,
        )
        head_grad, head_new = plain_update(
            feats_all, logits_all, head_weight, head_by_row, head_by_col
        )
        grad_bias_head = jnp.sum(logits_all.astype(f32), axis=0)
        conv_share = sum_blocks(conv_blocks)
        conv_own = gather(conv_share, ALL, chips, same_core).reshape(-1, channels)
    conv_grad, conv_new, conv_row_new, conv_col_new = conv_update(
        core.own,
        conv_own,
        core.fetch(conv_own, 1),
        conv_weight,
        conv_row_state,
        conv_col_state,
        decay,
    )
    vector_grad = jnp.concatenate([grad_gain, grad_shift, grad_bias_hidden, grad_bias_head])
    vector_state_new, vector_new = vector_step(
        vector_grad, vectors, vector_state, decay, (channels, channels, hidden, classes)
    )

    projected = jnp.sum(projected.astype(f32), axis=0)
    embedded = projected * lax.rsqrt(
        jnp.sum(projected * projected, axis=1, keepdims=True) + NORM_EPS
    )
    return (
        bn_sums[2 * channels],
        bn_sums[2 * channels + 1],
        embedded,
        conv_grad,
        conv_row_new,
        conv_col_new,
        conv_new,
        fc6_grad,
        fc6_row_new,
        fc6_col_new,
        fc6_new,
        head_grad,
        head_row_new,
        head_col_new,
        head_new,
        vector_grad,
        vector_state_new,
        vector_new,
    )


def solution(mesh):
    in_specs = (
        P(("grp", "wide"), None, None, None),
        P(("grp", "wide")),
        P(("grp", "wide")),
        P(),
        P("wide", None),
        P("wide", None),
        P(),
        P("wide", None),
        P(),
        P(),
        P("wide"),
        P(),
        P("wide"),
        P(),
        P(),
    )
    out_specs = (
        P(),
        P(),
        P(("grp", "wide"), None),
        P(),
        P(),
        P(),
        P(),
        P("wide", None),
        P("wide"),
        P(),
        P("wide", None),
        P("wide", None),
        P("wide"),
        P(),
        P("wide", None),
        P(),
        P(),
        P(),
    )
    return jax.shard_map(
        per_device, mesh=mesh, in_specs=in_specs, out_specs=out_specs, check_vma=False
    )
```

```python
import functools
import math

import jax
import jax.numpy as jnp
from jax import lax
from jax.experimental import pallas as pl
from jax.experimental.pallas import tpu as pltpu
from jax.sharding import PartitionSpec as P

STEP = 10


EPSILON = 1e-05
TINY = 1e-30
RATE = 0.5
FLOOR = 0.001
NORM_EPS = 1e-06
HIGHEST = lax.Precision.HIGHEST
ALL = ("grp", "wide")


def block_of(rows, row_bytes, limit):
    sizes = [n for n in range(16, rows + 1, 16) if rows % n == 0 and n * row_bytes <= limit]
    return max(sizes) if sizes else rows


def vmem(megabytes):
    return pltpu.CompilerParams(vmem_limit_bytes=megabytes << 20)


def follow_kernel(*refs):
    refs[-1][...] = refs[0][...]


def follow(values, *others):
    return pl.pallas_call(
        follow_kernel,
        in_specs=[pl.BlockSpec(memory_space=pltpu.VMEM)]
        + [pl.BlockSpec(memory_space=pl.ANY)] * len(others),
        out_specs=pl.BlockSpec(memory_space=pltpu.VMEM),
        out_shape=jax.ShapeDtypeStruct(values.shape, values.dtype),
        name="follow",
    )(values, *others)


def carry_kernel(values_ref, *refs):
    out_ref, arrived = refs[-2:]
    copy = pltpu.make_async_copy(values_ref, out_ref, arrived.at[0])
    copy.start()
    copy.wait()


def carry(values, *others):
    return pl.pallas_call(
        carry_kernel,
        in_specs=[VMEM] + [pl.BlockSpec(memory_space=pl.ANY)] * len(others),
        out_specs=HBM,
        out_shape=pltpu.HBM(values.shape, values.dtype),
        scratch_shapes=[pltpu.SemaphoreType.DMA((1,))],
        compiler_params=vmem(24),
        name="carry",
    )(values, *others)


def low_kernel(weight_ref, _, low_ref, square_ref):
    @pl.when(pl.program_id(0) == 0)
    def _():
        square_ref[...] = jnp.zeros_like(square_ref)

    weight = weight_ref[...]
    low_ref[...] = weight.astype(jnp.bfloat16)
    square_ref[...] += jnp.sum((weight * weight).reshape(-1, 8, weight.shape[1]), axis=0)


def in_hbm(array):
    return pltpu.with_memory_space_constraint(array, pltpu.HBM)


HBM = pl.BlockSpec(memory_space=pltpu.HBM)
VMEM = pl.BlockSpec(memory_space=pltpu.VMEM)


def spans(length, step):
    return [(first, min(first + step, length)) for first in range(0, length, step)]


class Fetch:
    def __init__(self, pairs, arrived, depth):
        self.copies = [
            pltpu.make_async_copy(source, target, arrived.at[number])
            for number, (source, target) in enumerate(pairs)
        ]
        self.depth, self.done = depth, 0
        for copy in self.copies[:depth]:
            copy.start()

    def wait(self):
        self.copies[self.done].wait()
        for copy in self.copies[self.done + self.depth : self.done + self.depth + 1]:
            copy.start()
        self.done += 1


def low_and_squares(weight, first, cols, start):
    rows = weight.shape[0]
    block = block_of(rows, 4 * cols, 4 << 20)
    low, squares = pl.pallas_call(
        low_kernel,
        grid=(rows // block,),
        in_specs=[
            pl.BlockSpec((block, cols), lambda i: (i, first // cols)),
            pl.BlockSpec(memory_space=pl.ANY),
        ],
        out_specs=[
            pl.BlockSpec((block, cols), lambda i: (i, 0)),
            pl.BlockSpec((8, cols), lambda i: (0, 0)),
        ],
        out_shape=[
            pltpu.HBM((rows, cols), jnp.bfloat16),
            jax.ShapeDtypeStruct((8, cols), jnp.float32),
        ],
        compiler_params=vmem(24),
        name="low_and_squares",
    )(in_hbm(weight), start)
    return low, squares


def fc6_kernel(rows_ref, left_ref, right_ref, out_ref, buffer, arrived):
    half = left_ref.shape[1]
    blocks = [
        (ref, first, last, side * half)
        for side, ref in enumerate((left_ref, right_ref))
        for first, last in spans(half, 512)
    ]
    fetch = Fetch(
        [
            (ref.at[:, first:last], buffer.at[:, base + first : base + last])
            for ref, first, last, base in blocks
        ],
        arrived,
        4,
    )
    for _, first, last, base in blocks:
        fetch.wait()
        out_ref[:, base + first : base + last] = jnp.dot(
            rows_ref[...],
            buffer[:, base + first : base + last],
            preferred_element_type=jnp.float32,
        ).astype(out_ref.dtype)


def fc6_forward(values, left, right):
    depth, half = left.shape
    blocks = 2 * len(spans(half, 512))
    return pl.pallas_call(
        fc6_kernel,
        in_specs=[VMEM, HBM, HBM],
        out_specs=VMEM,
        out_shape=jax.ShapeDtypeStruct((values.shape[0], 2 * half), jnp.bfloat16),
        scratch_shapes=[
            pltpu.VMEM((depth, 2 * half), left.dtype),
            pltpu.SemaphoreType.DMA((blocks,)),
        ],
        compiler_params=vmem(32),
        name="fc6_forward",
    )(values, in_hbm(left), in_hbm(right))


def fc6_back_kernel(grad_ref, left_ref, right_ref, *refs):
    out_ref, buffer, arrived = refs[-3:]
    rows, half = left_ref.shape
    blocks = spans(rows, 512)
    fetch = Fetch(
        [
            (ref.at[first:last], buffer.at[side, first:last])
            for first, last in blocks
            for side, ref in enumerate((left_ref, right_ref))
        ],
        arrived,
        4,
    )
    for first, last in blocks:
        part = 0.0
        for side in range(2):
            fetch.wait()
            part += lax.dot_general(
                grad_ref[:, side * half : (side + 1) * half],
                buffer[side, first:last],
                (((1,), (1,)), ((), ())),
                preferred_element_type=jnp.float32,
            )
        out_ref[:, first:last] = part.astype(out_ref.dtype)


def fc6_backward(grad, left, right, *others):
    rows, half = left.shape
    return pl.pallas_call(
        fc6_back_kernel,
        in_specs=[VMEM, HBM, HBM] + [pl.BlockSpec(memory_space=pl.ANY)] * len(others),
        out_specs=VMEM,
        out_shape=jax.ShapeDtypeStruct((grad.shape[0], rows), jnp.bfloat16),
        scratch_shapes=[
            pltpu.VMEM((2, rows, half), left.dtype),
            pltpu.SemaphoreType.DMA((2 * len(spans(rows, 512)),)),
        ],
        compiler_params=vmem(32),
        name="fc6_backward",
    )(grad, in_hbm(left), in_hbm(right), *others)


def head_kernel(feats_ref, weight_ref, out_ref, buffer, arrived):
    blocks = spans(weight_ref.shape[0], 1024)
    fetch = Fetch(
        [(weight_ref.at[first:last], buffer.at[first:last]) for first, last in blocks], arrived, 4
    )
    for first, last in blocks:
        fetch.wait()
        out_ref[:, first:last] = lax.dot_general(
            feats_ref[...],
            buffer[first:last],
            (((1,), (1,)), ((), ())),
            preferred_element_type=jnp.float32,
        ).astype(out_ref.dtype)


def head_forward(feats, weight):
    classes = weight.shape[0]
    return pl.pallas_call(
        head_kernel,
        in_specs=[VMEM, HBM],
        out_specs=VMEM,
        out_shape=jax.ShapeDtypeStruct((feats.shape[0], classes), jnp.bfloat16),
        scratch_shapes=[
            pltpu.VMEM(weight.shape, weight.dtype),
            pltpu.SemaphoreType.DMA((len(spans(classes, 1024)),)),
        ],
        compiler_params=vmem(32),
        name="head_forward",
    )(feats, in_hbm(weight))


def head_back_kernel(grad_ref, weight_ref, pre_ref, *refs):
    out_ref, grad_buffer, buffer, arrived = refs[-4:]
    blocks = spans(weight_ref.shape[0], 1024)
    fetch = Fetch(
        [(grad_ref, grad_buffer)]
        + [(weight_ref.at[first:last], buffer.at[first:last]) for first, last in blocks],
        arrived,
        5,
    )
    fetch.wait()
    total = 0.0
    for first, last in blocks:
        fetch.wait()
        total += jnp.dot(
            grad_buffer[:, first:last], buffer[first:last], preferred_element_type=jnp.float32
        )
    out_ref[...] = (total * silu_slope(pre_ref[...])).astype(out_ref.dtype)


def head_backward(grad, weight, pre_hidden, *others):
    return pl.pallas_call(
        head_back_kernel,
        in_specs=[HBM, HBM, VMEM] + [pl.BlockSpec(memory_space=pl.ANY)] * len(others),
        out_specs=VMEM,
        out_shape=jax.ShapeDtypeStruct(pre_hidden.shape, jnp.bfloat16),
        scratch_shapes=[
            pltpu.VMEM(grad.shape, grad.dtype),
            pltpu.VMEM(weight.shape, weight.dtype),
            pltpu.SemaphoreType.DMA((1 + len(spans(weight.shape[0], 1024)),)),
        ],
        compiler_params=vmem(32),
        name="head_backward",
    )(in_hbm(grad), in_hbm(weight), pre_hidden, *others)


def pieces(matrix):
    first = matrix.astype(jnp.bfloat16)
    rest = matrix - first.astype(jnp.float32)
    second = rest.astype(jnp.bfloat16)
    third = (rest - second.astype(jnp.float32)).astype(jnp.bfloat16)
    return first, second, third


def quadratic(matrix, values):
    product = sum(
        jnp.dot(piece, values, preferred_element_type=jnp.float32) for piece in pieces(matrix)
    )
    return jnp.sum(product * values.astype(jnp.float32), axis=0, keepdims=True)


def step_size(squares, count):
    return RATE * jnp.maximum(FLOOR, jnp.sqrt(squares / count))


def head_stats_kernel(
    decay,
    rows,
    sum_ref,
    left_ref,
    right_ref,
    gram_ref,
    state_ref,
    new_ref,
    scale_ref,
    total_ref,
    buffer,
    arrived,
):
    cols = right_ref.shape[1]
    blocks = spans(cols, 2048)
    fetch = Fetch(
        [(right_ref.at[:, first:last], buffer.at[:, first:last]) for first, last in blocks],
        arrived,
        len(blocks),
    )
    right_gram, totals = 0.0, []
    for first, last in blocks:
        fetch.wait()
        right = buffer[:, first:last]
        right_gram += lax.dot_general(
            right, right, (((1,), (1,)), ((), ())), preferred_element_type=jnp.float32
        )
        totals.append(jnp.sum(right.astype(jnp.float32), axis=0, keepdims=True))
    total_ref[...] = jnp.concatenate(totals, axis=1).reshape(cols)
    mean_square = jnp.sum(gram_ref[...] * right_gram) / (rows * cols)
    width = left_ref.shape[1]
    row_new = decay * state_ref[...].reshape(1, width) + (1.0 - decay) * (
        quadratic(right_gram, left_ref[...]) / cols + TINY
    )
    row_mean = decay * sum_ref[2] / rows + (1.0 - decay) * (mean_square + TINY)
    new_ref[...] = row_new.reshape(width)
    step = step_size(jnp.full(row_new.shape, sum_ref[3]), rows * cols)
    scale_ref[...] = step * lax.rsqrt(row_new / row_mean)


def head_stats(left, right, left_gram, row_state, sums, rows, decay):
    width, cols = left.shape[1], right.shape[1]
    smem = pl.BlockSpec(memory_space=pltpu.SMEM)
    return pl.pallas_call(
        functools.partial(head_stats_kernel, decay, rows),
        in_specs=[smem, VMEM, HBM, VMEM, VMEM],
        out_specs=[VMEM] * 3,
        out_shape=[
            jax.ShapeDtypeStruct((width,), jnp.float32),
            jax.ShapeDtypeStruct((1, width), jnp.float32),
            jax.ShapeDtypeStruct((cols,), jnp.float32),
        ],
        scratch_shapes=[
            pltpu.VMEM(right.shape, right.dtype),
            pltpu.SemaphoreType.DMA((len(spans(cols, 2048)),)),
        ],
        compiler_params=vmem(40),
        name="head_stats",
    )(sums, left, in_hbm(right), left_gram, row_state)


def fc6_stats_kernel(
    decay,
    rows,
    sum_ref,
    place_ref,
    left_ref,
    gram_ref,
    row_state_ref,
    col_state_ref,
    *refs,
):
    parts, refs = refs[:-9], refs[-9:]
    right_out, row_new_ref, col_new_ref, row_scale_out, col_scale_ref, total_ref = refs[:6]
    right_ref, row_scale_ref, left = refs[6:]
    height, cols = parts[0].shape
    for number, part in enumerate(parts):
        at = pl.multiple_of(place_ref[number] * height, height)
        right_ref[pl.ds(at, height), :] = part[...]
    copies = [
        pltpu.make_async_copy(right_ref, right_out, left.at[0]),
        pltpu.make_async_copy(row_scale_ref, row_scale_out, left.at[1]),
    ]
    copies[0].start()
    left_gram = gram_ref[...]
    width = left_ref.shape[1]
    col_state = col_state_ref[...].reshape(1, cols)
    right_gram, news, totals = 0.0, [], []
    for first, last in spans(cols, 512):
        right = right_ref[:, first:last]
        right_gram += lax.dot_general(
            right, right, (((1,), (1,)), ((), ())), preferred_element_type=jnp.float32
        )
        col_new = decay * col_state[:, first:last] + (1.0 - decay) * (
            quadratic(left_gram, right) / rows + TINY
        )
        col_scale_ref[:, first:last] = lax.rsqrt(col_new)
        news.append(col_new)
        totals.append(jnp.sum(right.astype(jnp.float32), axis=0, keepdims=True))
    col_new_ref[...] = jnp.concatenate(news, axis=1).reshape(cols)
    total_ref[...] = jnp.concatenate(totals, axis=1).reshape(cols)
    mean_square = jnp.sum(left_gram * right_gram) / (rows * cols)
    row_new = decay * row_state_ref[...].reshape(1, width) + (1.0 - decay) * (
        quadratic(right_gram, left_ref[...]) / cols + TINY
    )
    row_mean = decay * sum_ref[0] / rows + (1.0 - decay) * (mean_square + TINY)
    row_new_ref[...] = row_new.reshape(row_new_ref.shape)
    step = step_size(jnp.full(row_new.shape, sum_ref[1]), rows * cols)
    row_scale = step * lax.rsqrt(row_new / row_mean)
    row_scale_ref[...] = jnp.broadcast_to(row_scale, (128, row_scale.shape[1])).T
    copies[1].start()
    for copy in copies:
        copy.wait()


def fc6_stats(left, parts, places, left_gram, row_state, col_state, sums, rows, decay):
    height, cols = parts[0].shape
    width = left.shape[1]
    smem = pl.BlockSpec(memory_space=pltpu.SMEM)
    return pl.pallas_call(
        functools.partial(fc6_stats_kernel, decay, rows),
        in_specs=[smem] * 2 + [VMEM] * (4 + len(parts)),
        out_specs=[HBM, VMEM, VMEM, HBM, VMEM, VMEM],
        out_shape=[
            pltpu.HBM((height * len(parts), cols), jnp.bfloat16),
            jax.ShapeDtypeStruct((width,), jnp.float32),
            jax.ShapeDtypeStruct((cols,), jnp.float32),
            pltpu.HBM((width, 128), jnp.float32),
            jax.ShapeDtypeStruct((1, cols), jnp.float32),
            jax.ShapeDtypeStruct((cols,), jnp.float32),
        ],
        scratch_shapes=[
            pltpu.VMEM((height * len(parts), cols), jnp.bfloat16),
            pltpu.VMEM((width, 128), jnp.float32),
            pltpu.SemaphoreType.DMA((2,)),
        ],
        compiler_params=vmem(40),
        name="fc6_stats",
    )(sums, places, left, left_gram, row_state, col_state, *parts)


def transpose_kernel(values_ref, out_ref):
    out_ref[...] = values_ref[...].T


def transposed(values):
    return pl.pallas_call(
        transpose_kernel,
        out_shape=jax.ShapeDtypeStruct(values.shape[::-1], values.dtype),
        compiler_params=vmem(24),
        name="transposed",
    )(values)


def row_update_kernel(left_ref, right_ref, weight_ref, row_ref, col_ref, _, grad_ref, new_ref, mark_ref):
    mark_ref[...] = jnp.zeros_like(mark_ref)
    left = left_ref[...]
    row = row_ref[...]
    for first, last in spans(weight_ref.shape[1], 512):
        grad = jnp.dot(left, right_ref[:, first:last], preferred_element_type=jnp.float32)
        grad_ref[:, first:last] = grad
        for at in range(first, last, 128):
            new_ref[:, at : at + 128] = weight_ref[:, at : at + 128] - (
                row * grad[:, at - first : at - first + 128]
            ) * col_ref[:, at : at + 128]


def row_update(left, right, weight, row_scale, col_scale, start):
    rows, cols = weight.shape
    depth = left.shape[1]
    block = block_of(rows, 4 * cols, 8 << 20)
    out = jax.ShapeDtypeStruct((rows, cols), jnp.float32)
    return pl.pallas_call(
        row_update_kernel,
        grid=(rows // block,),
        in_specs=[
            pl.BlockSpec((block, depth), lambda i: (i, 0)),
            pl.BlockSpec((depth, cols), lambda i: (0, 0)),
            pl.BlockSpec((block, cols), lambda i: (i, 0)),
            pl.BlockSpec((block, 128), lambda i: (i, 0)),
            pl.BlockSpec((1, cols), lambda i: (0, 0)),
            pl.BlockSpec(memory_space=pl.ANY),
        ],
        out_specs=[pl.BlockSpec((block, cols), lambda i: (i, 0))] * 2
        + [pl.BlockSpec((8, 128), lambda i: (0, 0))],
        out_shape=[out, out, jax.ShapeDtypeStruct((8, 128), jnp.float32)],
        compiler_params=vmem(60),
        name="row_update",
    )(left, right, in_hbm(weight), row_scale, col_scale, start)


def col_update_kernel(
    decay, rows, left_ref, right_ref, weight_ref, gram_ref, state_ref, scale_ref, *refs
):
    grad_ref, new_ref, col_ref = refs[-3:]
    left = left_ref[...]
    grad = lax.dot_general(
        left, right_ref[...], (((0,), (0,)), ((), ())), preferred_element_type=jnp.float32
    )
    grad_ref[...] = grad
    col_new = decay * state_ref[...].reshape(1, left.shape[1]) + (1.0 - decay) * (
        quadratic(gram_ref[...], left) / rows + TINY
    )
    col_ref[...] = col_new.reshape(col_ref.shape)
    block, width = grad.shape
    by_class = jnp.broadcast_to(lax.rsqrt(col_new), (128, block)).T
    for at in range(0, width, 128):
        new_ref[:, at : at + 128] = weight_ref[:, at : at + 128] - (
            by_class * grad[:, at : at + 128]
        ) * scale_ref[:, at : at + 128]


def col_update(steps, begun, left, right, weight, right_gram, col_state, row_scale, rows, decay, start):
    classes, width = weight.shape
    depth = left.shape[0]
    block = 2048
    first, last = steps
    out = jax.ShapeDtypeStruct((classes, width), jnp.float32)
    any_space = pl.BlockSpec(memory_space=pl.ANY)
    return pl.pallas_call(
        functools.partial(col_update_kernel, decay, rows),
        grid=(last - first,),
        in_specs=[
            pl.BlockSpec((depth, block), lambda i: (0, i + first)),
            pl.BlockSpec((depth, width), lambda i: (0, 0)),
            pl.BlockSpec((block, width), lambda i: (i + first, 0)),
            pl.BlockSpec((depth, depth), lambda i: (0, 0)),
            pl.BlockSpec((block,), lambda i: (i + first,)),
            pl.BlockSpec((1, width), lambda i: (0, 0)),
            any_space,
        ]
        + [any_space] * len(begun),
        out_specs=[pl.BlockSpec((block, width), lambda i: (i + first, 0))] * 2
        + [pl.BlockSpec((block,), lambda i: (i + first,))],
        out_shape=[out, out, jax.ShapeDtypeStruct((classes,), jnp.float32)],
        input_output_aliases={7 + number: number for number in range(len(begun))},
        compiler_params=vmem(60),
        name="col_update",
    )(left, right, in_hbm(weight), right_gram, col_state, row_scale, start, *begun)


def pad_into(maps_ref, padded_ref):
    rows, cols = maps_ref.shape[0], maps_ref.shape[1]
    padded_ref[...] = jnp.zeros_like(padded_ref)
    padded_ref[1 : rows + 1, 1 : cols + 1] = maps_ref[...].astype(jnp.float32)


def norm_sums_kernel(parts_ref, factor_ref, total_ref, *refs):
    sum_ref, conv_ref = refs[-2:]
    channels = factor_ref.shape[1]
    sums = jnp.sum(parts_ref[...], axis=0)
    sum_ref[...] = sums
    conv_ref[0:1, :] = factor_ref[0:1, :] * factor_ref[1:2, :]
    conv_ref[1:2, :] = sums[:, channels : 2 * channels] / total_ref[:, 0:1]
    conv_ref[2:3, :] = sums[:, :channels] / total_ref[:, 0:1]


def norm_sums(parts, factors, pixel_total, *others):
    width, channels = parts.shape[2], factors.shape[1]
    return pl.pallas_call(
        norm_sums_kernel,
        in_specs=[VMEM] * 3
        + [pl.BlockSpec(memory_space=pl.ANY)] * len(others),
        out_specs=[VMEM] * 2,
        out_shape=[
            jax.ShapeDtypeStruct((1, width), jnp.float32),
            jax.ShapeDtypeStruct((3, channels), jnp.float32),
        ],
        compiler_params=vmem(24),
        name="norm_sums",
    )(parts, factors, pixel_total, *others)


def conv_grad_kernel(core_ref, maps_ref, grad_ref, normed_ref, mask_ref, factor_ref, *refs):
    send_ref, keep_ref, padded_ref, grad_buffer, normed_buffer, out, arrived, left = refs[-8:]
    rows, cols, samples, depth = maps_ref.shape
    channels = grad_buffer.shape[3]
    fetch = Fetch([(grad_ref, grad_buffer), (normed_ref, normed_buffer)], arrived, 2)
    pad_into(maps_ref, padded_ref)
    gain, shift_mean, gain_mean = factor_ref[0:1, :], factor_ref[1:2, :], factor_ref[2:3, :]
    fetch.wait()
    fetch.wait()
    mean = (shift_mean + normed_buffer[...] * gain_mean) * mask_ref[...]
    grad = gain * (grad_buffer[...] - mean)
    grad = grad.reshape(-1, channels).T.astype(jnp.bfloat16)
    for shift in range(9):
        down, right = shift // 3, shift % 3
        shifted = padded_ref[down : down + rows, right : right + cols]
        out[shift * depth : (shift + 1) * depth] = jnp.dot(
            grad,
            shifted.reshape(-1, depth).astype(jnp.bfloat16),
            preferred_element_type=jnp.float32,
        ).T.astype(out.dtype)
    half = keep_ref.shape[0]
    own = pl.multiple_of(core_ref[0] * half, half)
    other = pl.multiple_of((1 - core_ref[0]) * half, half)
    copies = [
        pltpu.make_async_copy(out.at[pl.ds(other, half)], send_ref, left.at[0]),
        pltpu.make_async_copy(out.at[pl.ds(own, half)], keep_ref, left.at[1]),
    ]
    for copy in copies:
        copy.start()
    for copy in copies:
        copy.wait()


def conv_grad_of(core, maps, grad_bn, normed, mask, factors):
    rows, cols, samples, depth = maps.shape
    channels = normed.shape[3]
    buffer = pltpu.VMEM(normed.shape, jnp.float32)
    half = pltpu.HBM((9 * depth // 2, channels), jnp.bfloat16)
    return pl.pallas_call(
        conv_grad_kernel,
        in_specs=[pl.BlockSpec(memory_space=pltpu.SMEM), VMEM, HBM, HBM, VMEM, VMEM],
        out_specs=[HBM] * 2,
        out_shape=[half, half],
        scratch_shapes=[
            pltpu.VMEM((rows + 2, cols + 2, samples, depth), jnp.float32),
            buffer,
            buffer,
            pltpu.VMEM((9 * depth, channels), jnp.bfloat16),
            pltpu.SemaphoreType.DMA((2,)),
            pltpu.SemaphoreType.DMA((2,)),
        ],
        compiler_params=vmem(32),
        name="conv_grad",
    )(core[None], maps, in_hbm(grad_bn), in_hbm(normed), mask[:, None], factors)


def silu_slope(values):
    sigma = jax.nn.sigmoid(values)
    return sigma * (1.0 + values * (1.0 - sigma))


def norm_kernel(parts_ref, conv_ref, affine_ref, *refs):
    normed_ref, pooled_ref, factor_ref, count_ref, normed, arrived = refs[-6:]
    grid, _, samples, channels = normed_ref.shape
    cells = (grid - 1) // 2
    sums = jnp.sum(parts_ref[...], axis=0)
    pixels = jnp.sum(sums[:, 2 * channels : 2 * channels + samples]) * (grid * grid)
    center = sums[:, :channels] / pixels
    inv_std = lax.rsqrt(sums[:, channels : 2 * channels] / pixels - center * center + EPSILON)
    gain, shift = affine_ref[0:1, :], affine_ref[1:2, :]
    factor_ref[0:1, :] = inv_std
    factor_ref[1:2, :] = gain
    factor_ref[2:3, :] = shift
    count_ref[...] = jnp.full(count_ref.shape, pixels)
    normed[...] = ((conv_ref[...] - center) * inv_std).reshape(normed.shape)
    copy = pltpu.make_async_copy(normed, normed_ref, arrived.at[0])
    copy.start()
    act = jax.nn.silu(normed[...] * gain + shift)
    for row in range(cells):
        line = act[2 * row] + act[2 * row + 1] + act[2 * row + 2]
        for col in range(cells):
            window = line[2 * col] + line[2 * col + 1] + line[2 * col + 2]
            pooled_ref[row * cells + col] = (window / 9.0).astype(jnp.bfloat16)
    copy.wait()


def norm_and_pool(parts, conv_out, affine, grid, samples, *others):
    channels = conv_out.shape[1]
    cells = ((grid - 1) // 2) ** 2
    shape = (grid, grid, samples, channels)
    return pl.pallas_call(
        norm_kernel,
        in_specs=[VMEM] * 3 + [pl.BlockSpec(memory_space=pl.ANY)] * len(others),
        out_specs=[HBM] + [VMEM] * 3,
        out_shape=[
            pltpu.HBM(shape, jnp.float32),
            jax.ShapeDtypeStruct((cells, samples, channels), jnp.bfloat16),
            jax.ShapeDtypeStruct((3, channels), jnp.float32),
            jax.ShapeDtypeStruct((1, 128), jnp.float32),
        ],
        scratch_shapes=[pltpu.VMEM(shape, jnp.float32), pltpu.SemaphoreType.DMA((1,))],
        compiler_params=vmem(24),
        name="norm_and_pool",
    )(parts, conv_out, affine, *others)


def norm_back_kernel(pooled_ref, normed_ref, factor_ref, *refs):
    grad_ref, sum_ref, normed_buffer, grad_buffer, arrived, left = refs[-6:]
    grid, _, samples, channels = normed_ref.shape
    cells = (grid - 1) // 2
    gain, shift = factor_ref[1:2, :], factor_ref[2:3, :]
    fetch = Fetch([(normed_ref.at[row], normed_buffer.at[row]) for row in range(grid)], arrived, grid)

    def windows(pixel):
        return [cell for cell in range(cells) if 2 * cell <= pixel <= 2 * cell + 2]

    piece = math.gcd(pooled_ref.shape[2], channels)
    blocks = [
        pooled_ref[number].astype(jnp.float32) for number in range(pooled_ref.shape[0])
    ]

    def pooled(cell):
        parts = []
        for at in range(cell * channels, (cell + 1) * channels, piece):
            block, first = divmod(at, pooled_ref.shape[2])
            parts.append(blocks[block][:, first : first + piece])
        return jnp.concatenate(parts, axis=1)

    with_normed = jnp.zeros((samples, channels), jnp.float32)
    alone = jnp.zeros((samples, channels), jnp.float32)
    copies = []
    for row in range(grid):
        line = [
            sum(pooled(cell * cells + col) for cell in windows(row)) / 9.0
            for col in range(cells)
        ]
        fetch.wait()
        for col in range(grid):
            act = sum(line[cell] for cell in windows(col))
            normed = normed_buffer[row, col]
            grad = act * silu_slope(normed * gain + shift)
            grad_buffer[row, col] = grad
            with_normed += grad * normed
            alone += grad
        copy = pltpu.make_async_copy(grad_buffer.at[row], grad_ref.at[row], left.at[row])
        copy.start()
        copies.append(copy)
    sum_ref[0:1, :] = jnp.sum(with_normed, axis=0, keepdims=True)
    sum_ref[1:2, :] = jnp.sum(alone, axis=0, keepdims=True)
    for copy in copies:
        copy.wait()


def norm_backward(grad_pooled, normed, factors, *others):
    buffer = pltpu.VMEM(normed.shape, jnp.float32)
    arrivals = pltpu.SemaphoreType.DMA((normed.shape[0],))
    return pl.pallas_call(
        norm_back_kernel,
        in_specs=[VMEM, HBM, VMEM] + [pl.BlockSpec(memory_space=pl.ANY)] * len(others),
        out_specs=[HBM, VMEM],
        out_shape=[
            pltpu.HBM(normed.shape, jnp.float32),
            jax.ShapeDtypeStruct((2, normed.shape[3]), jnp.float32),
        ],
        scratch_shapes=[buffer, buffer, arrivals, arrivals],
        compiler_params=vmem(24),
        name="norm_backward",
    )(grad_pooled, in_hbm(normed), factors, *others)


def conv_kernel(
    maps_ref,
    weight_ref,
    mask_ref,
    out_ref,
    sum_ref,
    maps_buffer,
    weight_buffer,
    padded_ref,
    patch_ref,
    arrived,
):
    rows, cols, samples, depth = maps_ref.shape
    fetch = Fetch([(maps_ref, maps_buffer), (weight_ref, weight_buffer)], arrived, 2)
    fetch.wait()
    pad_into(maps_buffer, padded_ref)
    for shift in range(9):
        down, right = shift // 3, shift % 3
        shifted = padded_ref[down : down + rows, right : right + cols]
        patch_ref[:, shift * depth : (shift + 1) * depth] = shifted.reshape(-1, depth).astype(
            jnp.bfloat16
        )
    fetch.wait()
    out = jnp.dot(
        patch_ref[...],
        weight_buffer[...].astype(jnp.bfloat16),
        preferred_element_type=jnp.float32,
    )
    out_ref[...] = out
    mask = mask_ref[...]
    by_sample = out.reshape(rows * cols, samples, out.shape[1])
    sum_ref[0:1, :] = jnp.sum(jnp.sum(by_sample, axis=0) * mask, axis=0, keepdims=True)
    sum_ref[1:2, :] = jnp.sum(
        jnp.sum(by_sample * by_sample, axis=0) * mask, axis=0, keepdims=True
    )


def conv_of(maps, weight, mask):
    rows, cols, samples, depth = maps.shape
    channels = weight.shape[1]
    pixels = rows * cols * samples
    return pl.pallas_call(
        conv_kernel,
        in_specs=[HBM, HBM, VMEM],
        out_specs=[VMEM] * 2,
        out_shape=[
            jax.ShapeDtypeStruct((pixels, channels), jnp.float32),
            jax.ShapeDtypeStruct((2, channels), jnp.float32),
        ],
        scratch_shapes=[
            pltpu.VMEM(maps.shape, maps.dtype),
            pltpu.VMEM(weight.shape, weight.dtype),
            pltpu.VMEM((rows + 2, cols + 2, samples, depth), jnp.float32),
            pltpu.VMEM((pixels, 9 * depth), jnp.bfloat16),
            pltpu.SemaphoreType.DMA((2,)),
        ],
        compiler_params=vmem(32),
        name="conv",
    )(in_hbm(maps), in_hbm(weight), mask[:, None])


def sum_kernel(blocks_ref, *refs):
    refs[-1][...] = jnp.sum(blocks_ref[...].astype(jnp.float32), axis=0).astype(jnp.bfloat16)


def sum_blocks(blocks, *others):
    return pl.pallas_call(
        sum_kernel,
        in_specs=[pl.BlockSpec(memory_space=pltpu.VMEM)]
        + [pl.BlockSpec(memory_space=pl.ANY)] * len(others),
        out_shape=jax.ShapeDtypeStruct(blocks.shape[1:], jnp.bfloat16),
        compiler_params=vmem(24),
        name="sum_blocks",
    )(blocks, *others)


def conv_update_kernel(
    decay, core_ref, own_ref, other_ref, weight_ref, row_ref, col_ref, *refs
):
    grad_out, new_out, row_new_ref, col_new_ref = refs[:4]
    own_buffer, weight_buffer, grad_buffer, new_buffer, arrived, left = refs[4:]
    rows, channels = weight_ref.shape
    half = rows // 2
    core = core_ref[0]
    fetch = Fetch(
        [(own_ref, own_buffer), (weight_ref, weight_buffer)],
        arrived,
        2,
    )
    at = pl.multiple_of((1 - core) * half, half)
    grad_buffer[pl.ds(at, half)] = other_ref[...].astype(jnp.float32)
    fetch.wait()
    at = pl.multiple_of(core * half, half)
    grad_buffer[pl.ds(at, half)] = own_buffer[...].astype(jnp.float32)
    copies = [pltpu.make_async_copy(grad_buffer, grad_out, left.at[0])]
    copies[0].start()
    squared = grad_buffer[...] * grad_buffer[...]
    row_square = jnp.broadcast_to(jnp.sum(squared, axis=1, keepdims=True), (rows, 128)).T[:1]
    row_new = decay * row_ref[...].reshape(1, rows) + (1.0 - decay) * (
        row_square / channels + TINY
    )
    col_new = decay * col_ref[...].reshape(1, channels) + (1.0 - decay) * (
        jnp.sum(squared, axis=0, keepdims=True) / rows + TINY
    )
    row_new_ref[...] = row_new.reshape(row_new_ref.shape)
    col_new_ref[...] = col_new.reshape(col_new_ref.shape)
    fetch.wait()
    weight = weight_buffer[...]
    mean_square = jnp.sum(jnp.sum(weight * weight, axis=0, keepdims=True)) / (rows * channels)
    row_mean = jnp.sum(row_new) / rows
    scale = RATE * jnp.maximum(FLOOR, jnp.sqrt(mean_square))
    by_row = jnp.broadcast_to(scale * lax.rsqrt(row_new / row_mean), (128, rows)).T
    by_col = lax.rsqrt(col_new)
    for number, (top, bottom) in enumerate(spans(rows, rows // 4)):
        for first, last in spans(channels, 128):
            new_buffer[top:bottom, first:last] = weight_buffer[top:bottom, first:last] - (
                by_row[top:bottom] * grad_buffer[top:bottom, first:last]
            ) * by_col[:, first:last]
        copy = pltpu.make_async_copy(
            new_buffer.at[top:bottom], new_out.at[top:bottom], left.at[1 + number]
        )
        copy.start()
        copies.append(copy)
    for copy in copies:
        copy.wait()


def conv_update(core, own, other, weight, row_state, col_state, decay):
    rows, channels = weight.shape
    out = pltpu.HBM(weight.shape, jnp.float32)
    buffer = pltpu.VMEM(weight.shape, jnp.float32)
    return pl.pallas_call(
        functools.partial(conv_update_kernel, decay),
        in_specs=[pl.BlockSpec(memory_space=pltpu.SMEM), HBM, VMEM, HBM, VMEM, VMEM],
        out_specs=[HBM, HBM, VMEM, VMEM],
        out_shape=[
            out,
            out,
            jax.ShapeDtypeStruct((rows,), jnp.float32),
            jax.ShapeDtypeStruct((channels,), jnp.float32),
        ],
        scratch_shapes=[
            pltpu.VMEM(own.shape, own.dtype),
            buffer,
            buffer,
            buffer,
            pltpu.SemaphoreType.DMA((2,)),
            pltpu.SemaphoreType.DMA((5,)),
        ],
        compiler_params=vmem(40),
        name="conv_update",
    )(core[None], in_hbm(own), other, in_hbm(weight), row_state, col_state)


def contract_rows(left, right):
    return lax.dot_general(
        left, right, (((0,), (0,)), ((), ())), preferred_element_type=jnp.float32
    )


def exchange(blocks, axis, groups=None):
    return lax.all_to_all(blocks, axis, 0, 0, tiled=True, axis_index_groups=groups)


def gather(values, axis, size, groups=None):
    return exchange(jnp.broadcast_to(values[None], (size,) + values.shape), axis, groups)


class Ring:
    def __init__(self, axis, size, inner):
        self.axis, self.size, self.inner = axis, size, inner
        self.length = lax.axis_size(axis)
        self.own = lax.axis_index(axis) // inner % size

    def other(self, index, shift):
        own = index // self.inner % self.size
        return index + ((own + shift) % self.size - own) * self.inner

    def fetch(self, values, shift):
        pairs = [(self.other(index, shift), index) for index in range(self.length)]
        return lax.ppermute(values, self.axis, pairs)

    def stack(self, parts):
        if self.size == 2:
            first = self.own == 0
            parts = [jnp.where(first, parts[0], parts[1]), jnp.where(first, parts[1], parts[0])]
            return jnp.stack(parts)
        return jnp.roll(jnp.stack(parts), self.own, axis=0)

    def gather(self, values):
        return self.stack([values] + [self.fetch(values, k) for k in range(1, self.size)])

    def scatter_sum(self, blocks, dim):
        def block(shift):
            return lax.dynamic_index_in_dim(
                blocks, (self.own + shift) % self.size, dim, keepdims=False
            )

        result = block(0).astype(jnp.float32)
        for shift in range(1, self.size):
            result += self.fetch(block(-shift), shift).astype(jnp.float32)
        return result


def double_sums(values, axis):
    size = lax.axis_size(axis)
    inner, steps = 1, []
    while inner < size:
        pairs = [(index, index ^ inner) for index in range(size)]
        values = values + lax.ppermute(values, axis, pairs)
        steps.append(values)
        inner *= 2
    return steps


def vector_step(gradient, values, state, decay, seg_widths):
    state_new = decay * state + (1.0 - decay) * (gradient * gradient + TINY)
    scales = []
    offset = 0
    for seg_width in seg_widths:
        segment = values[offset : offset + seg_width]
        scales.append(
            jnp.full((seg_width,), 1.0, jnp.float32)
            * (RATE * jnp.maximum(FLOOR, jnp.sqrt(jnp.mean(segment * segment))))
        )
        offset += seg_width
    return (state_new, values - jnp.concatenate(scales) * gradient * lax.rsqrt(state_new))


def gram(values):
    return lax.dot_general(
        values, values, (((1,), (1,)), ((), ())), preferred_element_type=jnp.float32
    )


def square_sums(gram_matrix, values):
    values = values.astype(jnp.float32)
    return jnp.sum(values * jnp.dot(gram_matrix, values, precision=HIGHEST), axis=0)


def factor_scales(
    left, right, left_gram, right_gram, row_state, col_state, sums, rows, decay
):
    cols = right.shape[1]
    row_new = decay * row_state + (1.0 - decay) * (square_sums(right_gram, left) / cols + TINY)
    col_new = decay * col_state + (1.0 - decay) * (square_sums(left_gram, right) / rows + TINY)
    mean_square = jnp.sum(left_gram * right_gram) / (rows * cols)
    row_mean = decay * sums[0] / rows + (1.0 - decay) * (mean_square + TINY)
    scale = RATE * jnp.maximum(FLOOR, jnp.sqrt(sums[1] / (rows * cols)))
    return row_new, col_new, scale * lax.rsqrt(row_new / row_mean), lax.rsqrt(col_new)


def plain_update(left, right, weight, row_scale, col_scale):
    grad = contract_rows(left, right)
    return grad, weight - (row_scale[:, None] * grad) * col_scale[None, :]


def per_device(
    stem_maps,
    validity,
    labels,
    conv_weight,
    fc6_weight,
    head_weight,
    vectors,
    pca_matrix,
    conv_row_state,
    conv_col_state,
    fc6_row_state,
    fc6_col_state,
    head_row_state,
    head_col_state,
    vector_state,
):
    bf16, f32 = jnp.bfloat16, jnp.float32
    samples, grid = stem_maps.shape[0], stem_maps.shape[1]
    pixels = grid * grid
    channels = conv_weight.shape[1]
    fc_rows, hidden = fc6_weight.shape
    head_rows, classes = head_weight.shape
    wide_count = lax.axis_size("wide")
    grp_count = lax.axis_size("grp")
    count = wide_count * grp_count
    group = samples * wide_count
    my_wide = lax.axis_index("wide")
    decay = 1.0 - STEP ** (-0.8)
    mask = validity.astype(f32)

    core = Ring("grp", 2, 1)
    planes = Ring("grp", grp_count // 2, 2)
    near = Ring("wide", wide_count // 4, 1)
    far = Ring("wide", 4, wide_count // 4)

    bn_gain = vectors[:channels]
    bn_shift = vectors[channels : 2 * channels]
    bias_hidden = vectors[2 * channels : 2 * channels + hidden]
    bias_head = vectors[2 * channels + hidden :]

    maps = stem_maps.transpose(1, 2, 0, 3)
    conv_out, conv_sums = conv_of(maps, conv_weight, mask)
    packed = jnp.concatenate([conv_sums.reshape(-1), mask, labels.astype(f32)])
    everyone = gather(packed[None], ALL, count)
    fc6_left, left_squares = low_and_squares(fc6_weight, 0, hidden // 2, packed)
    normed, pooled, factors, pixel_total = norm_and_pool(
        everyone, conv_out, jnp.stack([bn_gain, bn_shift]), grid, samples, left_squares
    )
    everyone = everyone[:, 0]
    mask_all = everyone[:, 2 * channels : 2 * channels + samples].reshape(-1)
    labels_all = everyone[:, 2 * channels + samples :].reshape(-1)
    valid_count = jnp.sum(mask_all)
    pooled_low = pooled.transpose(1, 0, 2).reshape(samples, -1)

    pooled_blocks = pooled_low.reshape(samples, wide_count, fc_rows).transpose(1, 0, 2)
    pooled_rows = exchange(pooled_blocks, "wide").reshape(group, fc_rows)
    fc6_right, right_squares = low_and_squares(
        fc6_weight, hidden // 2, hidden // 2, pooled_blocks
    )
    pre_part = fc6_forward(pooled_rows, fc6_left, fc6_right)
    pre_blocks = exchange(
        pre_part.reshape(group, wide_count, head_rows).transpose(1, 0, 2), "wide"
    )
    head_low, head_squares = low_and_squares(head_weight.T, 0, head_rows, pre_part)
    pre_hidden = jnp.sum(pre_blocks.astype(f32), axis=0)
    pre_hidden += lax.dynamic_slice_in_dim(bias_hidden, my_wide * head_rows, head_rows)
    feats = jax.nn.silu(pre_hidden).astype(bf16)

    logit_part = head_forward(feats, head_low)
    logit_blocks = exchange(logit_part.reshape(wide_count, samples, classes), "wide")

    pooled_all = lax.all_gather(pooled_rows, "grp", axis=0, tiled=True)
    feats_all = lax.all_gather(feats, "grp", axis=0, tiled=True)
    pooled_columns = transposed(pooled_all)
    pooled_gram, feats_gram = gram(pooled_all), gram(feats_all)
    numbers = jnp.stack(
        [
            jnp.sum(fc6_row_state),
            jnp.sum(left_squares + right_squares),
            jnp.sum(head_row_state),
            jnp.sum(head_squares),
        ]
    )
    all_samples = pooled_all.shape[0]
    per_share = 2 * all_samples // grp_count
    numbers = jnp.pad(numbers, (0, all_samples - numbers.size))
    both_part = jnp.concatenate([pooled_gram, feats_gram])
    both_part = lax.dynamic_slice_in_dim(
        both_part, lax.axis_index("grp") * per_share, per_share
    )
    both_part = jnp.concatenate([both_part, numbers[None]])
    both_steps = double_sums(both_part, "wide")
    both = lax.all_gather(both_steps[-1], "grp")
    sums = both[0, per_share, :8]
    both = both[:, :per_share].reshape(-1, all_samples)
    kept_all = feats_all.astype(f32) * mask_all[:, None]
    feat_center = jnp.sum(kept_all, axis=0) / valid_count
    feat_square = jnp.sum(kept_all * kept_all, axis=0) / valid_count
    feat_scale = lax.rsqrt(feat_square - feat_center * feat_center + EPSILON)
    group_mask = lax.dynamic_slice_in_dim(mask_all, lax.axis_index("grp") * group, group)
    kept = feats.astype(f32) * group_mask[:, None]
    standard = ((kept - feat_center) * feat_scale).astype(bf16)
    projected = jnp.dot(standard, pca_matrix.astype(bf16), preferred_element_type=f32)
    projected = projected.astype(bf16)
    logits = jnp.sum(logit_blocks.astype(f32), axis=0) + bias_head

    same = labels.astype(f32)[:, None] == labels_all[None, :]
    label_count = jnp.sum(jnp.where(same, mask_all[None, :], 0.0), axis=1)
    sample_weight = mask / jnp.maximum(label_count, 1.0)
    sample_weight = follow(sample_weight, both_steps[0], projected, pooled_columns)
    label_hits = labels[:, None] == jnp.arange(classes)[None, :]
    top_logit = jnp.max(logits, axis=1, keepdims=True)
    expo = jnp.exp(logits - top_logit)
    totals = jnp.sum(expo, axis=1, keepdims=True)
    log_total = top_logit[:, 0] + jnp.log(totals[:, 0])
    label_logit = jnp.sum(jnp.where(label_hits, logits, 0.0), axis=1)
    loss_part = jnp.sum(sample_weight * (log_total - label_logit))
    weight_part = jnp.sum(sample_weight)
    grad_logits = (
        sample_weight[:, None] * (expo / totals - label_hits.astype(f32))
    ).astype(bf16)

    logits_group = gather(grad_logits, "wide", wide_count).reshape(group, classes)
    grad_pre = head_backward(logits_group, head_low, pre_hidden)
    rows = samples * projected.shape[1] // head_rows
    pre_blocks = exchange(
        jnp.concatenate(
            [
                jnp.broadcast_to(grad_pre, (wide_count,) + grad_pre.shape),
                projected.reshape(wide_count, rows, head_rows),
            ],
            axis=1,
        ),
        "wide",
    )
    projected = pre_blocks[:, group:].reshape(wide_count, samples, -1)
    pre_blocks = pre_blocks[:, :group]
    pre_group = pre_blocks.transpose(1, 0, 2).reshape(group, hidden)
    grad_pooled_rows = fc6_backward(pre_group, fc6_left, fc6_right)
    feats_gram, pooled_gram = both[all_samples:], both[:all_samples]
    by_kernels = grp_count == 4 and all_samples <= 512
    fc6_rows_total = fc_rows * wide_count
    if by_kernels:
        parts = [pre_group, planes.fetch(pre_group, 1)]
        parts += [core.fetch(part, 1) for part in parts]
        my_grp = lax.axis_index("grp")
        places = jnp.stack([my_grp, my_grp ^ 2, my_grp ^ 1, my_grp ^ 3])
        pre_all, fc6_row_new, fc6_col_new, fc6_by_row, fc6_by_col, grad_bias_hidden = fc6_stats(
            pooled_all,
            parts,
            places,
            pooled_gram,
            fc6_row_state,
            fc6_col_state,
            sums,
            fc6_rows_total,
            decay,
        )
    else:
        pre_all = lax.all_gather(pre_group, "grp", axis=0, tiled=True)
        fc6_row_new, fc6_col_new, fc6_by_row, fc6_by_col = factor_scales(
            pooled_all,
            pre_all,
            pooled_gram,
            gram(pre_all),
            fc6_row_state,
            fc6_col_state,
            sums[:2],
            fc6_rows_total,
            decay,
        )
        grad_bias_hidden = jnp.sum(pre_all.astype(f32), axis=0)
    logits_all = lax.all_gather(logits_group, "grp", axis=0, tiled=True)
    grad_pooled = exchange(grad_pooled_rows.reshape(wide_count, samples, fc_rows), "wide")
    grad_bn, bn_sums = norm_backward(
        grad_pooled, normed, factors, both
    )
    bn_sums = jnp.concatenate([bn_sums.reshape(-1), jnp.stack([loss_part, weight_part])])
    bn_sums, conv_factors = norm_sums(
        gather(bn_sums[None], ALL, count), factors, pixel_total, fc6_by_col
    )
    bn_sums = bn_sums[0]
    grad_gain, grad_shift = bn_sums[:channels], bn_sums[channels : 2 * channels]
    conv_send, conv_keep = conv_grad_of(core.own, maps, grad_bn, normed, mask, conv_factors)
    chips = count // 2
    same_core = [
        [grp * wide_count + wide for grp in range(first, grp_count, 2) for wide in range(wide_count)]
        for first in range(2)
    ]
    conv_half = (conv_keep.astype(f32) + core.fetch(conv_send, 1).astype(f32)).astype(bf16)
    conv_blocks = exchange(conv_half.reshape(chips, -1, channels), ALL, same_core)

    if by_kernels:
        fc6_grad, fc6_new, mark = row_update(
            pooled_columns, pre_all, fc6_weight, fc6_by_row, fc6_by_col, conv_half
        )
        conv_share = sum_blocks(conv_blocks, mark)
        head_row_new, head_by_row, grad_bias_head = head_stats(
            feats_all,
            logits_all,
            feats_gram,
            head_row_state,
            sums,
            hidden,
            decay,
        )
        update_head = functools.partial(
            col_update,
            left=logits_all,
            right=feats_all,
            weight=head_weight.T,
            right_gram=feats_gram,
            col_state=head_col_state,
            row_scale=head_by_row,
            rows=hidden,
            decay=decay,
        )
        blocks = pl.cdiv(classes, 2048)
        begun = update_head((0, blocks // 2 + 1), (), start=conv_share)
        conv_own = gather(conv_share, ALL, chips, same_core).reshape(-1, channels)
        conv_own = carry(conv_own, begun[2])
        head_grad, head_new, head_col_new = update_head(
            (blocks // 2 + 1, blocks), begun, start=conv_own
        )
        head_grad, head_new = head_grad.T, head_new.T
    else:
        fc6_grad, fc6_new = plain_update(pooled_all, pre_all, fc6_weight, fc6_by_row, fc6_by_col)
        head_row_new, head_col_new, head_by_row, head_by_col = factor_scales(
            feats_all,
            logits_all,
            feats_gram,
            gram(logits_all),
            head_row_state,
            head_col_state,
            sums[2:],
            hidden,
            decay,
        )
        head_grad, head_new = plain_update(
            feats_all, logits_all, head_weight, head_by_row, head_by_col
        )
        grad_bias_head = jnp.sum(logits_all.astype(f32), axis=0)
        conv_share = sum_blocks(conv_blocks)
        conv_own = gather(conv_share, ALL, chips, same_core).reshape(-1, channels)
    conv_grad, conv_new, conv_row_new, conv_col_new = conv_update(
        core.own,
        conv_own,
        core.fetch(conv_own, 1),
        conv_weight,
        conv_row_state,
        conv_col_state,
        decay,
    )
    vector_grad = jnp.concatenate([grad_gain, grad_shift, grad_bias_hidden, grad_bias_head])
    vector_state_new, vector_new = vector_step(
        vector_grad, vectors, vector_state, decay, (channels, channels, hidden, classes)
    )

    projected = jnp.sum(projected.astype(f32), axis=0)
    embedded = projected * lax.rsqrt(
        jnp.sum(projected * projected, axis=1, keepdims=True) + NORM_EPS
    )
    return (
        bn_sums[2 * channels],
        bn_sums[2 * channels + 1],
        embedded,
        conv_grad,
        conv_row_new,
        conv_col_new,
        conv_new,
        fc6_grad,
        fc6_row_new,
        fc6_col_new,
        fc6_new,
        head_grad,
        head_row_new,
        head_col_new,
        head_new,
        vector_grad,
        vector_state_new,
        vector_new,
    )


def solution(mesh):
    in_specs = (
        P(("grp", "wide"), None, None, None),
        P(("grp", "wide")),
        P(("grp", "wide")),
        P(),
        P("wide", None),
        P("wide", None),
        P(),
        P("wide", None),
        P(),
        P(),
        P("wide"),
        P(),
        P("wide"),
        P(),
        P(),
    )
    out_specs = (
        P(),
        P(),
        P(("grp", "wide"), None),
        P(),
        P(),
        P(),
        P(),
        P("wide", None),
        P("wide"),
        P(),
        P("wide", None),
        P("wide", None),
        P("wide"),
        P(),
        P("wide", None),
        P(),
        P(),
        P(),
    )
    return jax.shard_map(
        per_device, mesh=mesh, in_specs=in_specs, out_specs=out_specs, check_vma=False
    )
```

```python
import functools
import math

import jax
import jax.numpy as jnp
from jax import lax
from jax.experimental import pallas as pl
from jax.experimental.pallas import tpu as pltpu
from jax.sharding import PartitionSpec as P

STEP = 10


EPSILON = 1e-05
TINY = 1e-30
RATE = 0.5
FLOOR = 0.001
NORM_EPS = 1e-06
HIGHEST = lax.Precision.HIGHEST
ALL = ("grp", "wide")


def block_of(rows, row_bytes, limit):
    sizes = [n for n in range(16, rows + 1, 16) if rows % n == 0 and n * row_bytes <= limit]
    return max(sizes) if sizes else rows


def vmem(megabytes):
    return pltpu.CompilerParams(vmem_limit_bytes=megabytes << 20)


def follow_kernel(*refs):
    refs[-1][...] = refs[0][...]


def follow(values, *others):
    return pl.pallas_call(
        follow_kernel,
        in_specs=[pl.BlockSpec(memory_space=pltpu.VMEM)]
        + [pl.BlockSpec(memory_space=pl.ANY)] * len(others),
        out_specs=pl.BlockSpec(memory_space=pltpu.VMEM),
        out_shape=jax.ShapeDtypeStruct(values.shape, values.dtype),
        name="follow",
    )(values, *others)


def carry_kernel(values_ref, *refs):
    out_ref, arrived = refs[-2:]
    copy = pltpu.make_async_copy(values_ref, out_ref, arrived.at[0])
    copy.start()
    copy.wait()


def carry(values, *others):
    return pl.pallas_call(
        carry_kernel,
        in_specs=[VMEM] + [pl.BlockSpec(memory_space=pl.ANY)] * len(others),
        out_specs=HBM,
        out_shape=pltpu.HBM(values.shape, values.dtype),
        scratch_shapes=[pltpu.SemaphoreType.DMA((1,))],
        compiler_params=vmem(24),
        name="carry",
    )(values, *others)


def low_kernel(weight_ref, _, low_ref, square_ref):
    @pl.when(pl.program_id(0) == 0)
    def _():
        square_ref[...] = jnp.zeros_like(square_ref)

    weight = weight_ref[...]
    low_ref[...] = weight.astype(jnp.bfloat16)
    square_ref[...] += jnp.sum((weight * weight).reshape(-1, 8, weight.shape[1]), axis=0)


def in_hbm(array):
    return pltpu.with_memory_space_constraint(array, pltpu.HBM)


HBM = pl.BlockSpec(memory_space=pltpu.HBM)
VMEM = pl.BlockSpec(memory_space=pltpu.VMEM)


def spans(length, step):
    return [(first, min(first + step, length)) for first in range(0, length, step)]


class Fetch:
    def __init__(self, pairs, arrived, depth):
        self.copies = [
            pltpu.make_async_copy(source, target, arrived.at[number])
            for number, (source, target) in enumerate(pairs)
        ]
        self.depth, self.done = depth, 0
        for copy in self.copies[:depth]:
            copy.start()

    def wait(self):
        self.copies[self.done].wait()
        for copy in self.copies[self.done + self.depth : self.done + self.depth + 1]:
            copy.start()
        self.done += 1


def low_and_squares(weight, first, cols, start):
    rows = weight.shape[0]
    block = block_of(rows, 4 * cols, 4 << 20)
    low, squares = pl.pallas_call(
        low_kernel,
        grid=(rows // block,),
        in_specs=[
            pl.BlockSpec((block, cols), lambda i: (i, first // cols)),
            pl.BlockSpec(memory_space=pl.ANY),
        ],
        out_specs=[
            pl.BlockSpec((block, cols), lambda i: (i, 0)),
            pl.BlockSpec((8, cols), lambda i: (0, 0)),
        ],
        out_shape=[
            pltpu.HBM((rows, cols), jnp.bfloat16),
            jax.ShapeDtypeStruct((8, cols), jnp.float32),
        ],
        compiler_params=vmem(24),
        name="low_and_squares",
    )(in_hbm(weight), start)
    return low, squares


def fc6_kernel(rows_ref, left_ref, right_ref, out_ref, buffer, arrived):
    half = left_ref.shape[1]
    blocks = [
        (ref, first, last, side * half)
        for side, ref in enumerate((left_ref, right_ref))
        for first, last in spans(half, 512)
    ]
    fetch = Fetch(
        [
            (ref.at[:, first:last], buffer.at[:, base + first : base + last])
            for ref, first, last, base in blocks
        ],
        arrived,
        4,
    )
    for _, first, last, base in blocks:
        fetch.wait()
        out_ref[:, base + first : base + last] = jnp.dot(
            rows_ref[...],
            buffer[:, base + first : base + last],
            preferred_element_type=jnp.float32,
        ).astype(out_ref.dtype)


def fc6_forward(values, left, right):
    depth, half = left.shape
    blocks = 2 * len(spans(half, 512))
    return pl.pallas_call(
        fc6_kernel,
        in_specs=[VMEM, HBM, HBM],
        out_specs=VMEM,
        out_shape=jax.ShapeDtypeStruct((values.shape[0], 2 * half), jnp.bfloat16),
        scratch_shapes=[
            pltpu.VMEM((depth, 2 * half), left.dtype),
            pltpu.SemaphoreType.DMA((blocks,)),
        ],
        compiler_params=vmem(32),
        name="fc6_forward",
    )(values, in_hbm(left), in_hbm(right))


def fc6_back_kernel(grad_ref, left_ref, right_ref, *refs):
    out_ref, buffer, arrived = refs[-3:]
    rows, half = left_ref.shape
    blocks = spans(rows, 512)
    fetch = Fetch(
        [
            (ref.at[first:last], buffer.at[side, first:last])
            for first, last in blocks
            for side, ref in enumerate((left_ref, right_ref))
        ],
        arrived,
        4,
    )
    for first, last in blocks:
        part = 0.0
        for side in range(2):
            fetch.wait()
            part += lax.dot_general(
                grad_ref[:, side * half : (side + 1) * half],
                buffer[side, first:last],
                (((1,), (1,)), ((), ())),
                preferred_element_type=jnp.float32,
            )
        out_ref[:, first:last] = part.astype(out_ref.dtype)


def fc6_backward(grad, left, right, *others):
    rows, half = left.shape
    return pl.pallas_call(
        fc6_back_kernel,
        in_specs=[VMEM, HBM, HBM] + [pl.BlockSpec(memory_space=pl.ANY)] * len(others),
        out_specs=VMEM,
        out_shape=jax.ShapeDtypeStruct((grad.shape[0], rows), jnp.bfloat16),
        scratch_shapes=[
            pltpu.VMEM((2, rows, half), left.dtype),
            pltpu.SemaphoreType.DMA((2 * len(spans(rows, 512)),)),
        ],
        compiler_params=vmem(32),
        name="fc6_backward",
    )(grad, in_hbm(left), in_hbm(right), *others)


def head_kernel(feats_ref, weight_ref, out_ref, buffer, arrived):
    blocks = spans(weight_ref.shape[0], 1024)
    fetch = Fetch(
        [(weight_ref.at[first:last], buffer.at[first:last]) for first, last in blocks], arrived, 4
    )
    for first, last in blocks:
        fetch.wait()
        out_ref[:, first:last] = lax.dot_general(
            feats_ref[...],
            buffer[first:last],
            (((1,), (1,)), ((), ())),
            preferred_element_type=jnp.float32,
        ).astype(out_ref.dtype)


def head_forward(feats, weight):
    classes = weight.shape[0]
    return pl.pallas_call(
        head_kernel,
        in_specs=[VMEM, HBM],
        out_specs=VMEM,
        out_shape=jax.ShapeDtypeStruct((feats.shape[0], classes), jnp.bfloat16),
        scratch_shapes=[
            pltpu.VMEM(weight.shape, weight.dtype),
            pltpu.SemaphoreType.DMA((len(spans(classes, 1024)),)),
        ],
        compiler_params=vmem(32),
        name="head_forward",
    )(feats, in_hbm(weight))


def head_back_kernel(grad_ref, weight_ref, pre_ref, *refs):
    out_ref, grad_buffer, buffer, arrived = refs[-4:]
    blocks = spans(weight_ref.shape[0], 1024)
    fetch = Fetch(
        [(grad_ref, grad_buffer)]
        + [(weight_ref.at[first:last], buffer.at[first:last]) for first, last in blocks],
        arrived,
        5,
    )
    fetch.wait()
    total = 0.0
    for first, last in blocks:
        fetch.wait()
        total += jnp.dot(
            grad_buffer[:, first:last], buffer[first:last], preferred_element_type=jnp.float32
        )
    out_ref[...] = (total * silu_slope(pre_ref[...])).astype(out_ref.dtype)


def head_backward(grad, weight, pre_hidden, *others):
    return pl.pallas_call(
        head_back_kernel,
        in_specs=[HBM, HBM, VMEM] + [pl.BlockSpec(memory_space=pl.ANY)] * len(others),
        out_specs=VMEM,
        out_shape=jax.ShapeDtypeStruct(pre_hidden.shape, jnp.bfloat16),
        scratch_shapes=[
            pltpu.VMEM(grad.shape, grad.dtype),
            pltpu.VMEM(weight.shape, weight.dtype),
            pltpu.SemaphoreType.DMA((1 + len(spans(weight.shape[0], 1024)),)),
        ],
        compiler_params=vmem(32),
        name="head_backward",
    )(in_hbm(grad), in_hbm(weight), pre_hidden, *others)


def pieces(matrix):
    first = matrix.astype(jnp.bfloat16)
    rest = matrix - first.astype(jnp.float32)
    second = rest.astype(jnp.bfloat16)
    third = (rest - second.astype(jnp.float32)).astype(jnp.bfloat16)
    return first, second, third


def quadratic(matrix, values):
    product = sum(
        jnp.dot(piece, values, preferred_element_type=jnp.float32) for piece in pieces(matrix)
    )
    return jnp.sum(product * values.astype(jnp.float32), axis=0, keepdims=True)


def step_size(squares, count):
    return RATE * jnp.maximum(FLOOR, jnp.sqrt(squares / count))


def head_stats_kernel(
    decay,
    rows,
    sum_ref,
    left_ref,
    right_ref,
    gram_ref,
    state_ref,
    new_ref,
    scale_ref,
    total_ref,
    buffer,
    arrived,
):
    cols = right_ref.shape[1]
    blocks = spans(cols, 2048)
    fetch = Fetch(
        [(right_ref.at[:, first:last], buffer.at[:, first:last]) for first, last in blocks],
        arrived,
        len(blocks),
    )
    right_gram, totals = 0.0, []
    for first, last in blocks:
        fetch.wait()
        right = buffer[:, first:last]
        right_gram += lax.dot_general(
            right, right, (((1,), (1,)), ((), ())), preferred_element_type=jnp.float32
        )
        totals.append(jnp.sum(right.astype(jnp.float32), axis=0, keepdims=True))
    total_ref[...] = jnp.concatenate(totals, axis=1).reshape(cols)
    mean_square = jnp.sum(gram_ref[...] * right_gram) / (rows * cols)
    width = left_ref.shape[1]
    row_new = decay * state_ref[...].reshape(1, width) + (1.0 - decay) * (
        quadratic(right_gram, left_ref[...]) / cols + TINY
    )
    row_mean = decay * sum_ref[2] / rows + (1.0 - decay) * (mean_square + TINY)
    new_ref[...] = row_new.reshape(width)
    step = step_size(jnp.full(row_new.shape, sum_ref[3]), rows * cols)
    scale_ref[...] = step * lax.rsqrt(row_new / row_mean)


def head_stats(left, right, left_gram, row_state, sums, rows, decay):
    width, cols = left.shape[1], right.shape[1]
    smem = pl.BlockSpec(memory_space=pltpu.SMEM)
    return pl.pallas_call(
        functools.partial(head_stats_kernel, decay, rows),
        in_specs=[smem, VMEM, HBM, VMEM, VMEM],
        out_specs=[VMEM] * 3,
        out_shape=[
            jax.ShapeDtypeStruct((width,), jnp.float32),
            jax.ShapeDtypeStruct((1, width), jnp.float32),
            jax.ShapeDtypeStruct((cols,), jnp.float32),
        ],
        scratch_shapes=[
            pltpu.VMEM(right.shape, right.dtype),
            pltpu.SemaphoreType.DMA((len(spans(cols, 2048)),)),
        ],
        compiler_params=vmem(40),
        name="head_stats",
    )(sums, left, in_hbm(right), left_gram, row_state)


def fc6_stats_kernel(
    decay,
    rows,
    sum_ref,
    place_ref,
    left_ref,
    gram_ref,
    row_state_ref,
    col_state_ref,
    *refs,
):
    parts, refs = refs[:-9], refs[-9:]
    right_out, row_new_ref, col_new_ref, row_scale_out, col_scale_ref, total_ref = refs[:6]
    right_ref, row_scale_ref, left = refs[6:]
    height, cols = parts[0].shape
    for number, part in enumerate(parts):
        at = pl.multiple_of(place_ref[number] * height, height)
        right_ref[pl.ds(at, height), :] = part[...]
    copies = [
        pltpu.make_async_copy(right_ref, right_out, left.at[0]),
        pltpu.make_async_copy(row_scale_ref, row_scale_out, left.at[1]),
    ]
    copies[0].start()
    left_gram = gram_ref[...]
    width = left_ref.shape[1]
    col_state = col_state_ref[...].reshape(1, cols)
    right_gram, news, totals = 0.0, [], []
    for first, last in spans(cols, 512):
        right = right_ref[:, first:last]
        right_gram += lax.dot_general(
            right, right, (((1,), (1,)), ((), ())), preferred_element_type=jnp.float32
        )
        col_new = decay * col_state[:, first:last] + (1.0 - decay) * (
            quadratic(left_gram, right) / rows + TINY
        )
        col_scale_ref[:, first:last] = lax.rsqrt(col_new)
        news.append(col_new)
        totals.append(jnp.sum(right.astype(jnp.float32), axis=0, keepdims=True))
    col_new_ref[...] = jnp.concatenate(news, axis=1).reshape(cols)
    total_ref[...] = jnp.concatenate(totals, axis=1).reshape(cols)
    mean_square = jnp.sum(left_gram * right_gram) / (rows * cols)
    row_new = decay * row_state_ref[...].reshape(1, width) + (1.0 - decay) * (
        quadratic(right_gram, left_ref[...]) / cols + TINY
    )
    row_mean = decay * sum_ref[0] / rows + (1.0 - decay) * (mean_square + TINY)
    row_new_ref[...] = row_new.reshape(row_new_ref.shape)
    step = step_size(jnp.full(row_new.shape, sum_ref[1]), rows * cols)
    row_scale = step * lax.rsqrt(row_new / row_mean)
    row_scale_ref[...] = jnp.broadcast_to(row_scale, (128, row_scale.shape[1])).T
    copies[1].start()
    for copy in copies:
        copy.wait()


def fc6_stats(left, parts, places, left_gram, row_state, col_state, sums, rows, decay):
    height, cols = parts[0].shape
    width = left.shape[1]
    smem = pl.BlockSpec(memory_space=pltpu.SMEM)
    return pl.pallas_call(
        functools.partial(fc6_stats_kernel, decay, rows),
        in_specs=[smem] * 2 + [VMEM] * (4 + len(parts)),
        out_specs=[HBM, VMEM, VMEM, HBM, VMEM, VMEM],
        out_shape=[
            pltpu.HBM((height * len(parts), cols), jnp.bfloat16),
            jax.ShapeDtypeStruct((width,), jnp.float32),
            jax.ShapeDtypeStruct((cols,), jnp.float32),
            pltpu.HBM((width, 128), jnp.float32),
            jax.ShapeDtypeStruct((1, cols), jnp.float32),
            jax.ShapeDtypeStruct((cols,), jnp.float32),
        ],
        scratch_shapes=[
            pltpu.VMEM((height * len(parts), cols), jnp.bfloat16),
            pltpu.VMEM((width, 128), jnp.float32),
            pltpu.SemaphoreType.DMA((2,)),
        ],
        compiler_params=vmem(40),
        name="fc6_stats",
    )(sums, places, left, left_gram, row_state, col_state, *parts)


def transpose_kernel(values_ref, out_ref):
    out_ref[...] = values_ref[...].T


def transposed(values):
    return pl.pallas_call(
        transpose_kernel,
        out_shape=jax.ShapeDtypeStruct(values.shape[::-1], values.dtype),
        compiler_params=vmem(24),
        name="transposed",
    )(values)


def row_update_kernel(left_ref, right_ref, weight_ref, row_ref, col_ref, _, grad_ref, new_ref, mark_ref):
    mark_ref[...] = jnp.zeros_like(mark_ref)
    left = left_ref[...]
    row = row_ref[...]
    for first, last in spans(weight_ref.shape[1], 512):
        grad = jnp.dot(left, right_ref[:, first:last], preferred_element_type=jnp.float32)
        grad_ref[:, first:last] = grad
        for at in range(first, last, 128):
            new_ref[:, at : at + 128] = weight_ref[:, at : at + 128] - (
                row * grad[:, at - first : at - first + 128]
            ) * col_ref[:, at : at + 128]


def row_update(left, right, weight, row_scale, col_scale, start):
    rows, cols = weight.shape
    depth = left.shape[1]
    block = block_of(rows, 4 * cols, 8 << 20)
    out = jax.ShapeDtypeStruct((rows, cols), jnp.float32)
    return pl.pallas_call(
        row_update_kernel,
        grid=(rows // block,),
        in_specs=[
            pl.BlockSpec((block, depth), lambda i: (i, 0)),
            pl.BlockSpec((depth, cols), lambda i: (0, 0)),
            pl.BlockSpec((block, cols), lambda i: (i, 0)),
            pl.BlockSpec((block, 128), lambda i: (i, 0)),
            pl.BlockSpec((1, cols), lambda i: (0, 0)),
            pl.BlockSpec(memory_space=pl.ANY),
        ],
        out_specs=[pl.BlockSpec((block, cols), lambda i: (i, 0))] * 2
        + [pl.BlockSpec((8, 128), lambda i: (0, 0))],
        out_shape=[out, out, jax.ShapeDtypeStruct((8, 128), jnp.float32)],
        compiler_params=vmem(60),
        name="row_update",
    )(left, right, in_hbm(weight), row_scale, col_scale, start)


def col_update_kernel(
    decay, rows, left_ref, right_ref, weight_ref, gram_ref, state_ref, scale_ref, *refs
):
    grad_ref, new_ref, col_ref = refs[-3:]
    left = left_ref[...]
    grad = lax.dot_general(
        left, right_ref[...], (((0,), (0,)), ((), ())), preferred_element_type=jnp.float32
    )
    grad_ref[...] = grad
    col_new = decay * state_ref[...].reshape(1, left.shape[1]) + (1.0 - decay) * (
        quadratic(gram_ref[...], left) / rows + TINY
    )
    col_ref[...] = col_new.reshape(col_ref.shape)
    block, width = grad.shape
    by_class = jnp.broadcast_to(lax.rsqrt(col_new), (128, block)).T
    for at in range(0, width, 128):
        new_ref[:, at : at + 128] = weight_ref[:, at : at + 128] - (
            by_class * grad[:, at : at + 128]
        ) * scale_ref[:, at : at + 128]


def col_update(steps, begun, left, right, weight, right_gram, col_state, row_scale, rows, decay, start):
    classes, width = weight.shape
    depth = left.shape[0]
    block = 2048
    first, last = steps
    out = jax.ShapeDtypeStruct((classes, width), jnp.float32)
    any_space = pl.BlockSpec(memory_space=pl.ANY)
    return pl.pallas_call(
        functools.partial(col_update_kernel, decay, rows),
        grid=(last - first,),
        in_specs=[
            pl.BlockSpec((depth, block), lambda i: (0, i + first)),
            pl.BlockSpec((depth, width), lambda i: (0, 0)),
            pl.BlockSpec((block, width), lambda i: (i + first, 0)),
            pl.BlockSpec((depth, depth), lambda i: (0, 0)),
            pl.BlockSpec((block,), lambda i: (i + first,)),
            pl.BlockSpec((1, width), lambda i: (0, 0)),
            any_space,
        ]
        + [any_space] * len(begun),
        out_specs=[pl.BlockSpec((block, width), lambda i: (i + first, 0))] * 2
        + [pl.BlockSpec((block,), lambda i: (i + first,))],
        out_shape=[out, out, jax.ShapeDtypeStruct((classes,), jnp.float32)],
        input_output_aliases={7 + number: number for number in range(len(begun))},
        compiler_params=vmem(60),
        name="col_update",
    )(left, right, in_hbm(weight), right_gram, col_state, row_scale, start, *begun)


def pad_into(maps_ref, padded_ref):
    rows, cols = maps_ref.shape[0], maps_ref.shape[1]
    padded_ref[...] = jnp.zeros_like(padded_ref)
    padded_ref[1 : rows + 1, 1 : cols + 1] = maps_ref[...].astype(jnp.float32)


def norm_sums_kernel(parts_ref, factor_ref, total_ref, *refs):
    sum_ref, conv_ref = refs[-2:]
    channels = factor_ref.shape[1]
    sums = jnp.sum(parts_ref[...], axis=0)
    sum_ref[...] = sums
    conv_ref[0:1, :] = factor_ref[0:1, :] * factor_ref[1:2, :]
    conv_ref[1:2, :] = sums[:, channels : 2 * channels] / total_ref[:, 0:1]
    conv_ref[2:3, :] = sums[:, :channels] / total_ref[:, 0:1]


def norm_sums(parts, factors, pixel_total, *others):
    width, channels = parts.shape[2], factors.shape[1]
    return pl.pallas_call(
        norm_sums_kernel,
        in_specs=[VMEM] * 3
        + [pl.BlockSpec(memory_space=pl.ANY)] * len(others),
        out_specs=[VMEM] * 2,
        out_shape=[
            jax.ShapeDtypeStruct((1, width), jnp.float32),
            jax.ShapeDtypeStruct((3, channels), jnp.float32),
        ],
        compiler_params=vmem(24),
        name="norm_sums",
    )(parts, factors, pixel_total, *others)


def conv_grad_kernel(core_ref, maps_ref, grad_ref, normed_ref, mask_ref, factor_ref, *refs):
    send_ref, keep_ref, padded_ref, grad_buffer, normed_buffer, out, arrived, left = refs[-8:]
    rows, cols, samples, depth = maps_ref.shape
    channels = grad_buffer.shape[3]
    fetch = Fetch([(grad_ref, grad_buffer), (normed_ref, normed_buffer)], arrived, 2)
    pad_into(maps_ref, padded_ref)
    gain, shift_mean, gain_mean = factor_ref[0:1, :], factor_ref[1:2, :], factor_ref[2:3, :]
    fetch.wait()
    fetch.wait()
    mean = (shift_mean + normed_buffer[...] * gain_mean) * mask_ref[...]
    grad = gain * (grad_buffer[...] - mean)
    grad = grad.reshape(-1, channels).T.astype(jnp.bfloat16)
    for shift in range(9):
        down, right = shift // 3, shift % 3
        shifted = padded_ref[down : down + rows, right : right + cols]
        out[shift * depth : (shift + 1) * depth] = jnp.dot(
            grad,
            shifted.reshape(-1, depth).astype(jnp.bfloat16),
            preferred_element_type=jnp.float32,
        ).T.astype(out.dtype)
    half = keep_ref.shape[0]
    own = pl.multiple_of(core_ref[0] * half, half)
    other = pl.multiple_of((1 - core_ref[0]) * half, half)
    copies = [
        pltpu.make_async_copy(out.at[pl.ds(other, half)], send_ref, left.at[0]),
        pltpu.make_async_copy(out.at[pl.ds(own, half)], keep_ref, left.at[1]),
    ]
    for copy in copies:
        copy.start()
    for copy in copies:
        copy.wait()


def conv_grad_of(core, maps, grad_bn, normed, mask, factors):
    rows, cols, samples, depth = maps.shape
    channels = normed.shape[3]
    buffer = pltpu.VMEM(normed.shape, jnp.float32)
    half = pltpu.HBM((9 * depth // 2, channels), jnp.bfloat16)
    return pl.pallas_call(
        conv_grad_kernel,
        in_specs=[pl.BlockSpec(memory_space=pltpu.SMEM), VMEM, HBM, HBM, VMEM, VMEM],
        out_specs=[HBM] * 2,
        out_shape=[half, half],
        scratch_shapes=[
            pltpu.VMEM((rows + 2, cols + 2, samples, depth), jnp.float32),
            buffer,
            buffer,
            pltpu.VMEM((9 * depth, channels), jnp.bfloat16),
            pltpu.SemaphoreType.DMA((2,)),
            pltpu.SemaphoreType.DMA((2,)),
        ],
        compiler_params=vmem(32),
        name="conv_grad",
    )(core[None], maps, in_hbm(grad_bn), in_hbm(normed), mask[:, None], factors)


def silu_slope(values):
    sigma = jax.nn.sigmoid(values)
    return sigma * (1.0 + values * (1.0 - sigma))


def norm_kernel(parts_ref, conv_ref, affine_ref, *refs):
    normed_ref, pooled_ref, factor_ref, count_ref, normed, arrived = refs[-6:]
    grid, _, samples, channels = normed_ref.shape
    cells = (grid - 1) // 2
    sums = jnp.sum(parts_ref[...], axis=0)
    pixels = jnp.sum(sums[:, 2 * channels : 2 * channels + samples]) * (grid * grid)
    center = sums[:, :channels] / pixels
    inv_std = lax.rsqrt(sums[:, channels : 2 * channels] / pixels - center * center + EPSILON)
    gain, shift = affine_ref[0:1, :], affine_ref[1:2, :]
    factor_ref[0:1, :] = inv_std
    factor_ref[1:2, :] = gain
    factor_ref[2:3, :] = shift
    count_ref[...] = jnp.full(count_ref.shape, pixels)
    normed[...] = ((conv_ref[...] - center) * inv_std).reshape(normed.shape)
    copy = pltpu.make_async_copy(normed, normed_ref, arrived.at[0])
    copy.start()
    act = jax.nn.silu(normed[...] * gain + shift)
    for row in range(cells):
        line = act[2 * row] + act[2 * row + 1] + act[2 * row + 2]
        for col in range(cells):
            window = line[2 * col] + line[2 * col + 1] + line[2 * col + 2]
            pooled_ref[row * cells + col] = (window / 9.0).astype(jnp.bfloat16)
    copy.wait()


def norm_and_pool(parts, conv_out, affine, grid, samples, *others):
    channels = conv_out.shape[1]
    cells = ((grid - 1) // 2) ** 2
    shape = (grid, grid, samples, channels)
    return pl.pallas_call(
        norm_kernel,
        in_specs=[VMEM] * 3 + [pl.BlockSpec(memory_space=pl.ANY)] * len(others),
        out_specs=[HBM] + [VMEM] * 3,
        out_shape=[
            pltpu.HBM(shape, jnp.float32),
            jax.ShapeDtypeStruct((cells, samples, channels), jnp.bfloat16),
            jax.ShapeDtypeStruct((3, channels), jnp.float32),
            jax.ShapeDtypeStruct((1, 128), jnp.float32),
        ],
        scratch_shapes=[pltpu.VMEM(shape, jnp.float32), pltpu.SemaphoreType.DMA((1,))],
        compiler_params=vmem(24),
        name="norm_and_pool",
    )(parts, conv_out, affine, *others)


def norm_back_kernel(pooled_ref, normed_ref, factor_ref, *refs):
    grad_ref, sum_ref, normed_buffer, grad_buffer, arrived, left = refs[-6:]
    grid, _, samples, channels = normed_ref.shape
    cells = (grid - 1) // 2
    gain, shift = factor_ref[1:2, :], factor_ref[2:3, :]
    fetch = Fetch([(normed_ref.at[row], normed_buffer.at[row]) for row in range(grid)], arrived, grid)

    def windows(pixel):
        return [cell for cell in range(cells) if 2 * cell <= pixel <= 2 * cell + 2]

    piece = math.gcd(pooled_ref.shape[2], channels)
    blocks = [
        pooled_ref[number].astype(jnp.float32) for number in range(pooled_ref.shape[0])
    ]

    def pooled(cell):
        parts = []
        for at in range(cell * channels, (cell + 1) * channels, piece):
            block, first = divmod(at, pooled_ref.shape[2])
            parts.append(blocks[block][:, first : first + piece])
        return jnp.concatenate(parts, axis=1)

    with_normed = jnp.zeros((samples, channels), jnp.float32)
    alone = jnp.zeros((samples, channels), jnp.float32)
    copies = []
    for row in range(grid):
        line = [
            sum(pooled(cell * cells + col) for cell in windows(row)) / 9.0
            for col in range(cells)
        ]
        fetch.wait()
        for col in range(grid):
            act = sum(line[cell] for cell in windows(col))
            normed = normed_buffer[row, col]
            grad = act * silu_slope(normed * gain + shift)
            grad_buffer[row, col] = grad
            with_normed += grad * normed
            alone += grad
        copy = pltpu.make_async_copy(grad_buffer.at[row], grad_ref.at[row], left.at[row])
        copy.start()
        copies.append(copy)
    sum_ref[0:1, :] = jnp.sum(with_normed, axis=0, keepdims=True)
    sum_ref[1:2, :] = jnp.sum(alone, axis=0, keepdims=True)
    for copy in copies:
        copy.wait()


def norm_backward(grad_pooled, normed, factors, *others):
    buffer = pltpu.VMEM(normed.shape, jnp.float32)
    arrivals = pltpu.SemaphoreType.DMA((normed.shape[0],))
    return pl.pallas_call(
        norm_back_kernel,
        in_specs=[VMEM, HBM, VMEM] + [pl.BlockSpec(memory_space=pl.ANY)] * len(others),
        out_specs=[HBM, VMEM],
        out_shape=[
            pltpu.HBM(normed.shape, jnp.float32),
            jax.ShapeDtypeStruct((2, normed.shape[3]), jnp.float32),
        ],
        scratch_shapes=[buffer, buffer, arrivals, arrivals],
        compiler_params=vmem(24),
        name="norm_backward",
    )(grad_pooled, in_hbm(normed), factors, *others)


def conv_kernel(
    maps_ref,
    weight_ref,
    mask_ref,
    out_ref,
    sum_ref,
    maps_buffer,
    weight_buffer,
    padded_ref,
    patch_ref,
    arrived,
):
    rows, cols, samples, depth = maps_ref.shape
    fetch = Fetch([(maps_ref, maps_buffer), (weight_ref, weight_buffer)], arrived, 2)
    fetch.wait()
    pad_into(maps_buffer, padded_ref)
    for shift in range(9):
        down, right = shift // 3, shift % 3
        shifted = padded_ref[down : down + rows, right : right + cols]
        patch_ref[:, shift * depth : (shift + 1) * depth] = shifted.reshape(-1, depth).astype(
            jnp.bfloat16
        )
    fetch.wait()
    out = jnp.dot(
        patch_ref[...],
        weight_buffer[...].astype(jnp.bfloat16),
        preferred_element_type=jnp.float32,
    )
    out_ref[...] = out
    mask = mask_ref[...]
    by_sample = out.reshape(rows * cols, samples, out.shape[1])
    sum_ref[0:1, :] = jnp.sum(jnp.sum(by_sample, axis=0) * mask, axis=0, keepdims=True)
    sum_ref[1:2, :] = jnp.sum(
        jnp.sum(by_sample * by_sample, axis=0) * mask, axis=0, keepdims=True
    )


def conv_of(maps, weight, mask):
    rows, cols, samples, depth = maps.shape
    channels = weight.shape[1]
    pixels = rows * cols * samples
    return pl.pallas_call(
        conv_kernel,
        in_specs=[HBM, HBM, VMEM],
        out_specs=[VMEM] * 2,
        out_shape=[
            jax.ShapeDtypeStruct((pixels, channels), jnp.float32),
            jax.ShapeDtypeStruct((2, channels), jnp.float32),
        ],
        scratch_shapes=[
            pltpu.VMEM(maps.shape, maps.dtype),
            pltpu.VMEM(weight.shape, weight.dtype),
            pltpu.VMEM((rows + 2, cols + 2, samples, depth), jnp.float32),
            pltpu.VMEM((pixels, 9 * depth), jnp.bfloat16),
            pltpu.SemaphoreType.DMA((2,)),
        ],
        compiler_params=vmem(32),
        name="conv",
    )(in_hbm(maps), in_hbm(weight), mask[:, None])


def sum_kernel(blocks_ref, *refs):
    out_ref = refs[-1]
    total = jnp.sum(blocks_ref[...].astype(jnp.float32), axis=0).astype(jnp.bfloat16)
    for number in range(out_ref.shape[0]):
        out_ref[number] = total


def sum_blocks(blocks, *others):
    return pl.pallas_call(
        sum_kernel,
        in_specs=[pl.BlockSpec(memory_space=pltpu.VMEM)]
        + [pl.BlockSpec(memory_space=pl.ANY)] * len(others),
        out_shape=jax.ShapeDtypeStruct(blocks.shape, jnp.bfloat16),
        compiler_params=vmem(24),
        name="sum_blocks",
    )(blocks, *others)


def conv_update_kernel(
    decay, core_ref, own_ref, other_ref, weight_ref, row_ref, col_ref, *refs
):
    grad_out, new_out, row_new_ref, col_new_ref = refs[:4]
    own_buffer, weight_buffer, grad_buffer, new_buffer, arrived, left = refs[4:]
    rows, channels = weight_ref.shape
    half = rows // 2
    core = core_ref[0]
    fetch = Fetch(
        [(own_ref, own_buffer), (weight_ref, weight_buffer)],
        arrived,
        2,
    )
    at = pl.multiple_of((1 - core) * half, half)
    grad_buffer[pl.ds(at, half)] = other_ref[...].astype(jnp.float32)
    fetch.wait()
    at = pl.multiple_of(core * half, half)
    grad_buffer[pl.ds(at, half)] = own_buffer[...].astype(jnp.float32)
    copies = [pltpu.make_async_copy(grad_buffer, grad_out, left.at[0])]
    copies[0].start()
    squared = grad_buffer[...] * grad_buffer[...]
    row_square = jnp.broadcast_to(jnp.sum(squared, axis=1, keepdims=True), (rows, 128)).T[:1]
    row_new = decay * row_ref[...].reshape(1, rows) + (1.0 - decay) * (
        row_square / channels + TINY
    )
    col_new = decay * col_ref[...].reshape(1, channels) + (1.0 - decay) * (
        jnp.sum(squared, axis=0, keepdims=True) / rows + TINY
    )
    row_new_ref[...] = row_new.reshape(row_new_ref.shape)
    col_new_ref[...] = col_new.reshape(col_new_ref.shape)
    fetch.wait()
    weight = weight_buffer[...]
    mean_square = jnp.sum(jnp.sum(weight * weight, axis=0, keepdims=True)) / (rows * channels)
    row_mean = jnp.sum(row_new) / rows
    scale = RATE * jnp.maximum(FLOOR, jnp.sqrt(mean_square))
    by_row = jnp.broadcast_to(scale * lax.rsqrt(row_new / row_mean), (128, rows)).T
    by_col = lax.rsqrt(col_new)
    for number, (top, bottom) in enumerate(spans(rows, rows // 4)):
        for first, last in spans(channels, 128):
            new_buffer[top:bottom, first:last] = weight_buffer[top:bottom, first:last] - (
                by_row[top:bottom] * grad_buffer[top:bottom, first:last]
            ) * by_col[:, first:last]
        copy = pltpu.make_async_copy(
            new_buffer.at[top:bottom], new_out.at[top:bottom], left.at[1 + number]
        )
        copy.start()
        copies.append(copy)
    for copy in copies:
        copy.wait()


def conv_update(core, own, other, weight, row_state, col_state, decay):
    rows, channels = weight.shape
    out = pltpu.HBM(weight.shape, jnp.float32)
    buffer = pltpu.VMEM(weight.shape, jnp.float32)
    return pl.pallas_call(
        functools.partial(conv_update_kernel, decay),
        in_specs=[pl.BlockSpec(memory_space=pltpu.SMEM), HBM, VMEM, HBM, VMEM, VMEM],
        out_specs=[HBM, HBM, VMEM, VMEM],
        out_shape=[
            out,
            out,
            jax.ShapeDtypeStruct((rows,), jnp.float32),
            jax.ShapeDtypeStruct((channels,), jnp.float32),
        ],
        scratch_shapes=[
            pltpu.VMEM(own.shape, own.dtype),
            buffer,
            buffer,
            buffer,
            pltpu.SemaphoreType.DMA((2,)),
            pltpu.SemaphoreType.DMA((5,)),
        ],
        compiler_params=vmem(40),
        name="conv_update",
    )(core[None], in_hbm(own), other, in_hbm(weight), row_state, col_state)


def contract_rows(left, right):
    return lax.dot_general(
        left, right, (((0,), (0,)), ((), ())), preferred_element_type=jnp.float32
    )


def exchange(blocks, axis, groups=None):
    return lax.all_to_all(blocks, axis, 0, 0, tiled=True, axis_index_groups=groups)


def gather(values, axis, size, groups=None):
    return exchange(jnp.broadcast_to(values[None], (size,) + values.shape), axis, groups)


class Ring:
    def __init__(self, axis, size, inner):
        self.axis, self.size, self.inner = axis, size, inner
        self.length = lax.axis_size(axis)
        self.own = lax.axis_index(axis) // inner % size

    def other(self, index, shift):
        own = index // self.inner % self.size
        return index + ((own + shift) % self.size - own) * self.inner

    def fetch(self, values, shift):
        pairs = [(self.other(index, shift), index) for index in range(self.length)]
        return lax.ppermute(values, self.axis, pairs)

    def stack(self, parts):
        if self.size == 2:
            first = self.own == 0
            parts = [jnp.where(first, parts[0], parts[1]), jnp.where(first, parts[1], parts[0])]
            return jnp.stack(parts)
        return jnp.roll(jnp.stack(parts), self.own, axis=0)

    def gather(self, values):
        return self.stack([values] + [self.fetch(values, k) for k in range(1, self.size)])

    def scatter_sum(self, blocks, dim):
        def block(shift):
            return lax.dynamic_index_in_dim(
                blocks, (self.own + shift) % self.size, dim, keepdims=False
            )

        result = block(0).astype(jnp.float32)
        for shift in range(1, self.size):
            result += self.fetch(block(-shift), shift).astype(jnp.float32)
        return result


def double_sums(values, axis):
    size = lax.axis_size(axis)
    inner, steps = 1, []
    while inner < size:
        pairs = [(index, index ^ inner) for index in range(size)]
        values = values + lax.ppermute(values, axis, pairs)
        steps.append(values)
        inner *= 2
    return steps


def vector_step(gradient, values, state, decay, seg_widths):
    state_new = decay * state + (1.0 - decay) * (gradient * gradient + TINY)
    scales = []
    offset = 0
    for seg_width in seg_widths:
        segment = values[offset : offset + seg_width]
        scales.append(
            jnp.full((seg_width,), 1.0, jnp.float32)
            * (RATE * jnp.maximum(FLOOR, jnp.sqrt(jnp.mean(segment * segment))))
        )
        offset += seg_width
    return (state_new, values - jnp.concatenate(scales) * gradient * lax.rsqrt(state_new))


def gram(values):
    return lax.dot_general(
        values, values, (((1,), (1,)), ((), ())), preferred_element_type=jnp.float32
    )


def square_sums(gram_matrix, values):
    values = values.astype(jnp.float32)
    return jnp.sum(values * jnp.dot(gram_matrix, values, precision=HIGHEST), axis=0)


def factor_scales(
    left, right, left_gram, right_gram, row_state, col_state, sums, rows, decay
):
    cols = right.shape[1]
    row_new = decay * row_state + (1.0 - decay) * (square_sums(right_gram, left) / cols + TINY)
    col_new = decay * col_state + (1.0 - decay) * (square_sums(left_gram, right) / rows + TINY)
    mean_square = jnp.sum(left_gram * right_gram) / (rows * cols)
    row_mean = decay * sums[0] / rows + (1.0 - decay) * (mean_square + TINY)
    scale = RATE * jnp.maximum(FLOOR, jnp.sqrt(sums[1] / (rows * cols)))
    return row_new, col_new, scale * lax.rsqrt(row_new / row_mean), lax.rsqrt(col_new)


def plain_update(left, right, weight, row_scale, col_scale):
    grad = contract_rows(left, right)
    return grad, weight - (row_scale[:, None] * grad) * col_scale[None, :]


def per_device(
    stem_maps,
    validity,
    labels,
    conv_weight,
    fc6_weight,
    head_weight,
    vectors,
    pca_matrix,
    conv_row_state,
    conv_col_state,
    fc6_row_state,
    fc6_col_state,
    head_row_state,
    head_col_state,
    vector_state,
):
    bf16, f32 = jnp.bfloat16, jnp.float32
    samples, grid = stem_maps.shape[0], stem_maps.shape[1]
    pixels = grid * grid
    channels = conv_weight.shape[1]
    fc_rows, hidden = fc6_weight.shape
    head_rows, classes = head_weight.shape
    wide_count = lax.axis_size("wide")
    grp_count = lax.axis_size("grp")
    count = wide_count * grp_count
    group = samples * wide_count
    my_wide = lax.axis_index("wide")
    decay = 1.0 - STEP ** (-0.8)
    mask = validity.astype(f32)

    core = Ring("grp", 2, 1)
    planes = Ring("grp", grp_count // 2, 2)
    near = Ring("wide", wide_count // 4, 1)
    far = Ring("wide", 4, wide_count // 4)

    bn_gain = vectors[:channels]
    bn_shift = vectors[channels : 2 * channels]
    bias_hidden = vectors[2 * channels : 2 * channels + hidden]
    bias_head = vectors[2 * channels + hidden :]

    maps = stem_maps.transpose(1, 2, 0, 3)
    conv_out, conv_sums = conv_of(maps, conv_weight, mask)
    packed = jnp.concatenate([conv_sums.reshape(-1), mask, labels.astype(f32)])
    everyone = gather(packed[None], ALL, count)
    fc6_left, left_squares = low_and_squares(fc6_weight, 0, hidden // 2, packed)
    normed, pooled, factors, pixel_total = norm_and_pool(
        everyone, conv_out, jnp.stack([bn_gain, bn_shift]), grid, samples, left_squares
    )
    everyone = everyone[:, 0]
    mask_all = everyone[:, 2 * channels : 2 * channels + samples].reshape(-1)
    labels_all = everyone[:, 2 * channels + samples :].reshape(-1)
    valid_count = jnp.sum(mask_all)
    pooled_low = pooled.transpose(1, 0, 2).reshape(samples, -1)

    pooled_blocks = pooled_low.reshape(samples, wide_count, fc_rows).transpose(1, 0, 2)
    pooled_rows = exchange(pooled_blocks, "wide").reshape(group, fc_rows)
    fc6_right, right_squares = low_and_squares(
        fc6_weight, hidden // 2, hidden // 2, pooled_blocks
    )
    pre_part = fc6_forward(pooled_rows, fc6_left, fc6_right)
    pre_blocks = exchange(
        pre_part.reshape(group, wide_count, head_rows).transpose(1, 0, 2), "wide"
    )
    head_low, head_squares = low_and_squares(head_weight.T, 0, head_rows, pre_part)
    pre_hidden = jnp.sum(pre_blocks.astype(f32), axis=0)
    pre_hidden += lax.dynamic_slice_in_dim(bias_hidden, my_wide * head_rows, head_rows)
    feats = jax.nn.silu(pre_hidden).astype(bf16)

    logit_part = head_forward(feats, head_low)
    logit_blocks = exchange(logit_part.reshape(wide_count, samples, classes), "wide")

    pooled_all = lax.all_gather(pooled_rows, "grp", axis=0, tiled=True)
    feats_all = lax.all_gather(feats, "grp", axis=0, tiled=True)
    pooled_columns = transposed(pooled_all)
    pooled_gram, feats_gram = gram(pooled_all), gram(feats_all)
    numbers = jnp.stack(
        [
            jnp.sum(fc6_row_state),
            jnp.sum(left_squares + right_squares),
            jnp.sum(head_row_state),
            jnp.sum(head_squares),
        ]
    )
    all_samples = pooled_all.shape[0]
    per_share = 2 * all_samples // grp_count
    numbers = jnp.pad(numbers, (0, all_samples - numbers.size))
    both_part = jnp.concatenate([pooled_gram, feats_gram])
    both_part = lax.dynamic_slice_in_dim(
        both_part, lax.axis_index("grp") * per_share, per_share
    )
    both_part = jnp.concatenate([both_part, numbers[None]])
    both_steps = double_sums(both_part, "wide")
    both = lax.all_gather(both_steps[-1], "grp")
    sums = both[0, per_share, :8]
    both = both[:, :per_share].reshape(-1, all_samples)
    kept_all = feats_all.astype(f32) * mask_all[:, None]
    feat_center = jnp.sum(kept_all, axis=0) / valid_count
    feat_square = jnp.sum(kept_all * kept_all, axis=0) / valid_count
    feat_scale = lax.rsqrt(feat_square - feat_center * feat_center + EPSILON)
    group_mask = lax.dynamic_slice_in_dim(mask_all, lax.axis_index("grp") * group, group)
    kept = feats.astype(f32) * group_mask[:, None]
    standard = ((kept - feat_center) * feat_scale).astype(bf16)
    projected = jnp.dot(standard, pca_matrix.astype(bf16), preferred_element_type=f32)
    projected = projected.astype(bf16)
    logits = jnp.sum(logit_blocks.astype(f32), axis=0) + bias_head

    same = labels.astype(f32)[:, None] == labels_all[None, :]
    label_count = jnp.sum(jnp.where(same, mask_all[None, :], 0.0), axis=1)
    sample_weight = mask / jnp.maximum(label_count, 1.0)
    sample_weight = follow(sample_weight, both_steps[0], projected, pooled_columns)
    label_hits = labels[:, None] == jnp.arange(classes)[None, :]
    top_logit = jnp.max(logits, axis=1, keepdims=True)
    expo = jnp.exp(logits - top_logit)
    totals = jnp.sum(expo, axis=1, keepdims=True)
    log_total = top_logit[:, 0] + jnp.log(totals[:, 0])
    label_logit = jnp.sum(jnp.where(label_hits, logits, 0.0), axis=1)
    loss_part = jnp.sum(sample_weight * (log_total - label_logit))
    weight_part = jnp.sum(sample_weight)
    grad_logits = (
        sample_weight[:, None] * (expo / totals - label_hits.astype(f32))
    ).astype(bf16)

    logits_group = gather(grad_logits, "wide", wide_count).reshape(group, classes)
    grad_pre = head_backward(logits_group, head_low, pre_hidden)
    rows = samples * projected.shape[1] // head_rows
    pre_blocks = exchange(
        jnp.concatenate(
            [
                jnp.broadcast_to(grad_pre, (wide_count,) + grad_pre.shape),
                projected.reshape(wide_count, rows, head_rows),
            ],
            axis=1,
        ),
        "wide",
    )
    projected = pre_blocks[:, group:].reshape(wide_count, samples, -1)
    pre_blocks = pre_blocks[:, :group]
    pre_group = pre_blocks.transpose(1, 0, 2).reshape(group, hidden)
    grad_pooled_rows = fc6_backward(pre_group, fc6_left, fc6_right)
    feats_gram, pooled_gram = both[all_samples:], both[:all_samples]
    by_kernels = grp_count == 4 and all_samples <= 512
    fc6_rows_total = fc_rows * wide_count
    if by_kernels:
        parts = [pre_group, planes.fetch(pre_group, 1)]
        parts += [core.fetch(part, 1) for part in parts]
        my_grp = lax.axis_index("grp")
        places = jnp.stack([my_grp, my_grp ^ 2, my_grp ^ 1, my_grp ^ 3])
        pre_all, fc6_row_new, fc6_col_new, fc6_by_row, fc6_by_col, grad_bias_hidden = fc6_stats(
            pooled_all,
            parts,
            places,
            pooled_gram,
            fc6_row_state,
            fc6_col_state,
            sums,
            fc6_rows_total,
            decay,
        )
    else:
        pre_all = lax.all_gather(pre_group, "grp", axis=0, tiled=True)
        fc6_row_new, fc6_col_new, fc6_by_row, fc6_by_col = factor_scales(
            pooled_all,
            pre_all,
            pooled_gram,
            gram(pre_all),
            fc6_row_state,
            fc6_col_state,
            sums[:2],
            fc6_rows_total,
            decay,
        )
        grad_bias_hidden = jnp.sum(pre_all.astype(f32), axis=0)
    logits_all = lax.all_gather(logits_group, "grp", axis=0, tiled=True)
    grad_pooled = exchange(grad_pooled_rows.reshape(wide_count, samples, fc_rows), "wide")
    grad_bn, bn_sums = norm_backward(
        grad_pooled, normed, factors, both
    )
    bn_sums = jnp.concatenate([bn_sums.reshape(-1), jnp.stack([loss_part, weight_part])])
    bn_sums, conv_factors = norm_sums(
        gather(bn_sums[None], ALL, count), factors, pixel_total, fc6_by_col
    )
    bn_sums = bn_sums[0]
    grad_gain, grad_shift = bn_sums[:channels], bn_sums[channels : 2 * channels]
    conv_send, conv_keep = conv_grad_of(core.own, maps, grad_bn, normed, mask, conv_factors)
    chips = count // 2
    same_core = [
        [grp * wide_count + wide for grp in range(first, grp_count, 2) for wide in range(wide_count)]
        for first in range(2)
    ]
    conv_half = (conv_keep.astype(f32) + core.fetch(conv_send, 1).astype(f32)).astype(bf16)
    conv_blocks = exchange(conv_half.reshape(chips, -1, channels), ALL, same_core)

    if by_kernels:
        fc6_grad, fc6_new, mark = row_update(
            pooled_columns, pre_all, fc6_weight, fc6_by_row, fc6_by_col, conv_half
        )
        conv_share = sum_blocks(conv_blocks, mark)
        head_row_new, head_by_row, grad_bias_head = head_stats(
            feats_all,
            logits_all,
            feats_gram,
            head_row_state,
            sums,
            hidden,
            decay,
        )
        update_head = functools.partial(
            col_update,
            left=logits_all,
            right=feats_all,
            weight=head_weight.T,
            right_gram=feats_gram,
            col_state=head_col_state,
            row_scale=head_by_row,
            rows=hidden,
            decay=decay,
        )
        blocks = pl.cdiv(classes, 2048)
        head_grad, head_new, head_col_new = update_head((0, blocks), (), start=conv_share)
        conv_own = exchange(conv_share, ALL, same_core).reshape(-1, channels)
        conv_own = carry(conv_own, head_col_new)
        head_grad, head_new = head_grad.T, head_new.T
    else:
        fc6_grad, fc6_new = plain_update(pooled_all, pre_all, fc6_weight, fc6_by_row, fc6_by_col)
        head_row_new, head_col_new, head_by_row, head_by_col = factor_scales(
            feats_all,
            logits_all,
            feats_gram,
            gram(logits_all),
            head_row_state,
            head_col_state,
            sums[2:],
            hidden,
            decay,
        )
        head_grad, head_new = plain_update(
            feats_all, logits_all, head_weight, head_by_row, head_by_col
        )
        grad_bias_head = jnp.sum(logits_all.astype(f32), axis=0)
        conv_share = sum_blocks(conv_blocks)
        conv_own = exchange(conv_share, ALL, same_core).reshape(-1, channels)
    conv_grad, conv_new, conv_row_new, conv_col_new = conv_update(
        core.own,
        conv_own,
        core.fetch(conv_own, 1),
        conv_weight,
        conv_row_state,
        conv_col_state,
        decay,
    )
    vector_grad = jnp.concatenate([grad_gain, grad_shift, grad_bias_hidden, grad_bias_head])
    vector_state_new, vector_new = vector_step(
        vector_grad, vectors, vector_state, decay, (channels, channels, hidden, classes)
    )

    projected = jnp.sum(projected.astype(f32), axis=0)
    embedded = projected * lax.rsqrt(
        jnp.sum(projected * projected, axis=1, keepdims=True) + NORM_EPS
    )
    return (
        bn_sums[2 * channels],
        bn_sums[2 * channels + 1],
        embedded,
        conv_grad,
        conv_row_new,
        conv_col_new,
        conv_new,
        fc6_grad,
        fc6_row_new,
        fc6_col_new,
        fc6_new,
        head_grad,
        head_row_new,
        head_col_new,
        head_new,
        vector_grad,
        vector_state_new,
        vector_new,
    )


def solution(mesh):
    in_specs = (
        P(("grp", "wide"), None, None, None),
        P(("grp", "wide")),
        P(("grp", "wide")),
        P(),
        P("wide", None),
        P("wide", None),
        P(),
        P("wide", None),
        P(),
        P(),
        P("wide"),
        P(),
        P("wide"),
        P(),
        P(),
    )
    out_specs = (
        P(),
        P(),
        P(("grp", "wide"), None),
        P(),
        P(),
        P(),
        P(),
        P("wide", None),
        P("wide"),
        P(),
        P("wide", None),
        P("wide", None),
        P("wide"),
        P(),
        P("wide", None),
        P(),
        P(),
        P(),
    )
    return jax.shard_map(
        per_device, mesh=mesh, in_specs=in_specs, out_specs=out_specs, check_vma=False
    )
```
